32 devices in a mesh: seq: 8 (over z, y), head: 4 (over x, core).
Axes of the slice: x: 2, y: 2, z: 4, core: 2. Of those that a mesh axis runs over, the one named last changes fastest.
Arguments:
- tokens: bfloat16 [2, 4096, 2048], P(None, 'seq'), may hold values from -6 to 6
- gain_attn: float32 [2048], replicated, may hold values from 0.5 to 1.5
- query_weight: bfloat16 [2048, 256], P(None, 'head'), may hold values from -0.125 to 0.125
- key_weight: bfloat16 [2048, 256], P(None, 'head'), may hold values from -0.125 to 0.125
- value_weight: bfloat16 [2048, 2048], P(None, 'head'), may hold values from -0.125 to 0.125
- output_weight: bfloat16 [2048, 2048], P('head'), may hold values from -1 to 1
- gain_mlp: float32 [2048], replicated, may hold values from 0.5 to 1.5
- sigmoid_switch_matrix: bfloat16 [2048, 5632], P(None, 'head'), may hold values from -0.125 to 0.125
- up_weight: bfloat16 [2048, 5632], P(None, 'head'), may hold values from -0.125 to 0.125
- down_weight: bfloat16 [5632, 2048], P('head'), may hold values from -0.078125 to 0.078125
- segment_ids: int32 [2, 4096], P(None, 'seq'), may hold values from 0 to 3, never falling along the last dimension, each value on 1 to 2000 neighbouring positions
- cotangent: bfloat16 [2, 4096, 2048], P(None, 'seq'), may hold values from -6 to 6
Outputs:
- result: bfloat16 [2, 4096, 2048], P(None, 'seq')
- d_tokens: float32 [2, 4096, 2048], P(None, 'seq')
- d_gain_attn: float32 [2048], P('seq')
- query_weight_gradient: float32 [2048, 256], P('seq', 'head')
- key_weight_gradient: float32 [2048, 256], P('seq', 'head')
- value_weight_gradient: float32 [2048, 2048], P('seq', 'head')
- output_weight_gradient: float32 [2048, 2048], P('head', 'seq')
- d_gain_mlp: float32 [2048], P('seq')
- gate_weight_gradient: float32 [2048, 5632], P('seq', 'head')
- up_weight_gradient: float32 [2048, 5632], P('seq', 'head')
- down_weight_gradient: float32 [5632, 2048], P('head', 'seq')
The draws below stay inside these ranges and needn't reach their ends.
Inputs may be any that keep to these rules, and one draw needn't show every extreme that they name: `segment_ids`: along each sequence the document numbers never fall; every number of the range occurs, on 1 to 2000 consecutive tokens, and some document has exactly 2000 tokens.
All inputs are finite; a program needn't handle non-finite values.
Results may differ from the reference program's by a relative error of at most 0.015.
Values sent between devices are 32-bit elements; how exact they have to be, the bound alone decides.
No kernel may reach another device: no remote copies, remote signals or barrier semaphores. Data moves between devices by JAX's collectives and lax.ppermute only.
A program may use at most 256 MiB of HBM per device.

```python
import math
import jax
import jax.numpy as jnp
import numpy as np
from jax import lax

D = 2048
HEADS = 16
FEAT = 16
HEAD_V = 128
FF = 5632
TOK_SEQ = 512
SEQS = 2
PASSAGE_CEILING = 2000
TAYLOR = 273
QK = 256
HV = 2048
LEN = 4096
DOCS = 4


def raised(values, stream_key, source, target, blocks, factor):
    owner, partner = [(jnp.arange(values.shape[position]) // (values.shape[position] // blocks)).reshape([-1 if axis == position else 1 for axis in range(values.ndim)]) for position in (source, target)]
    chosen = jax.random.permutation(stream_key, blocks)[partner]
    strong = (owner == chosen) | (owner == (partner + blocks // 2) % blocks)
    return jnp.where(strong, factor * values, values)


def shard_levels(stream_key, extent, shards, low, top_value):
    level = 1.0
    for position, parts in shards:
        heights = jax.random.uniform(jax.random.fold_in(jax.random.fold_in(stream_key, 6), position), (parts,), jnp.float32, low / len(shards), top_value / len(shards))
        level = level * jnp.repeat(jnp.exp(heights), extent[position] // parts).reshape((-1,) + (1,) * (len(extent) - 1 - position))
    return level


def profile(number_of, total, reach, slope):
    portions = [(1 << 20) // math.isqrt(standing ** slope) + 1 for standing in range(2, number_of + 1)]
    rest, holding = total - reach - (number_of - 1), [1] * (number_of - 1)
    while rest > 0:
        candidates = [i for i in range(number_of - 1) if holding[i] < reach]
        mass, budget = sum([portions[i] for i in candidates]), rest
        for i in candidates:
            addition = min(reach - holding[i], max(1, budget * portions[i] // mass), rest)
            holding[i] = holding[i] + addition
            rest = rest - addition
    return np.array([reach] + holding)


def uneven(key, count, total, reach, slope):
    if count == 2:
        one = jax.random.randint(key, (), max(1, total - reach), min(reach, total - 1) + 1)
        return jnp.stack([one, total - one])
    lengths = jnp.asarray(profile(count, total, reach, slope), jnp.int32)
    twos = (count - 1) // 2
    source_of, receiver = lengths[1:1 + 2 * twos:2], lengths[2:2 + 2 * twos:2]
    margin = jnp.minimum(source_of - 1, reach - receiver)
    shifted = jax.random.randint(jax.random.fold_in(key, 1), (twos,), 0, 1 << 20) % (margin + 1)
    lengths = lengths.at[1:1 + 2 * twos:2].set(source_of - shifted).at[2:2 + 2 * twos:2].set(receiver + shifted)
    return lengths[jax.random.permutation(jax.random.fold_in(key, 2), count)]


def bell_draw(stream_key, shape, deviation, limit, cuts=(), held_as=jnp.bfloat16):
    drawn = deviation * jax.random.normal(stream_key, shape, jnp.float32)
    if cuts:
        drawn = drawn * shard_levels(stream_key, shape, cuts, -0.22, 0.18)
    return jnp.clip(drawn, -limit, limit).astype(held_as)


def gaussian_with(stream_key, shape, deviation, limit, shards, heavy, dtype=jnp.bfloat16):
    entries = deviation * jax.random.normal(stream_key, shape, jnp.float32)
    if shards:
        entries = entries * shard_levels(stream_key, shape, shards, -0.22, 0.18)
    return jnp.clip(raised(entries, jax.random.fold_in(stream_key, 3), *heavy), -limit, limit).astype(dtype)


def setup_inputs(seed: int = 0) -> dict:
    seeds = jax.random.split(jax.random.key(seed), 13)
    return {
        "tokens": bell_draw(seeds[0], (SEQS, LEN, D), 1.0, 6.0, ((1, 8),)),
        "gain_attn": jnp.clip(1.0 + 0.1 * jax.random.normal(seeds[1], (D,), jnp.float32), 0.5, 1.5),
        "query_weight": bell_draw(seeds[2], (D, QK), D ** -0.5, 0.125, ((1, 4),)),
        "key_weight": bell_draw(seeds[3], (D, QK), D ** -0.5, 0.125, ((1, 4),)),
        "value_weight": bell_draw(seeds[4], (D, HV), D ** -0.5, 0.125, ((1, 4),)),
        "output_weight": bell_draw(seeds[5], (HV, D), (HV // 64) ** -0.5, 1.0, ((0, 4),)),
        "gain_mlp": jnp.clip(1.0 + 0.1 * jax.random.normal(seeds[6], (D,), jnp.float32), 0.5, 1.5),
        "sigmoid_switch_matrix": bell_draw(seeds[7], (D, FF), D ** -0.5, 0.125, ((1, 4),)),
        "up_weight": bell_draw(seeds[8], (D, FF), D ** -0.5, 0.125, ((1, 4),)),
        "down_weight": bell_draw(seeds[9], (FF, D), FF ** -0.5, 0.078125, ((0, 4),)),
        "segment_ids": jax.vmap(lambda own: jnp.searchsorted(jnp.cumsum(uneven(own, DOCS, LEN, PASSAGE_CEILING, 0)), jnp.arange(LEN), side="right"))(jax.random.split(seeds[10], SEQS)).reshape((SEQS, LEN)).astype(jnp.int32),
        "cotangent": gaussian_with(seeds[11], (SEQS, LEN, D), 1.0, 6.0, ((1, 8),), (1, 2, 8, 2.0)),
    }


EPS = 1e-05
EXACT_PRECISION = lax.Precision.HIGHEST

@jax.custom_vjp
def lower_precision(v):
    return lax.optimization_barrier(v.astype(jnp.bfloat16)).astype(jnp.float32)

@jax.custom_vjp
def lower_precision_backward(v):
    return v

def low_keep(v):
    return (lower_precision(v), None)

def low_pass(kept, grad):
    return (grad,)

def back_keep(v):
    return (v, None)

def back_low(kept, grad):
    return (lower_precision(grad),)
lower_precision.defvjp(low_keep, low_pass)
lower_precision_backward.defvjp(back_keep, back_low)

def rms_norm(values, gain):
    return values * lax.rsqrt(lax.optimization_barrier(jnp.mean(values * values, -1, keepdims=True)) + EPS) * gain

def taylor(feats):
    feat_width = feats.shape[-1]
    constant = jnp.ones_like(feats[..., :1])
    linear = feats * feat_width ** (-0.25)
    outer_prod = feats[..., :, None] * feats[..., None, :]
    second = outer_prod.reshape(feats.shape[:-1] + (feat_width * feat_width,)) / math.sqrt(2.0 * feat_width)
    return jnp.concatenate([constant, linear, second], -1)

def based_block(carry, inputs):
    prior_state, prior_norm, prior_seg = carry
    query_blk, key_blk, value_blk, seg_blk = inputs
    block_len = query_blk.shape[1]
    kernel_dot = jnp.einsum('sihf,sjhf->shij', query_blk, key_blk, precision=EXACT_PRECISION) / math.sqrt(query_blk.shape[-1])
    token_indices = jnp.arange(block_len)
    causal = token_indices[:, None] >= token_indices[None, :]
    same_doc = seg_blk[:, :, None] == seg_blk[:, None, :]
    visible = (causal[None] & same_doc)[:, None]
    scores = lower_precision_backward(lower_precision(jnp.where(visible, 1.0 + kernel_dot + 0.5 * kernel_dot * kernel_dot, 0.0)))
    numerator = lower_precision_backward(jnp.einsum('shij,sjhe->sihe', scores, value_blk, precision=EXACT_PRECISION))
    denominator = jnp.swapaxes(lax.optimization_barrier(jnp.sum(scores, -1)), 1, 2)
    feat_query = taylor(query_blk)
    uses_prior = (seg_blk == prior_seg[:, None]).astype(jnp.float32)
    numerator = numerator + uses_prior[:, :, None, None] * jnp.einsum('sihx,shxe->sihe', feat_query, prior_state, precision=EXACT_PRECISION)
    denominator = denominator + uses_prior[:, :, None] * jnp.einsum('sihx,shx->sih', feat_query, prior_norm, precision=EXACT_PRECISION)
    ratio_factor = numerator / denominator[..., None]
    feat_key = taylor(key_blk)
    in_tail = (seg_blk == seg_blk[:, -1:]).astype(jnp.float32)
    key_tail = feat_key * in_tail[:, :, None, None]
    add_state = jnp.einsum('sjhx,sjhe->shxe', key_tail, value_blk, precision=EXACT_PRECISION)
    add_norm = lax.optimization_barrier(jnp.sum(key_tail, 1))
    prefix_running_state = ((seg_blk[:, 0] == seg_blk[:, -1]) & (seg_blk[:, -1] == prior_seg)).astype(jnp.float32)
    next_state = prefix_running_state[:, None, None, None] * prior_state + add_state
    next_norm = prefix_running_state[:, None, None] * prior_norm + add_norm
    return ((next_state, next_norm, seg_blk[:, -1]), ratio_factor)

def based_attention(query_rows, key, value_rows, segment_ids):
    seq_count, length, _ = query_rows.shape
    blocks = length // TOK_SEQ

    def split(values, last_dim):
        return values.reshape(seq_count, blocks, TOK_SEQ, HEADS, last_dim).transpose(1, 0, 2, 3, 4)
    seg_blocks = segment_ids.reshape(seq_count, blocks, TOK_SEQ).transpose(1, 0, 2)
    start = (jnp.zeros((seq_count, HEADS, TAYLOR, HEAD_V), jnp.float32), jnp.zeros((seq_count, HEADS, TAYLOR), jnp.float32), jnp.full((seq_count,), -1, jnp.int32))
    _, ratios = lax.scan(jax.checkpoint(based_block), start, (split(query_rows, FEAT), split(key, FEAT), split(value_rows, HEAD_V), seg_blocks))
    return ratios.transpose(1, 0, 2, 3, 4).reshape(seq_count, length, HEADS * HEAD_V)

def reference(tokens, gain_attn, query_weight, key_weight, value_weight, output_weight, gain_mlp, sigmoid_switch_matrix, up_weight, down_weight, segment_ids, cotangent):

    def forward(resid, gain_a, query_weight_float, key_weight_float, value_weight_float, output_weight_float, gain_m, gate_weight_float, up_weight_float, down_weight_float):
        attention_hidden = lower_precision(rms_norm(resid, gain_a))
        query_rows = lower_precision_backward(lower_precision(jnp.einsum('enq,qb->enb', attention_hidden, query_weight_float, precision=EXACT_PRECISION)))
        key = lower_precision_backward(lower_precision(jnp.einsum('enq,qb->enb', attention_hidden, key_weight_float, precision=EXACT_PRECISION)))
        value_rows = lower_precision_backward(lower_precision(jnp.einsum('enq,qb->enb', attention_hidden, value_weight_float, precision=EXACT_PRECISION)))
        ratio_factor = based_attention(query_rows, key, value_rows, segment_ids)
        branch_output = lower_precision_backward(jnp.einsum('gfk,kh->gfh', lower_precision(ratio_factor), output_weight_float, precision=EXACT_PRECISION))
        residual_middle = resid + branch_output
        feedforward_hidden = lower_precision(rms_norm(residual_middle, gain_m))
        gate_projected = lower_precision_backward(jnp.einsum('nxt,tp->nxp', feedforward_hidden, gate_weight_float, precision=EXACT_PRECISION))
        up_projected = lower_precision_backward(jnp.einsum('nxt,tp->nxp', feedforward_hidden, up_weight_float, precision=EXACT_PRECISION))
        hidden_activation = lower_precision(jax.nn.silu(gate_projected) * up_projected)
        return residual_middle + jnp.einsum('jwe,ev->jwv', hidden_activation, down_weight_float, precision=EXACT_PRECISION)
    floats = [item.astype(jnp.float32) for item in (tokens, gain_attn, query_weight, key_weight, value_weight, output_weight, gain_mlp, sigmoid_switch_matrix, up_weight, down_weight)]
    output, pullback = jax.vjp(forward, *floats)
    grads = pullback(cotangent.astype(jnp.float32))
    return (output.astype(jnp.bfloat16), grads[0], grads[1], grads[2], grads[3], grads[4], grads[5], grads[6], grads[7], grads[8], grads[9])
```

```python
import math

import jax
import jax.numpy as jnp
from jax import lax
from jax.sharding import PartitionSpec as P

FEAT = 16
HEAD_V = 128


EPS = 1e-05


PASSAGE_CEILING = 2000


def swap(part, bit):
    count = lax.axis_size("head")
    return lax.ppermute(part, "head", [(k, k ^ bit) for k in range(count)])


def shift(part, by):
    count = lax.axis_size("seq")
    pairs = [(k, k + by) for k in range(count) if 0 <= k + by < count]
    return jax.tree.map(lambda leaf: lax.ppermute(leaf, "seq", pairs), part)


def head_sum(own, other):
    total = own + swap(other, 1)
    bit = 2
    while bit < lax.axis_size("head"):
        total = total + swap(total, bit)
        bit *= 2
    return total


def weighted(factor, part):
    return jax.tree.map(lambda leaf: factor.reshape((-1,) + (1,) * (leaf.ndim - 1)) * leaf, part)


def add(first, second):
    return jax.tree.map(lambda a, b: a + b, first, second)


def window(part, carries, direction, reach):
    near, far = shift(part, direction), shift(part, 2 * direction)
    carry = shift(carries, direction)
    total = add(near, weighted(carry, far))
    product = shift(carries * carry, direction)
    width = 2
    while width < reach:
        total = add(total, weighted(product, shift(total, width * direction)))
        product = product * shift(product, width * direction)
        width *= 2
    return total


def columns_dot(left, right):
    return lax.dot_general(left, right, (((0,), (0,)), ((), ())), preferred_element_type=jnp.float32)


def line_sum(pieces, place, length, along):
    def piece(at):
        return lax.dynamic_index_in_dim(pieces, jnp.clip(at, 0, length - 1), 0, keepdims=False)

    right = left = None
    for step in range(1, length):
        go_right = piece(place + length - step)
        go_left = piece(place - length + step)
        if right is not None:
            go_right, go_left = go_right + right, go_left + left
        right = along(go_right, [(k, k + 1) for k in range(step)])
        left = along(go_left, [(k, k - 1) for k in range(length - step, length)])
    return piece(place) + right + left


def line_along(part, pairs):
    return lax.ppermute(part, "seq", [(2 * a + y, 2 * b + y) for a, b in pairs for y in range(2)])


def pair_along(part):
    return lax.ppermute(part, "seq", [(k, k ^ 1) for k in range(lax.axis_size("seq"))])


class Columns:
    def __init__(self, value):
        count = lax.axis_size("seq")
        self.value = value
        tokens, width = value.shape
        self.block = width // count
        parts = value.reshape(tokens, count // 2, 2, self.block)
        y = lax.axis_index("seq") % 2
        self.mine = lax.dynamic_index_in_dim(parts, y, 2, keepdims=False).reshape(tokens, width // 2)
        self.theirs = lax.dynamic_index_in_dim(parts, 1 - y, 2, keepdims=False).reshape(tokens, width // 2)


def pair_first(left, right):
    count = lax.axis_size("seq")
    if count > 8:
        return lax.psum_scatter(columns_dot(left.value, right), "seq", scatter_dimension=0, tiled=True)
    came = pair_along(columns_dot(left.theirs, right))
    halves = columns_dot(left.mine, right) + came
    pieces = halves.reshape(count // 2, left.block, right.shape[1])
    return line_sum(pieces, lax.axis_index("seq") // 2, count // 2, line_along)


def line_first(left, right):
    count = lax.axis_size("seq")
    if count > 8:
        return lax.psum_scatter(columns_dot(left.value, right), "seq", scatter_dimension=0, tiled=True)
    whole = columns_dot(left.value, right).reshape(count // 2, 2 * left.block, right.shape[1])
    pairs = line_sum(whole, lax.axis_index("seq") // 2, count // 2, line_along)
    pairs = pairs.reshape(2, left.block, right.shape[1])
    y = lax.axis_index("seq") % 2
    theirs = lax.dynamic_index_in_dim(pairs, 1 - y, 0, keepdims=False)
    return lax.dynamic_index_in_dim(pairs, y, 0, keepdims=False) + pair_along(theirs)


def taylor(feats):
    feat_width = feats.shape[-1]
    constant = jnp.ones_like(feats[..., :1])
    linear = feats * feat_width ** (-0.25)
    outer_prod = feats[..., :, None] * feats[..., None, :]
    second = outer_prod.reshape(feats.shape[:-1] + (feat_width * feat_width,)) / math.sqrt(
        2.0 * feat_width
    )
    return jnp.concatenate([constant, linear, second], -1)


def taylor_back(feats, grad):
    feat_width = feats.shape[-1]
    linear = grad[..., 1 : 1 + feat_width] * feat_width ** (-0.25)
    second = grad[..., 1 + feat_width :].reshape(grad.shape[:-1] + (feat_width, feat_width))
    symmetric = second + jnp.swapaxes(second, -1, -2)
    return linear + jnp.einsum("sihab,sihb->siha", symmetric, feats) / math.sqrt(2.0 * feat_width)


def rms_norm(values):
    scale = lax.rsqrt(jnp.mean(values * values, -1, keepdims=True) + EPS)
    return values * scale, scale


def rms_back(normed, scale, gain, grad):
    d_normed = grad * gain
    d_values = scale * (d_normed - normed * jnp.mean(d_normed * normed, -1, keepdims=True))
    return (d_values, jnp.sum(grad * normed, 0))


def local_parts(query_rows, key_proj, segments):
    block_len = query_rows.shape[1]
    kernel_dot = jnp.einsum(
        "sihf,sjhf->shij", query_rows, key_proj, preferred_element_type=jnp.float32
    ) / math.sqrt(query_rows.shape[-1])
    token_indices = jnp.arange(block_len)
    causal = token_indices[:, None] >= token_indices[None, :]
    same_doc = segments[:, :, None] == segments[:, None, :]
    visible = (causal[None] & same_doc)[:, None]
    scores = jnp.where(visible, 1.0 + kernel_dot + 0.5 * kernel_dot * kernel_dot, 0.0).astype(
        jnp.bfloat16
    )
    feat_query = taylor(query_rows.astype(jnp.float32))
    feat_key = taylor(key_proj.astype(jnp.float32))
    return (kernel_dot, visible, scores, feat_query, feat_key)


def attention_forward(value_proj, segments, parts, carried, uses_prior, reach):
    feat_query, feat_key = (parts[3], parts[4])
    scores = parts[2]
    in_tail = (segments == segments[:, -1:]).astype(jnp.float32)
    key_tail = feat_key * in_tail[:, :, None, None]
    add_state = jnp.einsum("sjhx,sjhe->shxe", key_tail, value_proj.astype(jnp.float32))
    add_norm = jnp.sum(key_tail, 1)
    prior = window((add_state, add_norm), carried, 1, reach)
    numer_local = jnp.einsum(
        "shij,sjhe->sihe", scores, value_proj, preferred_element_type=jnp.float32
    )
    denom_local = jnp.swapaxes(jnp.sum(scores.astype(jnp.float32), -1), 1, 2)
    numerator = numer_local + uses_prior[:, :, None, None] * jnp.einsum(
        "sihx,shxe->sihe", feat_query, prior[0]
    )
    denominator = denom_local + uses_prior[:, :, None] * jnp.einsum(
        "sihx,shx->sih", feat_query, prior[1]
    )
    return (numerator / denominator[..., None], denominator, prior)


def attention_backward(
    query_rows, key_proj, value_proj, segments, parts, ratio_factor, denominator, prior, d_mixed,
    carried, uses_prior, reach,
):
    kernel_dot, visible, scores, feat_query, feat_key = parts
    prior_state, prior_norm = prior
    in_tail = (segments == segments[:, -1:]).astype(jnp.float32)
    query_f = query_rows.astype(jnp.float32)
    key_f = key_proj.astype(jnp.float32)
    value_f = value_proj.astype(jnp.float32)
    d_numer = d_mixed / denominator[..., None]
    d_denom = -jnp.sum(d_mixed * ratio_factor, -1) / denominator
    query_used = feat_query * uses_prior[:, :, None, None]
    d_state_in = jnp.einsum("sihx,sihe->shxe", query_used, d_numer)
    d_norm_in = jnp.einsum("sihx,sih->shx", query_used, d_denom)
    later_state, later_norm = window((d_state_in, d_norm_in), carried, -1, reach)
    d_numer_low = d_numer.astype(jnp.bfloat16)
    d_scores = jnp.einsum(
        "sihe,sjhe->shij", d_numer_low, value_proj, preferred_element_type=jnp.float32
    )
    d_scores = d_scores + jnp.swapaxes(d_denom, 1, 2)[..., None]
    d_scores = jnp.where(visible, d_scores, 0.0).astype(jnp.bfloat16)
    d_kernel = d_scores.astype(jnp.float32) * (1.0 + kernel_dot)
    dot_scale = 1.0 / math.sqrt(query_rows.shape[-1])
    query_gradient = jnp.einsum("shij,sjhf->sihf", d_kernel, key_f) * dot_scale
    key_gradient = jnp.einsum("shij,sihf->sjhf", d_kernel, query_f) * dot_scale
    value_gradient = jnp.einsum(
        "shij,sihe->sjhe", scores, d_numer_low, preferred_element_type=jnp.float32
    )
    d_feat_query = uses_prior[:, :, None, None] * (
        jnp.einsum("sihe,shxe->sihx", d_numer, prior_state) + d_denom[..., None] * prior_norm[:, None]
    )
    query_gradient = query_gradient + taylor_back(query_f, d_feat_query)
    d_feat_key = in_tail[:, :, None, None] * (
        jnp.einsum("sjhe,shxe->sjhx", value_f, later_state) + later_norm[:, None]
    )
    value_gradient = value_gradient + in_tail[:, :, None, None] * jnp.einsum(
        "sjhx,shxe->sjhe", feat_key, later_state
    )
    key_gradient = key_gradient + taylor_back(key_f, d_feat_key)
    return (
        query_gradient.astype(jnp.bfloat16),
        key_gradient.astype(jnp.bfloat16),
        value_gradient.astype(jnp.bfloat16),
    )


CHUNKS = 2


def dot(left, right):
    return jnp.dot(left, right, preferred_element_type=jnp.float32)


def dot_t(left, right):
    return lax.dot_general(left, right, (((left.ndim - 1,), (1,)), ((), ())), preferred_element_type=jnp.float32)


def per_device(
    tokens,
    gain_attn,
    query_weight,
    key_weight,
    value_weight,
    output_weight,
    gain_mlp,
    sigmoid_switch_matrix,
    up_weight,
    down_weight,
    segment_ids,
    cotangent,
):
    seq_count, tok_count, model_width = tokens.shape
    head_count = query_weight.shape[1] // FEAT
    reach = min(lax.axis_size("seq") - 1, -(-(PASSAGE_CEILING - 1) // tok_count))
    core = lax.axis_index("head") % 2

    def relative(whole):
        own = lax.dynamic_index_in_dim(whole, core, 0, keepdims=False)
        other = lax.dynamic_index_in_dim(whole, 1 - core, 0, keepdims=False)
        return jnp.stack([own, other])

    def absolute(own, other):
        return jnp.stack([jnp.where(core == 0, own, other), jnp.where(core == 0, other, own)])

    tokens, cotangent, segments = relative(tokens), relative(cotangent), relative(segment_ids)
    seg_float = segments.astype(jnp.float32)
    prior_last = shift(seg_float[:, -1] + 1.0, 1) - 1.0
    carried = ((segments[:, 0] == segments[:, -1]) & (seg_float[:, -1] == prior_last)).astype(jnp.float32)
    uses_prior = (seg_float == prior_last[:, None]).astype(jnp.float32)

    resid = tokens.astype(jnp.float32)
    normed_attn, scale_attn = rms_norm(resid)
    h_attn = (normed_attn * gain_attn).astype(jnp.bfloat16)
    shape = (seq_count, tok_count, head_count)
    query_rows = dot(h_attn, query_weight).astype(jnp.bfloat16).reshape(shape + (FEAT,))
    key_proj = dot(h_attn, key_weight).astype(jnp.bfloat16).reshape(shape + (FEAT,))
    value_proj = dot(h_attn, value_weight).astype(jnp.bfloat16).reshape(shape + (HEAD_V,))
    parts = local_parts(query_rows, key_proj, segments)
    ratio, denominator, prior = attention_forward(value_proj, segments, parts, carried, uses_prior, reach)
    mixed = ratio.reshape(seq_count, tok_count, head_count * HEAD_V).astype(jnp.bfloat16)

    step = tok_count // CHUNKS
    spans = [slice(k * step, (k + 1) * step) for k in range(CHUNKS)]
    branches = [head_sum(dot(mixed[0, s], output_weight), dot(mixed[1, s], output_weight)) for s in spans]

    mids, normeds, scales, h_mlps, hiddens, d_gates, d_ups, d_hs = [], [], [], [], [], [], [], []
    cots = [cotangent[:, s].reshape(-1, model_width) for s in spans]
    for s, branch, cot in zip(spans, branches, cots):
        mid = resid[:, s] + jnp.stack([branch, swap(branch, 1)])
        normed, scale = rms_norm(mid)
        h_mlp = (normed * gain_mlp).astype(jnp.bfloat16).reshape(-1, model_width)
        gate, up = dot(h_mlp, sigmoid_switch_matrix), dot(h_mlp, up_weight)
        sigmoid = jax.nn.sigmoid(gate)
        hidden = (gate * sigmoid * up).astype(jnp.bfloat16)
        d_hidden = dot_t(cot, down_weight)
        d_gate = (d_hidden * up * sigmoid * (1.0 + gate * (1.0 - sigmoid))).astype(jnp.bfloat16)
        d_up = (d_hidden * gate * sigmoid).astype(jnp.bfloat16)
        d_parts = [
            dot_t(d_gate[p], sigmoid_switch_matrix) + dot_t(d_up[p], up_weight)
            for p in (slice(0, step), slice(step, 2 * step))
        ]
        d_hs.append(head_sum(*d_parts))
        for into, value in zip((mids, normeds, scales, h_mlps, hiddens, d_gates, d_ups),
                               (mid, normed[0], scale[0], h_mlp, hidden, d_gate, d_up)):
            into.append(value)

    def join(values):
        return jnp.concatenate(values, 0)

    cot_columns, h_columns = Columns(join(cots)), Columns(join(h_mlps))
    hidden_all, d_gate_all, d_up_all = join(hiddens), join(d_gates), join(d_ups)
    cut = (hidden_all.shape[1] * 6 // 11) // 128 * 128
    down_a = pair_first(cot_columns, hidden_all[:, :cut])
    down_b = line_first(cot_columns, hidden_all[:, cut:])
    gate_weight_gradient = pair_first(h_columns, d_gate_all)
    up_weight_gradient = pair_first(h_columns, d_up_all)

    d_mids, d_gain_mlp = [], 0.0
    for s, normed, scale, d_h in zip(spans, normeds, scales, d_hs):
        d_own, d_gain = rms_back(normed, scale, gain_mlp, d_h)
        d_gain_mlp = d_gain_mlp + d_gain
        d_mids.append(cotangent[:, s].astype(jnp.float32) + jnp.stack([d_own, swap(d_own, 1)]))
    d_resid_mid = jnp.concatenate(d_mids, 1)
    d_branch = d_resid_mid.astype(jnp.bfloat16)
    d_mixed = dot_t(d_branch, output_weight).reshape(shape + (HEAD_V,))

    mlp_outs = []
    for k, s in enumerate(spans):
        out = head_sum(dot(hiddens[k][:step], down_weight), dot(hiddens[k][step:], down_weight))
        mlp_outs.append((mids[k] + jnp.stack([out, swap(out, 1)])).astype(jnp.bfloat16))
    result = jnp.concatenate(mlp_outs, 1)

    out_rows = pair_first(Columns(d_branch.reshape(-1, model_width)), mixed.reshape(-1, mixed.shape[-1]))

    d_query, d_key, d_value = attention_backward(
        query_rows, key_proj, value_proj, segments, parts, ratio, denominator, prior, d_mixed,
        carried, uses_prior, reach,
    )
    d_query, d_key, d_value = (
        part.reshape(seq_count * tok_count, -1) for part in (d_query, d_key, d_value)
    )
    d_in = []
    for p in (0, 1):
        rows = slice(p * tok_count, (p + 1) * tok_count)
        d_in.append(
            dot_t(d_query[rows], query_weight) + dot_t(d_key[rows], key_weight) + dot_t(d_value[rows], value_weight)
        )
    d_tokens = []
    d_gain_attn = 0.0
    for s in spans:
        d_h = head_sum(d_in[0][s], d_in[1][s])
        d_own, d_gain = rms_back(normed_attn[0, s], scale_attn[0, s], gain_attn, d_h)
        d_gain_attn = d_gain_attn + d_gain
        d_own = d_own + d_resid_mid[0, s]
        d_tokens.append(jnp.stack([d_own, swap(d_own, 1)]))
    d_tokens = jnp.concatenate(d_tokens, 1)
    qkv_rows = pair_first(
        Columns(h_attn.reshape(-1, model_width)), jnp.concatenate([d_query, d_key, d_value], 1)
    )

    gains = jnp.stack([d_gain_attn, d_gain_mlp])
    gains = gains + swap(gains, 1)
    count = lax.axis_size("seq")
    if count > 8:
        gains = lax.psum_scatter(gains, "seq", scatter_dimension=1, tiled=True)
    else:
        y = lax.axis_index("seq") % 2
        gains = gains.reshape(2, count // 2, 2, -1).transpose(1, 2, 0, 3)
        mine = lax.dynamic_index_in_dim(gains, y, 1, keepdims=False)
        theirs = lax.dynamic_index_in_dim(gains, 1 - y, 1, keepdims=False)
        gains = line_sum(mine + pair_along(theirs), lax.axis_index("seq") // 2, count // 2, line_along)

    narrow = query_weight.shape[1]
    return (
        absolute(result[0], result[1]),
        absolute(d_tokens[0], d_tokens[1]),
        gains[0],
        qkv_rows[:, :narrow],
        qkv_rows[:, narrow : 2 * narrow],
        qkv_rows[:, 2 * narrow :],
        out_rows.T,
        gains[1],
        gate_weight_gradient,
        up_weight_gradient,
        jnp.concatenate([down_a.T, down_b.T], 0),
    )


def solution(mesh):
    return jax.shard_map(
        per_device,
        mesh=mesh,
        in_specs=(
            P(None, "seq", None),
            P(),
            P(None, "head"),
            P(None, "head"),
            P(None, "head"),
            P("head", None),
            P(),
            P(None, "head"),
            P(None, "head"),
            P("head", None),
            P(None, "seq"),
            P(None, "seq", None),
        ),
        out_specs=(
            P(None, "seq", None),
            P(None, "seq", None),
            P("seq"),
            P("seq", "head"),
            P("seq", "head"),
            P("seq", "head"),
            P("head", "seq"),
            P("seq"),
            P("seq", "head"),
            P("seq", "head"),
            P("head", "seq"),
        ),
        check_vma=False,
    )
```

```python
import functools
import math

import jax
import jax.numpy as jnp
from jax import lax
from jax.experimental import pallas as pl
from jax.experimental.pallas import tpu as pltpu
from jax.sharding import PartitionSpec as P

FEAT = 16
HEAD_V = 128
EPS = 1e-05
PASSAGE_CEILING = 2000

MAPPED = 160
NORM = MAPPED
META = MAPPED + 16
ROWS = META + 8
FIRST, LAST, CARRIED = META, META + 1, META + 2

LONG = pl.CostEstimate(flops=1 << 39, bytes_accessed=1 << 20, transcendentals=0)


def swap(part, bit):
    count = lax.axis_size("head")
    return lax.ppermute(part, "head", [(k, k ^ bit) for k in range(count)])


def shift(part, by):
    count = lax.axis_size("seq")
    return lax.ppermute(part, "seq", [(k, k + by) for k in range(count) if 0 <= k + by < count])


def dot(left, right):
    return jnp.dot(left, right, preferred_element_type=jnp.float32)


def dot_t(left, right):
    return lax.dot_general(left, right, (((1,), (1,)), ((), ())), preferred_element_type=jnp.float32)


def columns_dot(left, right):
    return lax.dot_general(left, right, (((0,), (0,)), ((), ())), preferred_element_type=jnp.float32)


class Order:
    def __init__(self):
        self.last = None

    def after(self, *values):
        if self.last is not None:
            leaves, tree = jax.tree.flatten(values)
            values = jax.tree.unflatten(tree, lax.optimization_barrier((*leaves, self.last))[:-1])
        return values if len(values) > 1 else values[0]

    def mark(self, value):
        self.last = jax.tree.leaves(value)[0]
        return value

    def run(self, work, *values):
        if len(values) == 1:
            return self.mark(work(self.after(values[0])))
        return self.mark(work(*self.after(*values)))


def features(feats):
    row = lax.broadcasted_iota(jnp.int32, (8, feats.shape[1]), 0)
    parts = [jnp.where(row == 0, 1.0, 0.0), feats * 0.5, feats * feats * (1.0 / math.sqrt(32.0))]
    for k in range(1, 8):
        parts.append(feats * jnp.concatenate([feats[k:], feats[:k]], 0) * 0.25)
    parts.append(feats[:8] * feats[8:] * 0.25)
    return jnp.concatenate(parts, 0)


def features_back(feats, grad):
    total = grad[8:24] * 0.5 + grad[24:40] * feats * (2.0 / math.sqrt(32.0))
    for k in range(1, 8):
        part = grad[24 + 16 * k : 40 + 16 * k] * 0.25
        back = part * feats
        total = total + part * jnp.concatenate([feats[k:], feats[:k]], 0)
        total = total + jnp.concatenate([back[16 - k :], back[: 16 - k]], 0)
    part = grad[152:160] * 0.25
    return total + jnp.concatenate([part * feats[8:], part * feats[:8]], 0)


def low(value):
    return value.astype(jnp.bfloat16)


def dot_general(left, right, a, b):
    return lax.dot_general(left, right, (((a,), (b,)), ((), ())), preferred_element_type=jnp.float32)


def put_state(out_ref, h, mapped, right, weights):
    mapped = low(mapped)
    out_ref[0, h, :MAPPED, :] = dot_general(mapped, right, 1, 0)
    norm = dot_general(weights, mapped, 0, 1)
    out_ref[0, h, NORM : NORM + 8, :] = norm[:, :128]
    out_ref[0, h, NORM + 8 : NORM + 16, :] = jnp.concatenate(
        [norm[:, 128:], jnp.zeros((8, 256 - MAPPED), jnp.float32)], 1
    )


def get_norm(ref, h):
    return low(jnp.concatenate([ref[0, h, NORM : NORM + 8, :], ref[0, h, NORM + 8 : NORM + 16, : MAPPED - 128]], 1))


def transposed(ref):
    return jnp.transpose(ref[0].astype(jnp.float32))


def state_kernel(key_ref, value_ref, row_ref, meta_ref, out_ref):
    heads = key_ref.shape[2] // FEAT
    row = row_ref[0]
    tail = jnp.where(row == row[:, row.shape[1] - 1 :], 1.0, 0.0)
    key_t = transposed(key_ref)
    ones = jnp.ones((key_ref.shape[1], 8), jnp.bfloat16)
    for h in range(heads):
        mapped = features(key_t[FEAT * h : FEAT * (h + 1)]) * tail
        put_state(out_ref, h, mapped, value_ref[0, :, HEAD_V * h : HEAD_V * (h + 1)], ones)
        out_ref[0, h, META:, :] = meta_ref[0]


def seen(row_ref, column_ref):
    row, column = row_ref[0], column_ref[0]
    shape = (column.shape[0], row.shape[1])
    causal = lax.broadcasted_iota(jnp.int32, shape, 0) >= lax.broadcasted_iota(jnp.int32, shape, 1)
    return causal & (column == row)


def forward_kernel(query_ref, key_ref, value_ref, row_ref, column_ref, prior_ref, mixed_ref, ratio_ref, denom_ref):
    heads = key_ref.shape[2] // FEAT
    visible = seen(row_ref, column_ref)
    uses = jnp.where(column_ref[0] == prior_ref[0, 0, LAST : LAST + 1, :1], 1.0, 0.0)
    query_t = transposed(query_ref)
    ones = jnp.ones((key_ref.shape[1], HEAD_V), jnp.bfloat16)
    for h in range(heads):
        narrow, wide = slice(FEAT * h, FEAT * (h + 1)), slice(HEAD_V * h, HEAD_V * (h + 1))
        kernel_dot = dot_general(query_ref[0, :, narrow], key_ref[0, :, narrow], 1, 1) * 0.25
        scores = low(jnp.where(visible, 1.0 + kernel_dot + 0.5 * kernel_dot * kernel_dot, 0.0))
        both = dot(scores, jnp.concatenate([value_ref[0, :, wide], ones], 1))
        mapped = low(features(query_t[narrow]))
        numerator = both[:, :HEAD_V] + uses * dot_general(mapped, low(prior_ref[0, h, :MAPPED, :]), 0, 0)
        denominator = both[:, HEAD_V : HEAD_V + 1] + uses * dot_general(mapped, get_norm(prior_ref, h), 0, 1)[:, :1]
        ratio = numerator / denominator
        mixed_ref[0, :, wide] = low(ratio)
        ratio_ref[0, :, wide] = ratio
        denom_ref[0, :, h : h + 1] = denominator


def numer_back(h, d_mixed_ref, ratio_ref, denom_ref):
    wide = slice(HEAD_V * h, HEAD_V * (h + 1))
    inverse = 1.0 / denom_ref[0, :, h : h + 1]
    d_mixed = d_mixed_ref[0, :, wide]
    d_denom = -jnp.sum(d_mixed * ratio_ref[0, :, wide], 1, keepdims=True) * inverse
    return low(d_mixed * inverse), d_denom


def state_back_kernel(query_ref, d_mixed_ref, ratio_ref, denom_ref, row_ref, prior_ref, meta_ref, out_ref):
    heads = query_ref.shape[2] // FEAT
    uses = jnp.where(row_ref[0] == prior_ref[0, 0, LAST : LAST + 1, :1], 1.0, 0.0)
    query_t = transposed(query_ref)
    for h in range(heads):
        d_numer, d_denom = numer_back(h, d_mixed_ref, ratio_ref, denom_ref)
        mapped = features(query_t[FEAT * h : FEAT * (h + 1)]) * uses
        put_state(out_ref, h, mapped, d_numer, low(jnp.broadcast_to(d_denom, (d_denom.shape[0], 8))))
        out_ref[0, h, META:, :] = meta_ref[0]


def backward_kernel(
    query_ref, key_ref, value_ref, row_ref, column_ref, d_mixed_ref, ratio_ref, denom_ref, prior_ref, later_ref,
    d_query_ref, d_key_ref, d_value_ref,
):
    heads = key_ref.shape[2] // FEAT
    visible = seen(row_ref, column_ref)
    row, column = row_ref[0], column_ref[0]
    uses = jnp.where(row == prior_ref[0, 0, LAST : LAST + 1, :1], 1.0, 0.0)
    end = row.shape[1] - 1
    tail = jnp.where(row == row[:, end:], 1.0, 0.0)
    tail_column = jnp.where(column == row[:, end:], 1.0, 0.0)
    query_t, key_t = transposed(query_ref), transposed(key_ref)
    d_queries, d_keys = [], []
    for h in range(heads):
        narrow, wide = slice(FEAT * h, FEAT * (h + 1)), slice(HEAD_V * h, HEAD_V * (h + 1))
        query, key, value = query_ref[0, :, narrow], key_ref[0, :, narrow], value_ref[0, :, wide]
        d_numer, d_denom = numer_back(h, d_mixed_ref, ratio_ref, denom_ref)
        kernel_dot = dot_general(query, key, 1, 1) * 0.25
        scores = low(jnp.where(visible, 1.0 + kernel_dot + 0.5 * kernel_dot * kernel_dot, 0.0))
        d_scores = low(jnp.where(visible, dot_general(d_numer, value, 1, 1) + d_denom, 0.0))
        d_kernel = low(d_scores.astype(jnp.float32) * (1.0 + kernel_dot))
        d_query = dot_general(key, d_kernel, 0, 1) * 0.25
        d_key = dot_general(query, d_kernel, 0, 0) * 0.25
        d_value = dot_general(scores, d_numer, 0, 0)

        wide_denom = low(jnp.broadcast_to(d_denom, (d_denom.shape[0], 8)))
        mapped_back = dot_general(low(prior_ref[0, h, :MAPPED, :]), d_numer, 1, 1)
        mapped_back = mapped_back + dot_general(get_norm(prior_ref, h), wide_denom, 0, 1) * 0.125
        d_queries.append(d_query + features_back(query_t[narrow], mapped_back * uses))

        later = low(later_ref[0, h, :MAPPED, :])
        mapped_back = dot_general(later, value, 1, 1)
        mapped_back = mapped_back + dot_general(
            get_norm(later_ref, h), jnp.ones((value.shape[0], 8), jnp.bfloat16), 0, 1
        ) * 0.125
        d_keys.append(d_key + features_back(key_t[narrow], mapped_back * tail))
        d_value = d_value + tail_column * dot_general(low(features(key_t[narrow])), later, 0, 0)
        d_value_ref[0, :, wide] = low(d_value)
    d_query_ref[0] = low(jnp.transpose(jnp.concatenate(d_queries, 0)))
    d_key_ref[0] = low(jnp.transpose(jnp.concatenate(d_keys, 0)))


def per_sequence(kernel, out_shapes, *arrays, after=()):
    def spec(shape):
        rest = (0,) * (len(shape) - 1)
        return pl.BlockSpec((1,) + tuple(shape[1:]), lambda s: (s,) + rest)

    def body(*refs):
        kernel(*refs[: len(arrays)], *refs[len(arrays) + len(after) :])

    outs = [jax.ShapeDtypeStruct(shape, dtype) for shape, dtype in out_shapes]
    result = pl.pallas_call(
        body,
        grid=(arrays[0].shape[0],),
        in_specs=[spec(a.shape) for a in arrays] + [pl.BlockSpec(memory_space=pl.ANY) for _ in after],
        out_specs=[spec(o.shape) for o in outs],
        out_shape=outs,
        cost_estimate=LONG,
        compiler_params=pltpu.CompilerParams(vmem_limit_bytes=48 << 20),
    )(*arrays, *after)
    return result if len(outs) > 1 else result[0]


def along_pair(part):
    return lax.ppermute(part, "seq", [(k, k ^ 1) for k in range(lax.axis_size("seq"))])


def along_line(parts):
    groups = [[k for k in range(8) if k % 2 == y] for y in range(2)]
    return lax.psum_scatter(parts, "seq", scatter_dimension=0, axis_index_groups=groups, tiled=True)


def scattered(left, right):
    rows, columns = jnp.concatenate(left, 0), jnp.concatenate(right, 0)
    return lax.psum_scatter(columns_dot(rows, columns), "seq", scatter_dimension=0, tiled=True)


def blocks_dot(left, right, where, span, came=None, after=()):
    parts = len(left)
    block = left[0].shape[1] // lax.axis_size("seq")
    count, width = where.shape[0], span[1] - span[0]

    def kernel(where_ref, *refs):
        lefts, rights, out_ref = refs[:parts], refs[parts : 2 * parts], refs[-1]
        total = refs[2 * parts][...] if came is not None else None
        for left_ref, right_ref in zip(lefts, rights):
            part = dot_general(left_ref[...], right_ref[:, span[0] : span[1]], 0, 0)
            total = part if total is None else total + part
        out_ref[...] = total

    specs = [pl.BlockSpec((l.shape[0], block), lambda k, where: (0, where[k])) for l in left]
    specs += [pl.BlockSpec(r.shape, lambda k, where: (0, 0)) for r in right]
    extra = []
    if came is not None:
        specs.append(pl.BlockSpec((block, width), lambda k, where: (k, 0)))
        extra.append(came)
    specs += [pl.BlockSpec(memory_space=pl.ANY) for _ in after]
    tokens = sum(l.shape[0] for l in left)
    return pl.pallas_call(
        kernel,
        grid_spec=pltpu.PrefetchScalarGridSpec(
            num_scalar_prefetch=1,
            grid=(count,),
            in_specs=specs,
            out_specs=pl.BlockSpec((block, width), lambda k, where: (k, 0)),
        ),
        out_shape=jax.ShapeDtypeStruct((count * block, width), jnp.float32),
        compiler_params=pltpu.CompilerParams(vmem_limit_bytes=40 << 20),
        cost_estimate=LONG,
    )(where, *left, *right, *extra, *after)


def add_after(pair, after):
    rows, width = pair[0].shape

    def kernel(a_ref, b_ref, *refs):
        refs[-1][...] = a_ref[...] + b_ref[...]

    spec = pl.BlockSpec((rows // 4, width), lambda k: (k, 0))
    return pl.pallas_call(
        kernel,
        grid=(4,),
        in_specs=[spec, spec] + [pl.BlockSpec(memory_space=pl.ANY) for _ in after],
        out_specs=spec,
        out_shape=jax.ShapeDtypeStruct((rows, width), jnp.float32),
        cost_estimate=LONG,
    )(*pair, *after)


def dot_after(left, right, after):
    rows, inner = left.shape
    width = right.shape[1]
    tile = width // 4

    def kernel(left_ref, right_ref, *refs):
        refs[-1][...] = dot(left_ref[...], right_ref[...])

    return pl.pallas_call(
        kernel,
        grid=(4,),
        in_specs=[pl.BlockSpec((rows, inner), lambda k: (0, 0)), pl.BlockSpec((inner, tile), lambda k: (0, k))]
        + [pl.BlockSpec(memory_space=pl.ANY) for _ in after],
        out_specs=pl.BlockSpec((rows, tile), lambda k: (0, k)),
        out_shape=jax.ShapeDtypeStruct((rows, width), jnp.float32),
        cost_estimate=LONG,
        compiler_params=pltpu.CompilerParams(vmem_limit_bytes=40 << 20),
    )(left, right, *after)


class PairFirst:
    def __init__(self, left, right, span, after=()):
        self.left, self.right, self.span = left, right, span
        self.sent = self.whole = self.both = right[0]
        self.plain = lax.axis_size("seq") != 8
        if not self.plain:
            y = lax.axis_index("seq") % 2
            self.places = (2 * jnp.arange(4) + y).astype(jnp.int32)
            theirs = (2 * jnp.arange(4) + 1 - y).astype(jnp.int32)
            self.sent = blocks_dot(left, right, theirs, span, after=after)
            self.came = along_pair(self.sent)

    def line(self, after=()):
        if self.plain:
            self.sum = scattered(self.left, [r[:, self.span[0] : self.span[1]] for r in self.right])
            return
        self.whole = blocks_dot(self.left, self.right, self.places, self.span, self.came, after)
        self.sum = along_line(self.whole)


class LineFirst:
    def __init__(self, left, right, span, after=()):
        self.left, self.right, self.span = left, right, span
        self.sent = self.whole = self.both = right[0]
        self.plain = lax.axis_size("seq") != 8
        if not self.plain:
            self.block = left[0].shape[1] // 8
            self.whole = blocks_dot(left, right, jnp.arange(8, dtype=jnp.int32), span, after=after)
            self.both = along_line(self.whole)

    def pair(self):
        if not self.plain:
            y = lax.axis_index("seq") % 2
            low, high = self.both[: self.block], self.both[self.block :]
            self.mine = pick_by(y, low, high)
            self.came = along_pair(pick_by(y, high, low))

    def end(self, after):
        if self.plain:
            self.sum = scattered(self.left, [r[:, self.span[0] : self.span[1]] for r in self.right])
        else:
            self.sum = add_after((self.mine, self.came), after)


def pick_by(bit, zero, one):
    return jnp.where(bit == 0, zero, one)


def rms_norm(values):
    scale = lax.rsqrt(jnp.mean(values * values, -1, keepdims=True) + EPS)
    return values * scale, scale


def rms_back(normed, scale, gain, grad):
    d_normed = grad * gain
    d_values = scale * (d_normed - normed * jnp.mean(d_normed * normed, -1, keepdims=True))
    return (d_values, jnp.sum(grad * normed, 0))


CUTS = (0, 256, 512)


def per_device(
    tokens,
    gain_attn,
    query_weight,
    key_weight,
    value_weight,
    output_weight,
    gain_mlp,
    sigmoid_switch_matrix,
    up_weight,
    down_weight,
    segment_ids,
    cotangent,
):
    seq_count, tok_count, model_width = tokens.shape
    narrow, wide = query_weight.shape[1], value_weight.shape[1]
    head_count = narrow // FEAT
    reach = min(lax.axis_size("seq") - 1, -(-(PASSAGE_CEILING - 1) // tok_count))
    assert reach <= 4
    core = lax.axis_index("head") % 2
    order = Order()
    run = order.run

    segments = segment_ids.astype(jnp.float32) + 1.0
    row, column = segments[:, None, :], segments[:, :, None]
    first, last = segments[:, 0], segments[:, -1]

    def meta(*values):
        at = jnp.arange(8)[None, :, None]
        total = jnp.zeros((seq_count, 8, 128), jnp.float32)
        for k, value in enumerate(values):
            total = jnp.where(at == k, value[:, None, None], total)
        return total

    resid = tokens.astype(jnp.float32)
    h_attn = (rms_norm(resid)[0] * gain_attn).astype(jnp.bfloat16)
    h_rows = h_attn.reshape(-1, model_width)

    def project(h_rows, weight):
        return dot(h_rows, weight).astype(jnp.bfloat16).reshape(seq_count, tok_count, -1)

    key_proj, value_proj = project(h_rows, key_weight), project(h_rows, value_weight)
    payload = ((seq_count, head_count, ROWS, HEAD_V), jnp.float32)
    state = run(
        functools.partial(per_sequence, state_kernel, [payload]), key_proj, value_proj, row, meta(first, last)
    )
    near, far = shift(state, 1), shift(state, 2)
    query_rows = run(project, h_rows, query_weight)
    spans = [slice(a, b) for a, b in zip(CUTS[:-1], CUTS[1:])]
    cots = run(lambda cot: [cot[:, s].reshape(-1, model_width) for s in spans], cotangent)

    def at_row(part, k):
        return part[:, :, k : k + 1, :1]

    index = jnp.arange(ROWS)[None, None, :, None]

    def join_two(near, far, first, last):
        carried_near = (
            (at_row(near, FIRST) == at_row(near, LAST)) & (at_row(near, LAST) == at_row(far, LAST))
        ).astype(jnp.float32)
        first, last = first[:, None, None, None], last[:, None, None, None]
        carried = ((first == last) & (last == at_row(near, LAST))).astype(jnp.float32)
        total = jnp.where(index < META, near + carried_near * far, near)
        return jnp.where(index == CARRIED, carried, total), carried_near, carried

    two, carried_near, carried = run(join_two, near, far, first, last)
    carried = carried[:, 0, 0, 0]

    def join_four(two, four, carried_near):
        return jnp.where(index < META, two + carried_near * at_row(four, CARRIED) * four, two)

    if reach > 2:
        four = shift(two, 2)

    d_hiddens = [run(dot_t, cot, down_weight) for cot in cots]

    prior = run(join_four, two, four, carried_near) if reach > 2 else two
    block = (seq_count, tok_count)
    mixed, ratio, denominator = run(
        functools.partial(
            per_sequence,
            forward_kernel,
            [(block + (wide,), jnp.bfloat16), (block + (wide,), jnp.float32), (block + (head_count,), jnp.float32)],
        ),
        query_rows, key_proj, value_proj, row, column, prior,
    )
    head_size = lax.axis_size("head")

    def exchange(parts):
        groups = [[k, k + 1] for k in range(0, head_size, 2)]
        return lax.all_to_all(parts, "head", 0, 0, axis_index_groups=groups, tiled=True)

    def spread(own):
        return exchange(jnp.stack([own, own]))

    def mine(both):
        return jnp.where(core == 0, both[0], both[1])

    def head_part(work, *values):
        def summed(*values):
            both = exchange(work(*values))
            return both[0] + both[1]

        chip = run(summed, *values)
        bit = 2
        while 2 * bit < head_size:
            chip = chip + swap(chip, bit)
            bit *= 2
        return chip, swap(chip, bit) if bit < head_size else jnp.zeros_like(chip)

    def total(pair):
        return pair[0] + pair[1]

    def joined(parts):
        return jnp.concatenate(parts, 0)

    def flat(part):
        return part.reshape(-1, part.shape[-1])

    def paired(part):
        return part.reshape(seq_count, -1, part.shape[-1])

    def branch_part(mixed, weight):
        return paired(dot(flat(mixed), weight))

    branches = [head_part(branch_part, mixed[:, s], output_weight) for s in spans]

    mids, normeds, scales, h_mlps, hiddens, d_gates, d_ups, d_hs = [], [], [], [], [], [], [], []

    def feed(h_mlp, d_hidden, gate_weight, up_weight):
        gate, up = dot(h_mlp, gate_weight), dot(h_mlp, up_weight)
        sigmoid = jax.nn.sigmoid(gate)
        hidden = (gate * sigmoid * up).astype(jnp.bfloat16)
        d_gate = (d_hidden * up * sigmoid * (1.0 + gate * (1.0 - sigmoid))).astype(jnp.bfloat16)
        d_up = (d_hidden * gate * sigmoid).astype(jnp.bfloat16)
        return hidden, d_gate, d_up

    def feed_back(d_gate, d_up, gate_weight, up_weight):
        return paired(dot_t(d_gate, gate_weight) + dot_t(d_up, up_weight))

    hidden_width = down_weight.shape[0]
    cut_b = (hidden_width * 3 // 11) // 128 * 128
    cut = (hidden_width * 6 // 11) // 128 * 128
    for k, s in enumerate(spans):
        branch = run(lambda pair: spread(total(pair)), branches[k])

        def middle(tokens, branch):
            mid = tokens.astype(jnp.float32) + branch
            normed, scale = rms_norm(mid)
            return mid, mine(normed), mine(scale), flat((normed * gain_mlp).astype(jnp.bfloat16))

        mid, normed, scale, h_mlp = run(middle, tokens[:, s], branch)
        hidden, d_gate, d_up = run(feed, h_mlp, d_hiddens[k], sigmoid_switch_matrix, up_weight)
        for into, value in zip((mids, normeds, scales, h_mlps, hiddens, d_gates, d_ups),
                               (mid, normed, scale, h_mlp, hidden, d_gate, d_up)):
            into.append(value)
        if k == len(spans) - 1:
            down_a = PairFirst(cots, hiddens, (cut_b, hidden_width))
        d_hs.append(head_part(feed_back, d_gate, d_up, sigmoid_switch_matrix, up_weight))

    down_b = LineFirst(cots, hiddens, (0, cut_b), [d_hs[-1][0]])
    gate_a = PairFirst(h_mlps, d_gates, (0, cut), [down_b.whole])

    def out_part(k, after):
        return head_part(lambda hidden, weight: paired(dot_after(hidden, weight, after)), hiddens[k], down_weight)

    d_mids, d_branches, d_mixeds = [], [], []

    def middle_back(k, after):
        def work(d_h, normed, scale):
            d_own, d_gain = rms_back(normed, scale, gain_mlp, d_h)
            return spread(d_own), d_gain

        d_norm, d_gain = run(work, add_after(d_hs[k], after), normeds[k], scales[k])

        def work(d_norm, cot, weight):
            d_mid = cot.astype(jnp.float32) + d_norm
            d_branch = flat(d_mid.astype(jnp.bfloat16))
            return mine(d_mid), d_branch, paired(dot_t(d_branch, weight))

        d_mid, d_branch, d_mixed = run(work, d_norm, cotangent[:, spans[k]], output_weight)
        d_mids.append(d_mid)
        d_branches.append(d_branch)
        d_mixeds.append(d_mixed)
        return d_gain

    results = []

    def outcome(k, pair, after):
        own = add_after(pair, after)
        results.append(run(lambda mid, own: (mid + spread(own)).astype(jnp.bfloat16), mids[k], own))

    d_gain_mlp = middle_back(0, [gate_a.sent])
    out_0 = out_part(0, [d_mixeds[0]])
    d_gain_mlp = d_gain_mlp + middle_back(1, [out_0[0]])

    d_mixed = jnp.concatenate(d_mixeds, 1)
    d_state = run(
        functools.partial(per_sequence, state_back_kernel, [payload]),
        query_rows, d_mixed, ratio, denominator, row, prior, meta(first, last, carried),
    )
    near, far = shift(d_state, -1), shift(d_state, -2)
    down_a.line([d_state])
    outcome(0, out_0, [down_a.whole])
    out_1 = out_part(1, [results[0]])
    gate_b = PairFirst(h_mlps, d_gates, (cut, hidden_width), [out_1[0], down_b.both])
    down_b.pair()
    gate_a.line([gate_b.sent])
    mixed_rows = [flat(mixed[:, s]) for s in spans]

    def join_two_back(near, far, carried):
        total = jnp.where(index < META, near + at_row(near, CARRIED) * far, near)
        return jnp.where(index == CARRIED, carried[:, None, None, None], total), at_row(near, CARRIED)

    two, carried_near = run(join_two_back, near, far, carried)
    if reach > 2:
        four = shift(two, -2)
    up_a = PairFirst(h_mlps, d_ups, (0, cut), [two, gate_a.whole, down_a.sum])
    outcome(1, out_1, [up_a.sent])
    result = run(lambda parts: jnp.concatenate(parts, 1), results)
    later = run(join_four, two, four, carried_near) if reach > 2 else two
    d_query, d_key, d_value = run(
        functools.partial(
            per_sequence,
            backward_kernel,
            [(block + (narrow,), jnp.bfloat16), (block + (narrow,), jnp.bfloat16), (block + (wide,), jnp.bfloat16)],
            after=[results[1]],
        ),
        query_rows, key_proj, value_proj, row, column, d_mixed, ratio, denominator, prior, later,
    )

    def in_back(d_query, d_key, d_value, query_weight, key_weight, value_weight):
        d_query, d_key, d_value = flat(d_query), flat(d_key), flat(d_value)
        return paired(dot_t(d_query, query_weight) + dot_t(d_key, key_weight) + dot_t(d_value, value_weight))

    d_hs = [
        head_part(in_back, d_query[:, s], d_key[:, s], d_value[:, s], query_weight, key_weight, value_weight)
        for s in spans
    ]
    gate_b.line([d_hs[-1][0]])
    up_b = PairFirst(h_mlps, d_ups, (cut, hidden_width), [gate_b.whole, gate_a.sum])
    down_b.end([up_b.sent])
    qkv_right = flat(jnp.concatenate([d_query, d_key, d_value], -1))

    d_tokens = []

    def first_back(k, after):
        def work(d_h, tokens, d_mid):
            normed, scale = rms_norm(mine(tokens).astype(jnp.float32))
            d_own, d_gain = rms_back(normed, scale, gain_attn, d_h)
            return spread(d_own + d_mid), d_gain

        d_part, d_gain = run(work, add_after(d_hs[k], after), tokens[:, spans[k]], d_mids[k])
        d_tokens.append(d_part)
        return d_gain

    d_gain_attn = first_back(0, [down_b.sum])
    up_a.line([d_tokens[0]])
    out = PairFirst(d_branches, mixed_rows, (0, wide), [up_a.whole, gate_b.sum])
    d_gain_attn = d_gain_attn + first_back(1, [out.sent])
    count = lax.axis_size("seq")

    def gain_blocks(d_gain_attn, d_gain_mlp):
        gains = jnp.sum(spread(jnp.stack([d_gain_attn, d_gain_mlp])), 0)
        if count != 8:
            return gains
        y = lax.axis_index("seq") % 2
        blocks = gains.reshape(2, 4, 2, -1).transpose(2, 1, 3, 0)
        return pick_by(y, blocks[0], blocks[1]), pick_by(y, blocks[1], blocks[0])

    gains = run(gain_blocks, d_gain_attn, d_gain_mlp)
    if count == 8:
        gains_came = along_pair(gains[1])
    up_b.line([d_tokens[1]])
    if count == 8:
        gains = run(lambda mine, came, _: (mine + came).reshape(-1, 2), gains[0], gains_came, up_b.whole)
        gains = along_line(gains)
    else:
        gains = lax.psum_scatter(gains, "seq", scatter_dimension=1, tiled=True).T
    qkv = PairFirst([h_rows], [qkv_right], (0, qkv_right.shape[1]), [up_b.whole, up_a.sum])
    out.line([qkv.sent, up_b.sum])
    qkv.line([out.whole, out.sum, gains])
    gains = gains.T
    d_tokens = jnp.concatenate(d_tokens, 1)
    down = jnp.concatenate([down_b.sum, down_a.sum], 1).T
    gate = jnp.concatenate([gate_a.sum, gate_b.sum], 1)
    up = jnp.concatenate([up_a.sum, up_b.sum], 1)
    return (
        result,
        d_tokens,
        gains[0],
        qkv.sum[:, :narrow],
        qkv.sum[:, narrow : 2 * narrow],
        qkv.sum[:, 2 * narrow :],
        out.sum.T,
        gains[1],
        gate,
        up,
        down,
    )


def solution(mesh):
    return jax.shard_map(
        per_device,
        mesh=mesh,
        in_specs=(
            P(None, "seq", None),
            P(),
            P(None, "head"),
            P(None, "head"),
            P(None, "head"),
            P("head", None),
            P(),
            P(None, "head"),
            P(None, "head"),
            P("head", None),
            P(None, "seq"),
            P(None, "seq", None),
        ),
        out_specs=(
            P(None, "seq", None),
            P(None, "seq", None),
            P("seq"),
            P("seq", "head"),
            P("seq", "head"),
            P("seq", "head"),
            P("head", "seq"),
            P("seq"),
            P("seq", "head"),
            P("seq", "head"),
            P("head", "seq"),
        ),
        check_vma=False,
    )
```

```python
import functools
import math

import jax
import jax.numpy as jnp
from jax import lax
from jax.experimental import pallas as pl
from jax.experimental.pallas import tpu as pltpu
from jax.sharding import PartitionSpec as P

FEAT = 16
HEAD_V = 128
EPS = 1e-05
PASSAGE_CEILING = 2000

MAPPED = 160
NORM = MAPPED
META = MAPPED + 16
ROWS = META + 8
FIRST, LAST, CARRIED, NEXT = META, META + 1, META + 2, META + 3

LONG = pl.CostEstimate(flops=1 << 39, bytes_accessed=1 << 20, transcendentals=0)


def swap(part, bit):
    count = lax.axis_size("head")
    return lax.ppermute(part, "head", [(k, k ^ bit) for k in range(count)])


def shift(part, by):
    count = lax.axis_size("seq")
    return lax.ppermute(part, "seq", [(k, k + by) for k in range(count) if 0 <= k + by < count])


def dot(left, right):
    return jnp.dot(left, right, preferred_element_type=jnp.float32)


def dot_t(left, right):
    return lax.dot_general(left, right, (((1,), (1,)), ((), ())), preferred_element_type=jnp.float32)


def columns_dot(left, right):
    return lax.dot_general(left, right, (((0,), (0,)), ((), ())), preferred_element_type=jnp.float32)


class Order:
    def __init__(self):
        self.last = None

    def after(self, *values):
        if self.last is not None:
            leaves, tree = jax.tree.flatten(values)
            values = jax.tree.unflatten(tree, lax.optimization_barrier((*leaves, self.last))[:-1])
        return values if len(values) > 1 else values[0]

    def mark(self, value):
        self.last = jax.tree.leaves(value)[0]
        return value

    def run(self, work, *values):
        if len(values) == 1:
            return self.mark(work(self.after(values[0])))
        return self.mark(work(*self.after(*values)))


def features(feats):
    row = lax.broadcasted_iota(jnp.int32, (8, feats.shape[1]), 0)
    parts = [jnp.where(row == 0, 1.0, 0.0), feats * 0.5, feats * feats * (1.0 / math.sqrt(32.0))]
    for k in range(1, 8):
        parts.append(feats * jnp.concatenate([feats[k:], feats[:k]], 0) * 0.25)
    parts.append(feats[:8] * feats[8:] * 0.25)
    return jnp.concatenate(parts, 0)


def features_back(feats, grad):
    total = grad[8:24] * 0.5 + grad[24:40] * feats * (2.0 / math.sqrt(32.0))
    for k in range(1, 8):
        part = grad[24 + 16 * k : 40 + 16 * k] * 0.25
        back = part * feats
        total = total + part * jnp.concatenate([feats[k:], feats[:k]], 0)
        total = total + jnp.concatenate([back[16 - k :], back[: 16 - k]], 0)
    part = grad[152:160] * 0.25
    return total + jnp.concatenate([part * feats[8:], part * feats[:8]], 0)


def low(value):
    return value.astype(jnp.bfloat16)


def dot_general(left, right, a, b):
    return lax.dot_general(left, right, (((a,), (b,)), ((), ())), preferred_element_type=jnp.float32)


def put_state(out_ref, h, mapped, right, weights):
    mapped = low(mapped)
    out_ref[0, h, :MAPPED, :] = dot_general(mapped, right, 1, 0)
    norm = dot_general(weights, mapped, 0, 1)
    out_ref[0, h, NORM : NORM + 8, :] = norm[:, :128]
    out_ref[0, h, NORM + 8 : NORM + 16, :] = jnp.concatenate(
        [norm[:, 128:], jnp.zeros((8, 256 - MAPPED), jnp.float32)], 1
    )


def get_state(refs, h):
    two, four = refs
    joined = two[0, h] + two[0, h, NEXT : NEXT + 1, :1] * four[0, h, CARRIED : CARRIED + 1, :1] * four[0, h]
    norm = jnp.concatenate([joined[NORM : NORM + 8], joined[NORM + 8 : NORM + 16, : MAPPED - 128]], 1)
    return low(joined[:MAPPED]), low(norm)


def transposed(ref):
    return jnp.transpose(ref[0].astype(jnp.float32))


def state_kernel(key_ref, value_ref, row_ref, meta_ref, out_ref):
    heads = key_ref.shape[2] // FEAT
    row = row_ref[0]
    tail = jnp.where(row == row[:, row.shape[1] - 1 :], 1.0, 0.0)
    key_t = transposed(key_ref)
    ones = jnp.ones((key_ref.shape[1], 8), jnp.bfloat16)
    for h in range(heads):
        mapped = features(key_t[FEAT * h : FEAT * (h + 1)]) * tail
        put_state(out_ref, h, mapped, value_ref[0, :, HEAD_V * h : HEAD_V * (h + 1)], ones)
        out_ref[0, h, META:, :] = meta_ref[0]


def seen(row_ref, column_ref):
    row, column = row_ref[0], column_ref[0]
    shape = (column.shape[0], row.shape[1])
    causal = lax.broadcasted_iota(jnp.int32, shape, 0) >= lax.broadcasted_iota(jnp.int32, shape, 1)
    return causal & (column == row)


def forward_kernel(
    query_ref, key_ref, value_ref, row_ref, column_ref, prior_ref, prior_four_ref, mixed_ref, ratio_ref, denom_ref
):
    heads = key_ref.shape[2] // FEAT
    visible = seen(row_ref, column_ref)
    uses = jnp.where(column_ref[0] == prior_ref[0, 0, LAST : LAST + 1, :1], 1.0, 0.0)
    query_t = transposed(query_ref)
    ones = jnp.ones((key_ref.shape[1], HEAD_V), jnp.bfloat16)
    for h in range(heads):
        narrow, wide = slice(FEAT * h, FEAT * (h + 1)), slice(HEAD_V * h, HEAD_V * (h + 1))
        kernel_dot = dot_general(query_ref[0, :, narrow], key_ref[0, :, narrow], 1, 1) * 0.25
        scores = low(jnp.where(visible, 1.0 + kernel_dot + 0.5 * kernel_dot * kernel_dot, 0.0))
        both = dot(scores, jnp.concatenate([value_ref[0, :, wide], ones], 1))
        mapped = low(features(query_t[narrow]))
        state, norm = get_state((prior_ref, prior_four_ref), h)
        numerator = both[:, :HEAD_V] + uses * dot_general(mapped, state, 0, 0)
        denominator = both[:, HEAD_V : HEAD_V + 1] + uses * dot_general(mapped, norm, 0, 1)[:, :1]
        ratio = numerator / denominator
        mixed_ref[0, :, wide] = low(ratio)
        ratio_ref[0, :, wide] = ratio
        denom_ref[0, :, h : h + 1] = denominator


def numer_back(h, d_mixed_ref, ratio_ref, denom_ref):
    wide = slice(HEAD_V * h, HEAD_V * (h + 1))
    inverse = 1.0 / denom_ref[0, :, h : h + 1]
    d_mixed = d_mixed_ref[0, :, wide]
    d_denom = -jnp.sum(d_mixed * ratio_ref[0, :, wide], 1, keepdims=True) * inverse
    return low(d_mixed * inverse), d_denom


def state_back_kernel(query_ref, d_mixed_ref, ratio_ref, denom_ref, row_ref, prior_ref, meta_ref, out_ref):
    heads = query_ref.shape[2] // FEAT
    uses = jnp.where(row_ref[0] == prior_ref[0, 0, LAST : LAST + 1, :1], 1.0, 0.0)
    query_t = transposed(query_ref)
    for h in range(heads):
        d_numer, d_denom = numer_back(h, d_mixed_ref, ratio_ref, denom_ref)
        mapped = features(query_t[FEAT * h : FEAT * (h + 1)]) * uses
        put_state(out_ref, h, mapped, d_numer, low(jnp.broadcast_to(d_denom, (d_denom.shape[0], 8))))
        out_ref[0, h, META:, :] = meta_ref[0]


def join_back_kernel(near_ref, far_ref, carried_ref, out_ref):
    for h in range(near_ref.shape[1]):
        near, far = near_ref[0, h], far_ref[0, h]
        at = lax.broadcasted_iota(jnp.int32, near.shape, 0)
        total = jnp.where(at < META, near + near[CARRIED : CARRIED + 1, :1] * far, near)
        total = jnp.where(at == NEXT, near[CARRIED : CARRIED + 1, :1], total)
        out_ref[0, h] = jnp.where(at == CARRIED, carried_ref[0], total)


def backward_kernel(
    query_ref, key_ref, value_ref, row_ref, column_ref, d_mixed_ref, ratio_ref, denom_ref, prior_ref, prior_four_ref,
    later_ref, later_four_ref, d_query_ref, d_key_ref, d_value_ref,
):
    heads = key_ref.shape[2] // FEAT
    visible = seen(row_ref, column_ref)
    row, column = row_ref[0], column_ref[0]
    uses = jnp.where(row == prior_ref[0, 0, LAST : LAST + 1, :1], 1.0, 0.0)
    end = row.shape[1] - 1
    tail = jnp.where(row == row[:, end:], 1.0, 0.0)
    tail_column = jnp.where(column == row[:, end:], 1.0, 0.0)
    query_t, key_t = transposed(query_ref), transposed(key_ref)
    d_queries, d_keys = [], []
    for h in range(heads):
        narrow, wide = slice(FEAT * h, FEAT * (h + 1)), slice(HEAD_V * h, HEAD_V * (h + 1))
        query, key, value = query_ref[0, :, narrow], key_ref[0, :, narrow], value_ref[0, :, wide]
        d_numer, d_denom = numer_back(h, d_mixed_ref, ratio_ref, denom_ref)
        kernel_dot = dot_general(query, key, 1, 1) * 0.25
        scores = low(jnp.where(visible, 1.0 + kernel_dot + 0.5 * kernel_dot * kernel_dot, 0.0))
        d_scores = low(jnp.where(visible, dot_general(d_numer, value, 1, 1) + d_denom, 0.0))
        d_kernel = low(d_scores.astype(jnp.float32) * (1.0 + kernel_dot))
        d_query = dot_general(key, d_kernel, 0, 1) * 0.25
        d_key = dot_general(query, d_kernel, 0, 0) * 0.25
        d_value = dot_general(scores, d_numer, 0, 0)

        wide_denom = low(jnp.broadcast_to(d_denom, (d_denom.shape[0], 8)))
        state, norm = get_state((prior_ref, prior_four_ref), h)
        mapped_back = dot_general(state, d_numer, 1, 1)
        mapped_back = mapped_back + dot_general(norm, wide_denom, 0, 1) * 0.125
        d_queries.append(d_query + features_back(query_t[narrow], mapped_back * uses))

        later, norm = get_state((later_ref, later_four_ref), h)
        mapped_back = dot_general(later, value, 1, 1)
        mapped_back = mapped_back + dot_general(norm, jnp.ones((value.shape[0], 8), jnp.bfloat16), 0, 1) * 0.125
        d_keys.append(d_key + features_back(key_t[narrow], mapped_back * tail))
        d_value = d_value + tail_column * dot_general(low(features(key_t[narrow])), later, 0, 0)
        d_value_ref[0, :, wide] = low(d_value)
    d_query_ref[0] = low(jnp.transpose(jnp.concatenate(d_queries, 0)))
    d_key_ref[0] = low(jnp.transpose(jnp.concatenate(d_keys, 0)))


def per_sequence(kernel, out_shapes, *arrays, after=()):
    def spec(shape):
        rest = (0,) * (len(shape) - 1)
        return pl.BlockSpec((1,) + tuple(shape[1:]), lambda s: (s,) + rest)

    def body(*refs):
        kernel(*refs[: len(arrays)], *refs[len(arrays) + len(after) :])

    outs = [jax.ShapeDtypeStruct(shape, dtype) for shape, dtype in out_shapes]
    result = pl.pallas_call(
        body,
        grid=(arrays[0].shape[0],),
        in_specs=[spec(a.shape) for a in arrays] + [pl.BlockSpec(memory_space=pl.ANY) for _ in after],
        out_specs=[spec(o.shape) for o in outs],
        out_shape=outs,
        cost_estimate=LONG,
        compiler_params=pltpu.CompilerParams(vmem_limit_bytes=48 << 20),
    )(*arrays, *after)
    return result if len(outs) > 1 else result[0]


def along_pair(part):
    return lax.ppermute(part, "seq", [(k, k ^ 1) for k in range(lax.axis_size("seq"))])


def along_line(parts):
    groups = [[k for k in range(8) if k % 2 == y] for y in range(2)]
    return lax.psum_scatter(parts, "seq", scatter_dimension=0, axis_index_groups=groups, tiled=True)


def scattered(left, right):
    rows, columns = jnp.concatenate(left, 0), jnp.concatenate(right, 0)
    return lax.psum_scatter(columns_dot(rows, columns), "seq", scatter_dimension=0, tiled=True)


def named(k, where):
    return 0, where[k]


def blocks_dot(terms, where, span, came=None, after=()):
    parts = len(terms)
    block = terms[0][0].shape[1] // lax.axis_size("seq")
    count, width = where.shape[0], span[1] - span[0]

    wide = [t[3].dtype != jnp.bfloat16 for t in terms]
    scratch = [pltpu.VMEM((t[3].shape[0], width), jnp.bfloat16) for t, w in zip(terms, wide) if w]

    def kernel(where_ref, *refs):
        lefts, rights = refs[:parts], refs[parts : 2 * parts]
        out_ref, narrow = refs[len(refs) - 1 - len(scratch)], list(refs[len(refs) - len(scratch) :])
        total = refs[2 * parts][...] if came is not None else None
        for n in range(parts):
            left_ref, columns = lefts[n], slice(*terms[n][4])
            if wide[n]:
                kept_ref = narrow.pop(0)

                @pl.when(pl.program_id(0) == 0)
                def _():
                    kept_ref[...] = low(rights[n][:, columns])

                right = kept_ref[...]
            else:
                right = rights[n][:, columns]
            part = dot_general(low(left_ref[...]), right, 0, 0)
            total = part if total is None else total + part
        out_ref[...] = total

    specs = [pl.BlockSpec((rows, block), at) for _, rows, at, _, _ in terms]
    specs += [pl.BlockSpec(right.shape, lambda k, where: (0, 0)) for _, _, _, right, _ in terms]
    extra = []
    if came is not None:
        specs.append(pl.BlockSpec((block, width), lambda k, where: (k, 0)))
        extra.append(came)
    specs += [pl.BlockSpec(memory_space=pl.ANY) for _ in after]
    return pl.pallas_call(
        kernel,
        grid_spec=pltpu.PrefetchScalarGridSpec(
            num_scalar_prefetch=1,
            grid=(count,),
            in_specs=specs,
            out_specs=pl.BlockSpec((block, width), lambda k, where: (k, 0)),
            scratch_shapes=scratch,
        ),
        out_shape=jax.ShapeDtypeStruct((count * block, width), jnp.float32),
        compiler_params=pltpu.CompilerParams(vmem_limit_bytes=44 << 20),
        cost_estimate=LONG,
    )(where, *[t[0] for t in terms], *[t[3] for t in terms], *extra, *after)


def own_terms(left, right, span):
    return [(l, l.shape[0], named, r, span) for l, r in zip(left, right)]


def pair_places(y):
    return (2 * jnp.arange(4) + y).astype(jnp.int32)


def picked_columns(chunks, where, after=()):
    block = chunks[0].shape[1] // 8
    rows = [c.shape[0] for c in chunks]

    def kernel(where_ref, *refs):
        at = 0
        for ref, count in zip(refs, rows):
            refs[-1][at : at + count] = ref[...].astype(jnp.float32)
            at += count

    return pl.pallas_call(
        kernel,
        grid_spec=pltpu.PrefetchScalarGridSpec(
            num_scalar_prefetch=1,
            grid=(where.shape[0],),
            in_specs=[pl.BlockSpec((count, block), named) for count in rows]
            + [pl.BlockSpec(memory_space=pl.ANY) for _ in after],
            out_specs=pl.BlockSpec((sum(rows), block), lambda k, where: (0, k)),
        ),
        out_shape=jax.ShapeDtypeStruct((sum(rows), where.shape[0] * block), jnp.float32),
        cost_estimate=LONG,
    )(where, *chunks, *after)


def add_after(pair, after):
    rows, width = pair[0].shape
    steps = 4 if rows % 32 == 0 else 1

    def kernel(a_ref, b_ref, *refs):
        refs[-1][...] = a_ref[...] + b_ref[...]

    spec = pl.BlockSpec((rows // steps, width), lambda k: (k, 0))
    return pl.pallas_call(
        kernel,
        grid=(steps,),
        in_specs=[spec, spec] + [pl.BlockSpec(memory_space=pl.ANY) for _ in after],
        out_specs=spec,
        out_shape=jax.ShapeDtypeStruct((rows, width), jnp.float32),
        cost_estimate=LONG,
    )(*pair, *after)


def transposed_after(value, after):
    def kernel(in_ref, *refs):
        refs[-1][...] = jnp.transpose(in_ref[...])

    return pl.pallas_call(
        kernel,
        grid=(1,),
        in_specs=[pl.BlockSpec(value.shape, lambda k: (0, 0))] + [pl.BlockSpec(memory_space=pl.ANY) for _ in after],
        out_specs=pl.BlockSpec(value.shape[::-1], lambda k: (0, 0)),
        out_shape=jax.ShapeDtypeStruct(value.shape[::-1], value.dtype),
        cost_estimate=LONG,
    )(value, *after)


def dot_after(left, right, after):
    rows, inner = left.shape
    width = right.shape[1]
    tile = width // 4

    def kernel(left_ref, right_ref, *refs):
        refs[-1][...] = dot(left_ref[...], right_ref[...])

    return pl.pallas_call(
        kernel,
        grid=(4,),
        in_specs=[pl.BlockSpec((rows, inner), lambda k: (0, 0)), pl.BlockSpec((inner, tile), lambda k: (0, k))]
        + [pl.BlockSpec(memory_space=pl.ANY) for _ in after],
        out_specs=pl.BlockSpec((rows, tile), lambda k: (0, k)),
        out_shape=jax.ShapeDtypeStruct((rows, width), jnp.float32),
        cost_estimate=LONG,
        compiler_params=pltpu.CompilerParams(vmem_limit_bytes=40 << 20),
    )(left, right, *after)


def dots_after(lefts, rights, after):
    rows, width, count = lefts[0].shape[0], rights[0].shape[0], len(lefts)
    tile = width // 4

    def kernel(*refs):
        refs[-1][...] = sum(dot_t(refs[k][...], refs[count + k][...]) for k in range(count))

    return pl.pallas_call(
        kernel,
        grid=(4,),
        in_specs=[pl.BlockSpec(left.shape, lambda k: (0, 0)) for left in lefts]
        + [pl.BlockSpec((tile, right.shape[1]), lambda k: (k, 0)) for right in rights]
        + [pl.BlockSpec(memory_space=pl.ANY) for _ in after],
        out_specs=pl.BlockSpec((rows, tile), lambda k: (0, k)),
        out_shape=jax.ShapeDtypeStruct((rows, width), jnp.float32),
        cost_estimate=LONG,
        compiler_params=pltpu.CompilerParams(vmem_limit_bytes=40 << 20),
    )(*lefts, *rights, *after)


class PairFirst:
    def __init__(self, left, right, span, after=()):
        self.left, self.right, self.span = left, right, span
        self.sent = self.whole = self.both = right[0]
        self.plain = lax.axis_size("seq") != 8
        if not self.plain:
            y = lax.axis_index("seq") % 2
            self.places = pair_places(y)
            self.sent = blocks_dot(own_terms(left, right, span), pair_places(1 - y), span, after=after)
            self.came = along_pair(self.sent)

    def line(self, after=()):
        if self.plain:
            self.sum = scattered(self.left, [r[:, self.span[0] : self.span[1]] for r in self.right])
            return
        self.whole = blocks_dot(own_terms(self.left, self.right, self.span), self.places, self.span, self.came, after)
        self.sum = along_line(self.whole)


class FactorsFirst:
    def __init__(self, left, span, after=()):
        self.left, self.span, self.right, self.came = left, span, [], []
        self.left_came = self.whole = self.sent = left[0]
        self.plain = lax.axis_size("seq") != 8
        if not self.plain:
            y = lax.axis_index("seq") % 2
            self.places = pair_places(y)
            self.left_came = along_pair(picked_columns(left, pair_places(1 - y), after))

    def add(self, right):
        self.right.append(right)
        if not self.plain:
            self.sent = right[:, self.span[0] : self.span[1]].astype(jnp.float32)
            self.came.append(along_pair(self.sent))

    def line(self, after=()):
        if self.plain:
            self.sum = scattered(self.left, [r[:, self.span[0] : self.span[1]] for r in self.right])
            return
        terms, width = own_terms(self.left, self.right, self.span), self.span[1] - self.span[0]
        for n, came in enumerate(self.came):
            terms.append((self.left_came, came.shape[0], lambda k, where, n=n: (n, k), came, (0, width)))
        self.whole = blocks_dot(terms, self.places, self.span, after=after)
        self.sum = along_line(self.whole)


class LineFirst:
    def __init__(self, left, right, span, after=()):
        self.left, self.right, self.span = left, right, span
        self.sent = self.whole = self.both = right[0]
        self.plain = lax.axis_size("seq") != 8
        if not self.plain:
            self.block = left[0].shape[1] // 8
            y = lax.axis_index("seq") % 2
            both = 2 * jnp.arange(4)[:, None] + jnp.stack([y, 1 - y])[None, :]
            self.whole = blocks_dot(own_terms(left, right, span), both.reshape(8).astype(jnp.int32), span, after=after)
            self.both = along_line(self.whole)

    def pair(self):
        if not self.plain:
            self.came = along_pair(self.both[self.block :])

    def end(self, after):
        if self.plain:
            self.sum = scattered(self.left, [r[:, self.span[0] : self.span[1]] for r in self.right])
        else:
            self.sum = add_after((self.both[: self.block], self.came), after)


def pick_by(bit, zero, one):
    return jnp.where(bit == 0, zero, one)


def rms_norm(values):
    scale = lax.rsqrt(jnp.mean(values * values, -1, keepdims=True) + EPS)
    return values * scale, scale


def rms_back(normed, scale, gain, grad):
    d_normed = grad * gain
    d_values = scale * (d_normed - normed * jnp.mean(d_normed * normed, -1, keepdims=True))
    return (d_values, jnp.sum(grad * normed, 0))


CUTS = (0, 256, 512)


def per_device(
    tokens,
    gain_attn,
    query_weight,
    key_weight,
    value_weight,
    output_weight,
    gain_mlp,
    sigmoid_switch_matrix,
    up_weight,
    down_weight,
    segment_ids,
    cotangent,
):
    seq_count, tok_count, model_width = tokens.shape
    narrow, wide = query_weight.shape[1], value_weight.shape[1]
    head_count = narrow // FEAT
    reach = min(lax.axis_size("seq") - 1, -(-(PASSAGE_CEILING - 1) // tok_count))
    assert reach <= 4
    core = lax.axis_index("head") % 2
    order = Order()
    run = order.run

    segments = segment_ids.astype(jnp.float32) + 1.0
    row, column = segments[:, None, :], segments[:, :, None]
    first, last = segments[:, 0], segments[:, -1]

    def meta(*values):
        at = jnp.arange(8)[None, :, None]
        total = jnp.zeros((seq_count, 8, 128), jnp.float32)
        for k, value in enumerate(values):
            total = jnp.where(at == k, value[:, None, None], total)
        return total

    resid = tokens.astype(jnp.float32)
    h_attn = (rms_norm(resid)[0] * gain_attn).astype(jnp.bfloat16)
    h_rows = h_attn.reshape(-1, model_width)

    def project(h_rows, weight):
        return dot(h_rows, weight).astype(jnp.bfloat16).reshape(seq_count, tok_count, -1)

    key_proj, value_proj = project(h_rows, key_weight), project(h_rows, value_weight)
    payload = ((seq_count, head_count, ROWS, HEAD_V), jnp.float32)
    state = run(
        functools.partial(per_sequence, state_kernel, [payload]), key_proj, value_proj, row, meta(first, last)
    )
    near, far = shift(state, 1), shift(state, 2)
    query_rows = run(project, h_rows, query_weight)
    spans = [slice(a, b) for a, b in zip(CUTS[:-1], CUTS[1:])]
    cots = run(lambda cot: [cot[:, s].reshape(-1, model_width) for s in spans], cotangent)

    def at_row(part, k):
        return part[:, :, k : k + 1, :1]

    index = jnp.arange(ROWS)[None, None, :, None]

    def join_two(near, far, first, last):
        carried_near = (
            (at_row(near, FIRST) == at_row(near, LAST)) & (at_row(near, LAST) == at_row(far, LAST))
        ).astype(jnp.float32)
        first, last = first[:, None, None, None], last[:, None, None, None]
        carried = ((first == last) & (last == at_row(near, LAST))).astype(jnp.float32)
        total = jnp.where(index < META, near + carried_near * far, near)
        total = jnp.where(index == NEXT, carried_near, total)
        return jnp.where(index == CARRIED, carried, total), carried

    hidden_width = down_weight.shape[0]
    cut_b = (hidden_width * 3 // 11) // 128 * 128
    cut = (hidden_width * 6 // 11) // 128 * 128
    down_a = FactorsFirst(cots, (cut_b, hidden_width), [query_rows])
    prior_two, carried = run(join_two, near, far, first, last)
    carried = carried[:, 0, 0, 0]

    prior_four = shift(prior_two, 2) if reach > 2 else jnp.zeros_like(prior_two)

    d_hiddens = [run(dot_t, cot, down_weight) for cot in cots]

    block = (seq_count, tok_count)
    mixed, ratio, denominator = run(
        functools.partial(
            per_sequence,
            forward_kernel,
            [(block + (wide,), jnp.bfloat16), (block + (wide,), jnp.float32), (block + (head_count,), jnp.float32)],
        ),
        query_rows, key_proj, value_proj, row, column, prior_two, prior_four,
    )
    head_size = lax.axis_size("head")

    def exchange(parts):
        groups = [[k, k + 1] for k in range(0, head_size, 2)]
        return lax.all_to_all(parts, "head", 0, 0, axis_index_groups=groups, tiled=True)

    def spread(own):
        return exchange(jnp.stack([own, own]))

    def mine(both):
        return jnp.where(core == 0, both[0], both[1])

    def head_part(work, *values):
        def summed(*values):
            both = exchange(work(*values))
            return both[0] + both[1]

        chip = run(summed, *values)
        bit = 2
        while 2 * bit < head_size:
            chip = chip + swap(chip, bit)
            bit *= 2
        return chip, swap(chip, bit) if bit < head_size else jnp.zeros_like(chip)

    def total(pair):
        return pair[0] + pair[1]

    def joined(parts):
        return jnp.concatenate(parts, 0)

    def flat(part):
        return part.reshape(-1, part.shape[-1])

    def paired(part):
        return part.reshape(seq_count, -1, part.shape[-1])

    def branch_part(mixed, weight):
        return paired(dot(flat(mixed), weight))

    branches = [head_part(branch_part, mixed[:, s], output_weight) for s in spans]

    mids, normeds, scales, h_mlps, hiddens, d_gates, d_ups, d_hs = [], [], [], [], [], [], [], []

    def feed(h_mlp, d_hidden, gate_weight, up_weight):
        gate, up = dot(h_mlp, gate_weight), dot(h_mlp, up_weight)
        sigmoid = jax.nn.sigmoid(gate)
        hidden = (gate * sigmoid * up).astype(jnp.bfloat16)
        d_gate = (d_hidden * up * sigmoid * (1.0 + gate * (1.0 - sigmoid))).astype(jnp.bfloat16)
        d_up = (d_hidden * gate * sigmoid).astype(jnp.bfloat16)
        return hidden, d_gate, d_up

    def feed_back(d_gate, d_up, gate_weight, up_weight, after):
        return paired(dots_after((d_gate, d_up), (gate_weight, up_weight), after))

    for k, s in enumerate(spans):
        branch = run(lambda pair: spread(total(pair)), branches[k])

        def middle(tokens, branch):
            mid = tokens.astype(jnp.float32) + branch
            normed, scale = rms_norm(mid)
            return mid, mine(normed), mine(scale), flat((normed * gain_mlp).astype(jnp.bfloat16))

        mid, normed, scale, h_mlp = run(middle, tokens[:, s], branch)
        hidden, d_gate, d_up = run(feed, h_mlp, d_hiddens[k], sigmoid_switch_matrix, up_weight)
        for into, value in zip((mids, normeds, scales, h_mlps, hiddens, d_gates, d_ups),
                               (mid, normed, scale, h_mlp, hidden, d_gate, d_up)):
            into.append(value)
        down_a.add(hidden)
        begun = [down_a.left_came]
        if k == len(spans) - 1:
            gate_a = PairFirst(h_mlps, d_gates, (0, cut), [down_a.sent])
            down_b = LineFirst(cots, hiddens, (0, cut_b), [gate_a.sent])
            begun = [down_b.whole]
        d_hs.append(head_part(feed_back, d_gate, d_up, sigmoid_switch_matrix, up_weight, begun))


    def out_part(k, after):
        return head_part(lambda hidden, weight: paired(dot_after(hidden, weight, after)), hiddens[k], down_weight)

    d_mids, d_branches, d_mixeds = [], [], []

    def middle_back(k, after):
        def work(d_h, normed, scale):
            d_own, d_gain = rms_back(normed, scale, gain_mlp, d_h)
            return spread(d_own), d_gain

        d_norm, d_gain = run(work, add_after(d_hs[k], after), normeds[k], scales[k])

        def work(d_norm, cot, weight):
            d_mid = cot.astype(jnp.float32) + d_norm
            d_branch = flat(d_mid.astype(jnp.bfloat16))
            return mine(d_mid), d_branch, paired(dot_t(d_branch, weight))

        d_mid, d_branch, d_mixed = run(work, d_norm, cotangent[:, spans[k]], output_weight)
        d_mids.append(d_mid)
        d_branches.append(d_branch)
        d_mixeds.append(d_mixed)
        return d_gain

    results = []

    def outcome(k, pair, after):
        own = add_after(pair, after)
        results.append(run(lambda mid, own: (mid + spread(own)).astype(jnp.bfloat16), mids[k], own))

    d_gain_mlp = middle_back(0, [d_hs[1][0]])
    down_a.line([d_mixeds[0]])
    out_0 = out_part(0, [down_a.whole, down_b.both])
    d_gain_mlp = d_gain_mlp + middle_back(1, [out_0[0]])

    d_mixed = jnp.concatenate(d_mixeds, 1)
    d_state = run(
        functools.partial(per_sequence, state_back_kernel, [payload]),
        query_rows, d_mixed, ratio, denominator, row, prior_two, meta(first, last, carried),
    )
    near, far = shift(d_state, -1), shift(d_state, -2)
    gate_b = PairFirst(h_mlps, d_gates, (cut, hidden_width), [d_state])
    down_b.pair()
    outcome(0, out_0, [gate_b.sent])
    gate_a.line([results[0]])
    up_a = PairFirst(h_mlps, d_ups, (0, cut), [gate_a.whole, down_a.sum])
    out_1 = out_part(1, [up_a.sent])
    mixed_rows = [flat(mixed[:, s]) for s in spans]

    two = per_sequence(
        join_back_kernel, [payload], near, far, jnp.broadcast_to(carried[:, None, None], (seq_count, 1, HEAD_V)),
        after=[out_1[0]],
    )
    four = shift(two, -2) if reach > 2 else jnp.zeros_like(two)
    gate_b.line([two])
    up_b = PairFirst(h_mlps, d_ups, (cut, hidden_width), [gate_b.whole, gate_a.sum])
    d_query, d_key, d_value = run(
        functools.partial(
            per_sequence,
            backward_kernel,
            [(block + (narrow,), jnp.bfloat16), (block + (narrow,), jnp.bfloat16), (block + (wide,), jnp.bfloat16)],
            after=[up_b.sent],
        ),
        query_rows, key_proj, value_proj, row, column, d_mixed, ratio, denominator, prior_two, prior_four,
        two, four,
    )

    def in_part(k, after):
        def work(*parts):
            return paired(dots_after([flat(p) for p in parts], (query_weight, key_weight, value_weight), after))

        s = spans[k]
        return head_part(work, d_query[:, s], d_key[:, s], d_value[:, s])

    up_a.line([d_query])
    outcome(1, out_1, [up_a.whole])
    out = PairFirst(d_branches, mixed_rows, (0, wide), [results[1], gate_b.sum])
    in_0 = in_part(0, [out.sent])
    down_b.end([in_0[0]])
    in_1 = in_part(1, [down_b.sum])
    up_b.line([in_1[0]])
    qkv_right = flat(jnp.concatenate([d_query, d_key, d_value], -1))

    d_tokens = []

    def first_back(k, pair, after):
        def work(d_h, tokens, d_mid):
            normed, scale = rms_norm(mine(tokens).astype(jnp.float32))
            d_own, d_gain = rms_back(normed, scale, gain_attn, d_h)
            return spread(d_own + d_mid), d_gain

        d_part, d_gain = run(work, add_after(pair, after), tokens[:, spans[k]], d_mids[k])
        d_tokens.append(d_part)
        return d_gain

    qkv = PairFirst([h_rows], [qkv_right], (0, qkv_right.shape[1]), [up_b.whole, up_a.sum])
    d_gain_attn = first_back(0, in_0, [qkv.sent])
    out.line([d_tokens[0]])
    d_gain_attn = d_gain_attn + first_back(1, in_1, [out.whole, up_b.sum])
    count = lax.axis_size("seq")

    def gain_blocks(d_gain_attn, d_gain_mlp):
        gains = jnp.sum(spread(jnp.stack([d_gain_attn, d_gain_mlp])), 0)
        if count != 8:
            return gains
        y = lax.axis_index("seq") % 2
        blocks = gains.reshape(2, 4, 2, -1).transpose(2, 1, 0, 3).reshape(2, 8, -1)
        return pick_by(y, blocks[0], blocks[1]), pick_by(y, blocks[1], blocks[0])

    gains = run(gain_blocks, d_gain_attn, d_gain_mlp)
    if count == 8:
        gains_came = along_pair(gains[1])
    if count == 8:
        gains = along_line(add_after((gains[0], gains_came), [d_tokens[1]]))
    else:
        gains = lax.psum_scatter(gains, "seq", scatter_dimension=1, tiled=True)
    qkv.line([gains])
    output_weight_gradient = transposed_after(out.sum, [qkv.whole])
    qkv = qkv.sum
    result = jnp.concatenate(results, 1)
    d_tokens = jnp.concatenate(d_tokens, 1)
    down = jnp.concatenate([down_b.sum, down_a.sum], 1).T
    gate = jnp.concatenate([gate_a.sum, gate_b.sum], 1)
    up = jnp.concatenate([up_a.sum, up_b.sum], 1)
    return (
        result,
        d_tokens,
        gains[0],
        qkv[:, :narrow],
        qkv[:, narrow : 2 * narrow],
        qkv[:, 2 * narrow :],
        output_weight_gradient,
        gains[1],
        gate,
        up,
        down,
    )


def solution(mesh):
    return jax.shard_map(
        per_device,
        mesh=mesh,
        in_specs=(
            P(None, "seq", None),
            P(),
            P(None, "head"),
            P(None, "head"),
            P(None, "head"),
            P("head", None),
            P(),
            P(None, "head"),
            P(None, "head"),
            P("head", None),
            P(None, "seq"),
            P(None, "seq", None),
        ),
        out_specs=(
            P(None, "seq", None),
            P(None, "seq", None),
            P("seq"),
            P("seq", "head"),
            P("seq", "head"),
            P("seq", "head"),
            P("head", "seq"),
            P("seq"),
            P("seq", "head"),
            P("seq", "head"),
            P("head", "seq"),
        ),
        check_vma=False,
    )
```

```python
import functools
import math

import jax
import jax.numpy as jnp
from jax import lax
from jax.experimental import pallas as pl
from jax.experimental.pallas import tpu as pltpu
from jax.sharding import PartitionSpec as P

FEAT = 16
HEAD_V = 128
EPS = 1e-05
PASSAGE_CEILING = 2000

MAPPED = 160
NORM = MAPPED
META = MAPPED + 16
ROWS = META + 8
FIRST, LAST, CARRIED, NEXT = META, META + 1, META + 2, META + 3

LONG = pl.CostEstimate(flops=1 << 39, bytes_accessed=1 << 20, transcendentals=0)


def swap(part, bit):
    count = lax.axis_size("head")
    return lax.ppermute(part, "head", [(k, k ^ bit) for k in range(count)])


def shift(part, by):
    count = lax.axis_size("seq")
    return lax.ppermute(part, "seq", [(k, k + by) for k in range(count) if 0 <= k + by < count])


def dot(left, right):
    return jnp.dot(left, right, preferred_element_type=jnp.float32)


def dot_t(left, right):
    return lax.dot_general(left, right, (((1,), (1,)), ((), ())), preferred_element_type=jnp.float32)


def columns_dot(left, right):
    return lax.dot_general(left, right, (((0,), (0,)), ((), ())), preferred_element_type=jnp.float32)


class Order:
    def __init__(self):
        self.last = None

    def after(self, *values):
        if self.last is not None:
            leaves, tree = jax.tree.flatten(values)
            values = jax.tree.unflatten(tree, lax.optimization_barrier((*leaves, self.last))[:-1])
        return values if len(values) > 1 else values[0]

    def mark(self, value):
        self.last = jax.tree.leaves(value)[0]
        return value

    def run(self, work, *values):
        if len(values) == 1:
            return self.mark(work(self.after(values[0])))
        return self.mark(work(*self.after(*values)))


def features(feats):
    row = lax.broadcasted_iota(jnp.int32, (8, feats.shape[1]), 0)
    parts = [jnp.where(row == 0, 1.0, 0.0), feats * 0.5, feats * feats * (1.0 / math.sqrt(32.0))]
    for k in range(1, 8):
        parts.append(feats * jnp.concatenate([feats[k:], feats[:k]], 0) * 0.25)
    parts.append(feats[:8] * feats[8:] * 0.25)
    return jnp.concatenate(parts, 0)


def features_back(feats, grad):
    total = grad[8:24] * 0.5 + grad[24:40] * feats * (2.0 / math.sqrt(32.0))
    for k in range(1, 8):
        part = grad[24 + 16 * k : 40 + 16 * k] * 0.25
        back = part * feats
        total = total + part * jnp.concatenate([feats[k:], feats[:k]], 0)
        total = total + jnp.concatenate([back[16 - k :], back[: 16 - k]], 0)
    part = grad[152:160] * 0.25
    return total + jnp.concatenate([part * feats[8:], part * feats[:8]], 0)


def low(value):
    return value.astype(jnp.bfloat16)


def dot_general(left, right, a, b):
    return lax.dot_general(left, right, (((a,), (b,)), ((), ())), preferred_element_type=jnp.float32)


def put_state(out_ref, h, mapped, right, weights):
    mapped = low(mapped)
    out_ref[0, h, :MAPPED, :] = dot_general(mapped, right, 1, 0)
    norm = dot_general(weights, mapped, 0, 1)
    out_ref[0, h, NORM : NORM + 8, :] = norm[:, :128]
    out_ref[0, h, NORM + 8 : NORM + 16, :] = jnp.concatenate(
        [norm[:, 128:], jnp.zeros((8, 256 - MAPPED), jnp.float32)], 1
    )


def get_state(refs, h):
    two, four = refs
    joined = two[0, h] + two[0, h, NEXT : NEXT + 1, :1] * four[0, h, CARRIED : CARRIED + 1, :1] * four[0, h]
    norm = jnp.concatenate([joined[NORM : NORM + 8], joined[NORM + 8 : NORM + 16, : MAPPED - 128]], 1)
    return low(joined[:MAPPED]), low(norm)


def transposed(ref):
    return jnp.transpose(ref[0].astype(jnp.float32))


def state_kernel(key_ref, value_ref, row_ref, meta_ref, out_ref):
    heads = key_ref.shape[2] // FEAT
    row = row_ref[0]
    tail = jnp.where(row == row[:, row.shape[1] - 1 :], 1.0, 0.0)
    key_t = transposed(key_ref)
    ones = jnp.ones((key_ref.shape[1], 8), jnp.bfloat16)
    for h in range(heads):
        mapped = features(key_t[FEAT * h : FEAT * (h + 1)]) * tail
        put_state(out_ref, h, mapped, value_ref[0, :, HEAD_V * h : HEAD_V * (h + 1)], ones)
        out_ref[0, h, META:, :] = meta_ref[0]


def seen(row_ref, column_ref):
    row, column = row_ref[0], column_ref[0]
    shape = (column.shape[0], row.shape[1])
    causal = lax.broadcasted_iota(jnp.int32, shape, 0) >= lax.broadcasted_iota(jnp.int32, shape, 1)
    return causal & (column == row)


def forward_kernel(
    query_ref, key_ref, value_ref, row_ref, column_ref, prior_ref, prior_four_ref, mixed_ref, ratio_ref, denom_ref
):
    heads = key_ref.shape[2] // FEAT
    visible = seen(row_ref, column_ref)
    uses = jnp.where(column_ref[0] == prior_ref[0, 0, LAST : LAST + 1, :1], 1.0, 0.0)
    query_t = transposed(query_ref)
    ones = jnp.ones((key_ref.shape[1], HEAD_V), jnp.bfloat16)
    for h in range(heads):
        narrow, wide = slice(FEAT * h, FEAT * (h + 1)), slice(HEAD_V * h, HEAD_V * (h + 1))
        kernel_dot = dot_general(query_ref[0, :, narrow], key_ref[0, :, narrow], 1, 1) * 0.25
        scores = low(jnp.where(visible, 1.0 + kernel_dot + 0.5 * kernel_dot * kernel_dot, 0.0))
        both = dot(scores, jnp.concatenate([value_ref[0, :, wide], ones], 1))
        mapped = low(features(query_t[narrow]))
        state, norm = get_state((prior_ref, prior_four_ref), h)
        numerator = both[:, :HEAD_V] + uses * dot_general(mapped, state, 0, 0)
        denominator = both[:, HEAD_V : HEAD_V + 1] + uses * dot_general(mapped, norm, 0, 1)[:, :1]
        ratio = numerator / denominator
        mixed_ref[0, :, wide] = low(ratio)
        ratio_ref[0, :, wide] = ratio
        denom_ref[0, :, h : h + 1] = denominator


def numer_back(h, d_mixed_ref, ratio_ref, denom_ref):
    wide = slice(HEAD_V * h, HEAD_V * (h + 1))
    inverse = 1.0 / denom_ref[0, :, h : h + 1]
    d_mixed = d_mixed_ref[0, :, wide]
    d_denom = -jnp.sum(d_mixed * ratio_ref[0, :, wide], 1, keepdims=True) * inverse
    return low(d_mixed * inverse), d_denom


def state_back_kernel(query_ref, d_mixed_ref, ratio_ref, denom_ref, row_ref, prior_ref, meta_ref, out_ref):
    heads = query_ref.shape[2] // FEAT
    uses = jnp.where(row_ref[0] == prior_ref[0, 0, LAST : LAST + 1, :1], 1.0, 0.0)
    query_t = transposed(query_ref)
    for h in range(heads):
        d_numer, d_denom = numer_back(h, d_mixed_ref, ratio_ref, denom_ref)
        mapped = features(query_t[FEAT * h : FEAT * (h + 1)]) * uses
        put_state(out_ref, h, mapped, d_numer, low(jnp.broadcast_to(d_denom, (d_denom.shape[0], 8))))
        out_ref[0, h, META:, :] = meta_ref[0]


def join_back_kernel(near_ref, far_ref, carried_ref, out_ref):
    for h in range(near_ref.shape[1]):
        near, far = near_ref[0, h], far_ref[0, h]
        at = lax.broadcasted_iota(jnp.int32, near.shape, 0)
        total = jnp.where(at < META, near + near[CARRIED : CARRIED + 1, :1] * far, near)
        total = jnp.where(at == NEXT, near[CARRIED : CARRIED + 1, :1], total)
        out_ref[0, h] = jnp.where(at == CARRIED, carried_ref[0], total)


def backward_kernel(
    query_ref, key_ref, value_ref, row_ref, column_ref, d_mixed_ref, ratio_ref, denom_ref, prior_ref, prior_four_ref,
    later_ref, later_four_ref, d_query_ref, d_key_ref, d_value_ref,
):
    heads = key_ref.shape[2] // FEAT
    visible = seen(row_ref, column_ref)
    row, column = row_ref[0], column_ref[0]
    uses = jnp.where(row == prior_ref[0, 0, LAST : LAST + 1, :1], 1.0, 0.0)
    end = row.shape[1] - 1
    tail = jnp.where(row == row[:, end:], 1.0, 0.0)
    tail_column = jnp.where(column == row[:, end:], 1.0, 0.0)
    query_t, key_t = transposed(query_ref), transposed(key_ref)
    d_queries, d_keys = [], []
    for h in range(heads):
        narrow, wide = slice(FEAT * h, FEAT * (h + 1)), slice(HEAD_V * h, HEAD_V * (h + 1))
        query, key, value = query_ref[0, :, narrow], key_ref[0, :, narrow], value_ref[0, :, wide]
        d_numer, d_denom = numer_back(h, d_mixed_ref, ratio_ref, denom_ref)
        kernel_dot = dot_general(query, key, 1, 1) * 0.25
        scores = low(jnp.where(visible, 1.0 + kernel_dot + 0.5 * kernel_dot * kernel_dot, 0.0))
        d_scores = low(jnp.where(visible, dot_general(d_numer, value, 1, 1) + d_denom, 0.0))
        d_kernel = low(d_scores.astype(jnp.float32) * (1.0 + kernel_dot))
        d_query = dot_general(key, d_kernel, 0, 1) * 0.25
        d_key = dot_general(query, d_kernel, 0, 0) * 0.25
        d_value = dot_general(scores, d_numer, 0, 0)

        wide_denom = low(jnp.broadcast_to(d_denom, (d_denom.shape[0], 8)))
        state, norm = get_state((prior_ref, prior_four_ref), h)
        mapped_back = dot_general(state, d_numer, 1, 1)
        mapped_back = mapped_back + dot_general(norm, wide_denom, 0, 1) * 0.125
        d_queries.append(d_query + features_back(query_t[narrow], mapped_back * uses))

        later, norm = get_state((later_ref, later_four_ref), h)
        mapped_back = dot_general(later, value, 1, 1)
        mapped_back = mapped_back + dot_general(norm, jnp.ones((value.shape[0], 8), jnp.bfloat16), 0, 1) * 0.125
        d_keys.append(d_key + features_back(key_t[narrow], mapped_back * tail))
        d_value = d_value + tail_column * dot_general(low(features(key_t[narrow])), later, 0, 0)
        d_value_ref[0, :, wide] = low(d_value)
    d_query_ref[0] = low(jnp.transpose(jnp.concatenate(d_queries, 0)))
    d_key_ref[0] = low(jnp.transpose(jnp.concatenate(d_keys, 0)))


def per_sequence(kernel, out_shapes, *arrays, after=()):
    def spec(shape):
        rest = (0,) * (len(shape) - 1)
        return pl.BlockSpec((1,) + tuple(shape[1:]), lambda s: (s,) + rest)

    def body(*refs):
        kernel(*refs[: len(arrays)], *refs[len(arrays) + len(after) :])

    outs = [jax.ShapeDtypeStruct(shape, dtype) for shape, dtype in out_shapes]
    result = pl.pallas_call(
        body,
        grid=(arrays[0].shape[0],),
        in_specs=[spec(a.shape) for a in arrays] + [pl.BlockSpec(memory_space=pl.ANY) for _ in after],
        out_specs=[spec(o.shape) for o in outs],
        out_shape=outs,
        cost_estimate=LONG,
        compiler_params=pltpu.CompilerParams(vmem_limit_bytes=48 << 20),
    )(*arrays, *after)
    return result if len(outs) > 1 else result[0]


def along_pair(part):
    return lax.ppermute(part, "seq", [(k, k ^ 1) for k in range(lax.axis_size("seq"))])


def along_line(parts):
    groups = [[k for k in range(8) if k % 2 == y] for y in range(2)]
    return lax.psum_scatter(parts, "seq", scatter_dimension=0, axis_index_groups=groups, tiled=True)


def scattered(left, right):
    rows, columns = jnp.concatenate(left, 0), jnp.concatenate(right, 0)
    return lax.psum_scatter(columns_dot(rows, columns), "seq", scatter_dimension=0, tiled=True)


def named(k, where):
    return 0, where[k]


def blocks_dot(terms, where, span, came=None, after=()):
    parts = len(terms)
    block = terms[0][0].shape[1] // lax.axis_size("seq")
    count, width = where.shape[0], span[1] - span[0]

    wide = [t[3].dtype != jnp.bfloat16 for t in terms]
    scratch = [pltpu.VMEM((t[3].shape[0], width), jnp.bfloat16) for t, w in zip(terms, wide) if w]

    def kernel(where_ref, *refs):
        lefts, rights = refs[:parts], refs[parts : 2 * parts]
        out_ref, narrow = refs[len(refs) - 1 - len(scratch)], list(refs[len(refs) - len(scratch) :])
        total = refs[2 * parts][...] if came is not None else None
        for n in range(parts):
            left_ref, columns = lefts[n], slice(*terms[n][4])
            if wide[n]:
                kept_ref = narrow.pop(0)

                @pl.when(pl.program_id(0) == 0)
                def _():
                    kept_ref[...] = low(rights[n][:, columns])

                right = kept_ref[...]
            else:
                right = rights[n][:, columns]
            part = dot_general(low(left_ref[...]), right, 0, 0)
            total = part if total is None else total + part
        out_ref[...] = total

    specs = [pl.BlockSpec((rows, block), at) for _, rows, at, _, _ in terms]
    specs += [pl.BlockSpec(right.shape, lambda k, where: (0, 0)) for _, _, _, right, _ in terms]
    extra = []
    if came is not None:
        specs.append(pl.BlockSpec((block, width), lambda k, where: (k, 0)))
        extra.append(came)
    specs += [pl.BlockSpec(memory_space=pl.ANY) for _ in after]
    return pl.pallas_call(
        kernel,
        grid_spec=pltpu.PrefetchScalarGridSpec(
            num_scalar_prefetch=1,
            grid=(count,),
            in_specs=specs,
            out_specs=pl.BlockSpec((block, width), lambda k, where: (k, 0)),
            scratch_shapes=scratch,
        ),
        out_shape=jax.ShapeDtypeStruct((count * block, width), jnp.float32),
        compiler_params=pltpu.CompilerParams(vmem_limit_bytes=44 << 20),
        cost_estimate=LONG,
    )(where, *[t[0] for t in terms], *[t[3] for t in terms], *extra, *after)


def own_terms(left, right, span):
    return [(l, l.shape[0], named, r, span) for l, r in zip(left, right)]


def pair_places(y):
    return (2 * jnp.arange(4) + y).astype(jnp.int32)


def picked_columns(chunks, where, after=()):
    block = chunks[0].shape[1] // 8
    rows = [c.shape[0] for c in chunks]

    def kernel(where_ref, *refs):
        at = 0
        for ref, count in zip(refs, rows):
            refs[-1][at : at + count] = ref[...].astype(jnp.float32)
            at += count

    return pl.pallas_call(
        kernel,
        grid_spec=pltpu.PrefetchScalarGridSpec(
            num_scalar_prefetch=1,
            grid=(where.shape[0],),
            in_specs=[pl.BlockSpec((count, block), named) for count in rows]
            + [pl.BlockSpec(memory_space=pl.ANY) for _ in after],
            out_specs=pl.BlockSpec((sum(rows), block), lambda k, where: (0, k)),
        ),
        out_shape=jax.ShapeDtypeStruct((sum(rows), where.shape[0] * block), jnp.float32),
        cost_estimate=LONG,
    )(where, *chunks, *after)


def add_after(terms, after):
    rows, width = terms[0].shape
    steps = 4 if rows % 32 == 0 else 1

    def kernel(*refs):
        refs[-1][...] = sum(ref[...] for ref in refs[: len(terms)])

    spec = pl.BlockSpec((rows // steps, width), lambda k: (k, 0))
    return pl.pallas_call(
        kernel,
        grid=(steps,),
        in_specs=[spec] * len(terms) + [pl.BlockSpec(memory_space=pl.ANY) for _ in after],
        out_specs=spec,
        out_shape=jax.ShapeDtypeStruct((rows, width), jnp.float32),
        cost_estimate=LONG,
    )(*terms, *after)


def transposed_after(terms, after):
    value = terms[0]

    def kernel(*refs):
        refs[-1][...] = jnp.transpose(sum(ref[...] for ref in refs[: len(terms)]))

    return pl.pallas_call(
        kernel,
        grid=(1,),
        in_specs=[pl.BlockSpec(value.shape, lambda k: (0, 0)) for _ in terms]
        + [pl.BlockSpec(memory_space=pl.ANY) for _ in after],
        out_specs=pl.BlockSpec(value.shape[::-1], lambda k: (0, 0)),
        out_shape=jax.ShapeDtypeStruct(value.shape[::-1], value.dtype),
        cost_estimate=LONG,
    )(*terms, *after)


def dot_after(left, right, after):
    rows, inner = left.shape
    width = right.shape[1]
    tile = width // 4

    def kernel(left_ref, right_ref, *refs):
        refs[-1][...] = dot(left_ref[...], right_ref[...])

    return pl.pallas_call(
        kernel,
        grid=(4,),
        in_specs=[pl.BlockSpec((rows, inner), lambda k: (0, 0)), pl.BlockSpec((inner, tile), lambda k: (0, k))]
        + [pl.BlockSpec(memory_space=pl.ANY) for _ in after],
        out_specs=pl.BlockSpec((rows, tile), lambda k: (0, k)),
        out_shape=jax.ShapeDtypeStruct((rows, width), jnp.float32),
        cost_estimate=LONG,
        compiler_params=pltpu.CompilerParams(vmem_limit_bytes=40 << 20),
    )(left, right, *after)


def dots_after(lefts, rights, after):
    rows, width, count = lefts[0].shape[0], rights[0].shape[0], len(lefts)
    tile = width // 4

    def kernel(*refs):
        refs[-1][...] = sum(dot_t(refs[k][...], refs[count + k][...]) for k in range(count))

    return pl.pallas_call(
        kernel,
        grid=(4,),
        in_specs=[pl.BlockSpec(left.shape, lambda k: (0, 0)) for left in lefts]
        + [pl.BlockSpec((tile, right.shape[1]), lambda k: (k, 0)) for right in rights]
        + [pl.BlockSpec(memory_space=pl.ANY) for _ in after],
        out_specs=pl.BlockSpec((rows, tile), lambda k: (0, k)),
        out_shape=jax.ShapeDtypeStruct((rows, width), jnp.float32),
        cost_estimate=LONG,
        compiler_params=pltpu.CompilerParams(vmem_limit_bytes=40 << 20),
    )(*lefts, *rights, *after)


class PairFirst:
    def __init__(self, left, right, span, after=()):
        self.left, self.right, self.span = left, right, span
        self.sent = self.whole = self.both = right[0]
        self.plain = lax.axis_size("seq") != 8
        if not self.plain:
            y = lax.axis_index("seq") % 2
            self.places, theirs = pair_places(y), pair_places(1 - y)
            self.sent = blocks_dot(own_terms(left, right, span), theirs, span, after=after)
            self.came = along_pair(self.sent)

    def line(self, after=()):
        if self.plain:
            self.sum = scattered(self.left, [r[:, self.span[0] : self.span[1]] for r in self.right])
            return
        terms = own_terms(self.left, self.right, self.span)
        self.whole = blocks_dot(terms, self.places, self.span, self.came, after)
        self.sum = along_line(self.whole)


class FactorsFirst:
    def __init__(self, left, span, after=()):
        self.left, self.span, self.right, self.came = left, span, [], []
        self.left_came = self.whole = self.sent = left[0]
        self.plain = lax.axis_size("seq") != 8
        if not self.plain:
            y = lax.axis_index("seq") % 2
            self.places = pair_places(y)
            self.left_came = along_pair(picked_columns(left, pair_places(1 - y), after))

    def add(self, right):
        self.right.append(right)
        if not self.plain:
            self.sent = right[:, self.span[0] : self.span[1]].astype(jnp.float32)
            self.came.append(along_pair(self.sent))

    def line(self, after=()):
        if self.plain:
            self.sum = scattered(self.left, [r[:, self.span[0] : self.span[1]] for r in self.right])
            return
        terms, width = own_terms(self.left, self.right, self.span), self.span[1] - self.span[0]
        for n, came in enumerate(self.came):
            terms.append((self.left_came, came.shape[0], lambda k, where, n=n: (n, k), came, (0, width)))
        self.whole = blocks_dot(terms, self.places, self.span, after=after)
        self.sum = along_line(self.whole)


class LineFirst:
    def __init__(self, left, right, span, after=()):
        self.left, self.right, self.span = left, right, span
        self.sent = self.whole = self.both = right[0]
        self.plain = lax.axis_size("seq") != 8
        if not self.plain:
            self.block = left[0].shape[1] // 8
            y = lax.axis_index("seq") % 2
            both = 2 * jnp.arange(4)[:, None] + jnp.stack([y, 1 - y])[None, :]
            self.whole = blocks_dot(own_terms(left, right, span), both.reshape(8).astype(jnp.int32), span, after=after)
            self.both = along_line(self.whole)

    def pair(self, after):
        if not self.plain:
            self.came = along_pair(add_after((self.both[self.block :],), after))

    def end(self, after):
        if self.plain:
            self.sum = scattered(self.left, [r[:, self.span[0] : self.span[1]] for r in self.right])
        else:
            self.sum = add_after((self.both[: self.block], self.came), after)


def pick_by(bit, zero, one):
    return jnp.where(bit == 0, zero, one)


def rms_norm(values):
    scale = lax.rsqrt(jnp.mean(values * values, -1, keepdims=True) + EPS)
    return values * scale, scale


def rms_back(normed, scale, gain, grad):
    d_normed = grad * gain
    d_values = scale * (d_normed - normed * jnp.mean(d_normed * normed, -1, keepdims=True))
    return (d_values, jnp.sum(grad * normed, 0))


CUTS = (0, 256, 512)


def per_device(
    tokens,
    gain_attn,
    query_weight,
    key_weight,
    value_weight,
    output_weight,
    gain_mlp,
    sigmoid_switch_matrix,
    up_weight,
    down_weight,
    segment_ids,
    cotangent,
):
    seq_count, tok_count, model_width = tokens.shape
    narrow, wide = query_weight.shape[1], value_weight.shape[1]
    head_count = narrow // FEAT
    reach = min(lax.axis_size("seq") - 1, -(-(PASSAGE_CEILING - 1) // tok_count))
    assert reach <= 4
    core = lax.axis_index("head") % 2
    order = Order()
    run = order.run

    segments = segment_ids.astype(jnp.float32) + 1.0
    row, column = segments[:, None, :], segments[:, :, None]
    first, last = segments[:, 0], segments[:, -1]

    def meta(*values):
        at = jnp.arange(8)[None, :, None]
        total = jnp.zeros((seq_count, 8, 128), jnp.float32)
        for k, value in enumerate(values):
            total = jnp.where(at == k, value[:, None, None], total)
        return total

    resid = tokens.astype(jnp.float32)
    h_attn = (rms_norm(resid)[0] * gain_attn).astype(jnp.bfloat16)
    h_rows = h_attn.reshape(-1, model_width)

    def project(h_rows, weight):
        return dot(h_rows, weight).astype(jnp.bfloat16).reshape(seq_count, tok_count, -1)

    key_proj, value_proj = project(h_rows, key_weight), project(h_rows, value_weight)
    payload = ((seq_count, head_count, ROWS, HEAD_V), jnp.float32)
    state = run(
        functools.partial(per_sequence, state_kernel, [payload]), key_proj, value_proj, row, meta(first, last)
    )
    near, far = shift(state, 1), shift(state, 2)
    query_rows = run(project, h_rows, query_weight)
    spans = [slice(a, b) for a, b in zip(CUTS[:-1], CUTS[1:])]
    cots = run(lambda cot: [cot[:, s].reshape(-1, model_width) for s in spans], cotangent)

    def at_row(part, k):
        return part[:, :, k : k + 1, :1]

    index = jnp.arange(ROWS)[None, None, :, None]

    def join_two(near, far, first, last):
        carried_near = (
            (at_row(near, FIRST) == at_row(near, LAST)) & (at_row(near, LAST) == at_row(far, LAST))
        ).astype(jnp.float32)
        first, last = first[:, None, None, None], last[:, None, None, None]
        carried = ((first == last) & (last == at_row(near, LAST))).astype(jnp.float32)
        total = jnp.where(index < META, near + carried_near * far, near)
        total = jnp.where(index == NEXT, carried_near, total)
        return jnp.where(index == CARRIED, carried, total), carried

    hidden_width = down_weight.shape[0]
    cut_b = (hidden_width * 3 // 11) // 128 * 128
    cut = (hidden_width * 6 // 11) // 128 * 128
    down_a = FactorsFirst(cots, (cut_b, hidden_width), [query_rows])
    prior_two, carried = run(join_two, near, far, first, last)
    carried = carried[:, 0, 0, 0]

    prior_four = shift(prior_two, 2) if reach > 2 else jnp.zeros_like(prior_two)

    d_hiddens = [run(dot_t, cot, down_weight) for cot in cots]

    block = (seq_count, tok_count)
    mixed, ratio, denominator = run(
        functools.partial(
            per_sequence,
            forward_kernel,
            [(block + (wide,), jnp.bfloat16), (block + (wide,), jnp.float32), (block + (head_count,), jnp.float32)],
        ),
        query_rows, key_proj, value_proj, row, column, prior_two, prior_four,
    )
    head_size = lax.axis_size("head")

    def exchange(parts):
        groups = [[k, k + 1] for k in range(0, head_size, 2)]
        return lax.all_to_all(parts, "head", 0, 0, axis_index_groups=groups, tiled=True)

    def spread(own):
        return exchange(jnp.stack([own, own]))

    def mine(both):
        return jnp.where(core == 0, both[0], both[1])

    def head_part(work, *values):
        def summed(*values):
            both = exchange(work(*values))
            return both[0] + both[1]

        chip = run(summed, *values)
        bit = 2
        while 2 * bit < head_size:
            chip = chip + swap(chip, bit)
            bit *= 2
        return chip, swap(chip, bit) if bit < head_size else jnp.zeros_like(chip)

    def total(pair):
        return pair[0] + pair[1]

    def joined(parts):
        return jnp.concatenate(parts, 0)

    def flat(part):
        return part.reshape(-1, part.shape[-1])

    def paired(part):
        return part.reshape(seq_count, -1, part.shape[-1])

    def branch_part(mixed, weight):
        return paired(dot(flat(mixed), weight))

    branches = [head_part(branch_part, mixed[:, s], output_weight) for s in spans]

    mids, normeds, scales, h_mlps, hiddens, d_gates, d_ups, d_hs = [], [], [], [], [], [], [], []

    def feed(h_mlp, d_hidden, gate_weight, up_weight):
        gate, up = dot(h_mlp, gate_weight), dot(h_mlp, up_weight)
        sigmoid = jax.nn.sigmoid(gate)
        hidden = (gate * sigmoid * up).astype(jnp.bfloat16)
        d_gate = (d_hidden * up * sigmoid * (1.0 + gate * (1.0 - sigmoid))).astype(jnp.bfloat16)
        d_up = (d_hidden * gate * sigmoid).astype(jnp.bfloat16)
        return hidden, d_gate, d_up

    def feed_back(d_gate, d_up, gate_weight, up_weight, after):
        return paired(dots_after((d_gate, d_up), (gate_weight, up_weight), after))

    for k, s in enumerate(spans):
        branch = run(lambda pair: spread(total(pair)), branches[k])

        def middle(tokens, branch):
            mid = tokens.astype(jnp.float32) + branch
            normed, scale = rms_norm(mid)
            return mid, mine(normed), mine(scale), flat((normed * gain_mlp).astype(jnp.bfloat16))

        mid, normed, scale, h_mlp = run(middle, tokens[:, s], branch)
        hidden, d_gate, d_up = run(feed, h_mlp, d_hiddens[k], sigmoid_switch_matrix, up_weight)
        for into, value in zip((mids, normeds, scales, h_mlps, hiddens, d_gates, d_ups),
                               (mid, normed, scale, h_mlp, hidden, d_gate, d_up)):
            into.append(value)
        down_a.add(hidden)
        begun = [down_a.left_came]
        if k == len(spans) - 1:
            down_b = LineFirst(cots, hiddens, (0, cut_b), [down_a.sent])
            gate_a = PairFirst(h_mlps, d_gates, (0, cut), [down_b.whole])
            begun = [gate_a.sent]
        d_hs.append(head_part(feed_back, d_gate, d_up, sigmoid_switch_matrix, up_weight, begun))


    def out_part(k, after):
        return head_part(lambda hidden, weight: paired(dot_after(hidden, weight, after)), hiddens[k], down_weight)

    d_mids, d_branches, d_mixeds = [], [], []

    def middle_back(k, after):
        def work(d_h, normed, scale):
            d_own, d_gain = rms_back(normed, scale, gain_mlp, d_h)
            return spread(d_own), d_gain

        d_norm, d_gain = run(work, add_after(d_hs[k], after), normeds[k], scales[k])

        def work(d_norm, cot, weight):
            d_mid = cot.astype(jnp.float32) + d_norm
            d_branch = flat(d_mid.astype(jnp.bfloat16))
            return mine(d_mid), d_branch, paired(dot_t(d_branch, weight))

        d_mid, d_branch, d_mixed = run(work, d_norm, cotangent[:, spans[k]], output_weight)
        d_mids.append(d_mid)
        d_branches.append(d_branch)
        d_mixeds.append(d_mixed)
        return d_gain

    results = []

    def outcome(k, pair, after):
        own = add_after(pair, after)
        results.append(run(lambda mid, own: (mid + spread(own)).astype(jnp.bfloat16), mids[k], own))

    down_a.line([d_hs[1][0]])
    d_gain_mlp = middle_back(0, [down_a.whole, down_b.both])
    gate_b = PairFirst(h_mlps, d_gates, (cut, hidden_width), [d_mixeds[0]])
    d_gain_mlp = d_gain_mlp + middle_back(1, [gate_b.sent])

    d_mixed = jnp.concatenate(d_mixeds, 1)
    d_state = run(
        functools.partial(per_sequence, state_back_kernel, [payload]),
        query_rows, d_mixed, ratio, denominator, row, prior_two, meta(first, last, carried),
    )
    near, far = shift(d_state, -1), shift(d_state, -2)
    gate_a.line([d_state])
    up_a = PairFirst(h_mlps, d_ups, (0, cut), [gate_a.whole, down_a.sum])
    gate_b.line([up_a.sent])
    mixed_rows = [flat(mixed[:, s]) for s in spans]

    two = per_sequence(
        join_back_kernel, [payload], near, far, jnp.broadcast_to(carried[:, None, None], (seq_count, 1, HEAD_V)),
        after=[gate_b.whole],
    )
    four = shift(two, -2) if reach > 2 else jnp.zeros_like(two)
    out_0 = out_part(0, [two])
    up_b = PairFirst(h_mlps, d_ups, (cut, hidden_width), [out_0[0]])
    d_query, d_key, d_value = run(
        functools.partial(
            per_sequence,
            backward_kernel,
            [(block + (narrow,), jnp.bfloat16), (block + (narrow,), jnp.bfloat16), (block + (wide,), jnp.bfloat16)],
            after=[up_b.sent, gate_a.sum],
        ),
        query_rows, key_proj, value_proj, row, column, d_mixed, ratio, denominator, prior_two, prior_four,
        two, four,
    )

    def in_part(k, after):
        def work(*parts):
            return paired(dots_after([flat(p) for p in parts], (query_weight, key_weight, value_weight), after))

        s = spans[k]
        return head_part(work, d_query[:, s], d_key[:, s], d_value[:, s])

    up_a.line([d_query])
    out = PairFirst(d_branches, mixed_rows, (0, wide), [up_a.whole])
    in_0 = in_part(0, [out.sent, gate_b.sum])
    outcome(0, out_0, [in_0[0]])
    in_1 = in_part(1, [results[0]])
    up_b.line([in_1[0]])
    qkv_right = flat(jnp.concatenate([d_query, d_key, d_value], -1))

    d_tokens = []

    def first_back(k, pair, after):
        def work(d_h, tokens, d_mid):
            normed, scale = rms_norm(mine(tokens).astype(jnp.float32))
            d_own, d_gain = rms_back(normed, scale, gain_attn, d_h)
            return spread(d_own + d_mid), d_gain

        d_part, d_gain = run(work, add_after(pair, after), tokens[:, spans[k]], d_mids[k])
        d_tokens.append(d_part)
        return d_gain

    qkv = PairFirst([h_rows], [qkv_right], (0, qkv_right.shape[1]), [up_b.whole])
    d_gain_attn = first_back(0, in_0, [qkv.sent, up_a.sum])
    out_1 = out_part(1, [d_tokens[0]])
    out.line([out_1[0]])
    qkv.line([out.whole, up_b.sum])
    d_gain_attn = d_gain_attn + first_back(1, in_1, [qkv.whole])
    down_b.pair([d_tokens[1]])
    count = lax.axis_size("seq")

    def gain_blocks(d_gain_attn, d_gain_mlp):
        gains = jnp.sum(spread(jnp.stack([d_gain_attn, d_gain_mlp])), 0)
        if count != 8:
            return gains
        y = lax.axis_index("seq") % 2
        blocks = gains.reshape(2, 4, 2, -1).transpose(2, 1, 0, 3).reshape(2, 8, -1)
        return pick_by(y, blocks[0], blocks[1]), pick_by(y, blocks[1], blocks[0])

    gains = run(gain_blocks, d_gain_attn, d_gain_mlp)
    if count == 8:
        gains_came = along_pair(gains[1])
    if count == 8:
        gains = along_line(add_after((gains[0], gains_came), [d_tokens[1]]))
    else:
        gains = lax.psum_scatter(gains, "seq", scatter_dimension=1, tiled=True)
    outcome(1, out_1, [d_tokens[1], out.sum])
    down_b.end([results[1]])
    output_weight_gradient = transposed_after([out.sum], [qkv.whole])
    qkv = qkv.sum
    result = jnp.concatenate(results, 1)
    d_tokens = jnp.concatenate(d_tokens, 1)
    down = jnp.concatenate([down_b.sum, down_a.sum], 1).T
    gate = jnp.concatenate([gate_a.sum, gate_b.sum], 1)
    up = jnp.concatenate([up_a.sum, up_b.sum], 1)
    return (
        result,
        d_tokens,
        gains[0],
        qkv[:, :narrow],
        qkv[:, narrow : 2 * narrow],
        qkv[:, 2 * narrow :],
        output_weight_gradient,
        gains[1],
        gate,
        up,
        down,
    )


def solution(mesh):
    return jax.shard_map(
        per_device,
        mesh=mesh,
        in_specs=(
            P(None, "seq", None),
            P(),
            P(None, "head"),
            P(None, "head"),
            P(None, "head"),
            P("head", None),
            P(),
            P(None, "head"),
            P(None, "head"),
            P("head", None),
            P(None, "seq"),
            P(None, "seq", None),
        ),
        out_specs=(
            P(None, "seq", None),
            P(None, "seq", None),
            P("seq"),
            P("seq", "head"),
            P("seq", "head"),
            P("seq", "head"),
            P("head", "seq"),
            P("seq"),
            P("seq", "head"),
            P("seq", "head"),
            P("head", "seq"),
        ),
        check_vma=False,
    )
```

```python
import functools
import math

import jax
import jax.numpy as jnp
from jax import lax
from jax.experimental import pallas as pl
from jax.experimental.pallas import tpu as pltpu
from jax.sharding import PartitionSpec as P

FEAT = 16
HEAD_V = 128
EPS = 1e-05
PASSAGE_CEILING = 2000

MAPPED = 160
NORM = MAPPED
META = MAPPED + 2
ROWS = MAPPED + 8
FIRST, LAST, CARRIED, NEXT = META, META + 1, META + 2, META + 3

LONG = pl.CostEstimate(flops=1 << 39, bytes_accessed=1 << 20, transcendentals=0)


def swap(part, bit):
    count = lax.axis_size("head")
    return lax.ppermute(part, "head", [(k, k ^ bit) for k in range(count)])


def shift(part, by):
    count = lax.axis_size("seq")
    return lax.ppermute(part, "seq", [(k, k + by) for k in range(count) if 0 <= k + by < count])


def dot(left, right):
    return jnp.dot(left, right, preferred_element_type=jnp.float32)


def dot_t(left, right):
    return lax.dot_general(left, right, (((1,), (1,)), ((), ())), preferred_element_type=jnp.float32)


def columns_dot(left, right):
    return lax.dot_general(left, right, (((0,), (0,)), ((), ())), preferred_element_type=jnp.float32)


class Order:
    def __init__(self):
        self.last = None

    def after(self, *values):
        if self.last is not None:
            leaves, tree = jax.tree.flatten(values)
            values = jax.tree.unflatten(tree, lax.optimization_barrier((*leaves, self.last))[:-1])
        return values if len(values) > 1 else values[0]

    def mark(self, value):
        self.last = jax.tree.leaves(value)[0]
        return value

    def run(self, work, *values):
        if len(values) == 1:
            return self.mark(work(self.after(values[0])))
        return self.mark(work(*self.after(*values)))


def features(feats):
    row = lax.broadcasted_iota(jnp.int32, (8, feats.shape[1]), 0)
    parts = [jnp.where(row == 0, 1.0, 0.0), feats * 0.5, feats * feats * (1.0 / math.sqrt(32.0))]
    for k in range(1, 8):
        parts.append(feats * jnp.concatenate([feats[k:], feats[:k]], 0) * 0.25)
    parts.append(feats[:8] * feats[8:] * 0.25)
    return jnp.concatenate(parts, 0)


def features_back(feats, grad):
    total = grad[8:24] * 0.5 + grad[24:40] * feats * (2.0 / math.sqrt(32.0))
    for k in range(1, 8):
        part = grad[24 + 16 * k : 40 + 16 * k] * 0.25
        back = part * feats
        total = total + part * jnp.concatenate([feats[k:], feats[:k]], 0)
        total = total + jnp.concatenate([back[16 - k :], back[: 16 - k]], 0)
    part = grad[152:160] * 0.25
    return total + jnp.concatenate([part * feats[8:], part * feats[:8]], 0)


def low(value):
    return value.astype(jnp.bfloat16)


def dot_general(left, right, a, b):
    return lax.dot_general(left, right, (((a,), (b,)), ((), ())), preferred_element_type=jnp.float32)


def put_state(out_ref, h, mapped, right, weights, meta):
    mapped = low(mapped)
    out_ref[0, h, :MAPPED, :] = dot_general(mapped, right, 1, 0)
    norm = dot_general(weights, mapped, 0, 1)
    rest = jnp.concatenate([norm[:, 128:], jnp.zeros((8, 256 - MAPPED), jnp.float32)], 1)
    at = lax.broadcasted_iota(jnp.int32, (8, HEAD_V), 0)
    out_ref[0, h, NORM:, :] = jnp.where(at == 0, norm[:, :128], jnp.where(at == 1, rest, meta))


def get_state(refs, h):
    two, four = refs
    joined = two[0, h] + two[0, h, NEXT : NEXT + 1, :1] * four[0, h, CARRIED : CARRIED + 1, :1] * four[0, h]
    norm = jnp.concatenate([joined[NORM : NORM + 1], joined[NORM + 1 : NORM + 2, : MAPPED - 128]], 1)
    return low(joined[:MAPPED]), low(jnp.broadcast_to(norm, (8, MAPPED)))


def transposed(ref):
    return jnp.transpose(ref[0].astype(jnp.float32))


def state_kernel(key_ref, value_ref, row_ref, meta_ref, out_ref):
    heads = key_ref.shape[2] // FEAT
    row = row_ref[0]
    tail = jnp.where(row == row[:, row.shape[1] - 1 :], 1.0, 0.0)
    key_t = transposed(key_ref)
    ones = jnp.ones((key_ref.shape[1], 8), jnp.bfloat16)
    for h in range(heads):
        mapped = features(key_t[FEAT * h : FEAT * (h + 1)]) * tail
        put_state(out_ref, h, mapped, value_ref[0, :, HEAD_V * h : HEAD_V * (h + 1)], ones, meta_ref[0])


def seen(row_ref, column_ref):
    row, column = row_ref[0], column_ref[0]
    shape = (column.shape[0], row.shape[1])
    causal = lax.broadcasted_iota(jnp.int32, shape, 0) >= lax.broadcasted_iota(jnp.int32, shape, 1)
    return causal & (column == row)


def forward_kernel(
    query_ref, key_ref, value_ref, row_ref, column_ref, prior_ref, prior_four_ref, mixed_ref, ratio_ref, denom_ref
):
    heads = key_ref.shape[2] // FEAT
    visible = seen(row_ref, column_ref)
    uses = jnp.where(column_ref[0] == prior_ref[0, 0, LAST : LAST + 1, :1], 1.0, 0.0)
    query_t = transposed(query_ref)
    ones = jnp.ones((key_ref.shape[1], HEAD_V), jnp.bfloat16)
    for h in range(heads):
        narrow, wide = slice(FEAT * h, FEAT * (h + 1)), slice(HEAD_V * h, HEAD_V * (h + 1))
        kernel_dot = dot_general(query_ref[0, :, narrow], key_ref[0, :, narrow], 1, 1) * 0.25
        scores = low(jnp.where(visible, 1.0 + kernel_dot + 0.5 * kernel_dot * kernel_dot, 0.0))
        both = dot(scores, jnp.concatenate([value_ref[0, :, wide], ones], 1))
        mapped = low(features(query_t[narrow]))
        state, norm = get_state((prior_ref, prior_four_ref), h)
        numerator = both[:, :HEAD_V] + uses * dot_general(mapped, state, 0, 0)
        denominator = both[:, HEAD_V : HEAD_V + 1] + uses * dot_general(mapped, norm, 0, 1)[:, :1]
        ratio = numerator / denominator
        mixed_ref[0, :, wide] = low(ratio)
        ratio_ref[0, :, wide] = ratio
        denom_ref[0, :, h : h + 1] = denominator


def numer_back(h, d_mixed_ref, ratio_ref, denom_ref):
    wide = slice(HEAD_V * h, HEAD_V * (h + 1))
    inverse = 1.0 / denom_ref[0, :, h : h + 1]
    d_mixed = d_mixed_ref[0, :, wide]
    d_denom = -jnp.sum(d_mixed * ratio_ref[0, :, wide], 1, keepdims=True) * inverse
    return low(d_mixed * inverse), d_denom


def state_back_kernel(query_ref, d_mixed_ref, ratio_ref, denom_ref, row_ref, prior_ref, meta_ref, out_ref):
    heads = query_ref.shape[2] // FEAT
    uses = jnp.where(row_ref[0] == prior_ref[0, 0, LAST : LAST + 1, :1], 1.0, 0.0)
    query_t = transposed(query_ref)
    for h in range(heads):
        d_numer, d_denom = numer_back(h, d_mixed_ref, ratio_ref, denom_ref)
        mapped = features(query_t[FEAT * h : FEAT * (h + 1)]) * uses
        put_state(out_ref, h, mapped, d_numer, low(jnp.broadcast_to(d_denom, (d_denom.shape[0], 8))), meta_ref[0])


def join_back_kernel(near_ref, far_ref, carried_ref, out_ref):
    for h in range(near_ref.shape[1]):
        near, far = near_ref[0, h], far_ref[0, h]
        at = lax.broadcasted_iota(jnp.int32, near.shape, 0)
        total = jnp.where(at < META, near + near[CARRIED : CARRIED + 1, :1] * far, near)
        total = jnp.where(at == NEXT, near[CARRIED : CARRIED + 1, :1], total)
        out_ref[0, h] = jnp.where(at == CARRIED, carried_ref[0], total)


def backward_kernel(
    query_ref, key_ref, value_ref, row_ref, column_ref, d_mixed_ref, ratio_ref, denom_ref, prior_ref, prior_four_ref,
    later_ref, later_four_ref, d_query_ref, d_key_ref, d_value_ref,
):
    heads = key_ref.shape[2] // FEAT
    visible = seen(row_ref, column_ref)
    row, column = row_ref[0], column_ref[0]
    uses = jnp.where(row == prior_ref[0, 0, LAST : LAST + 1, :1], 1.0, 0.0)
    end = row.shape[1] - 1
    tail = jnp.where(row == row[:, end:], 1.0, 0.0)
    tail_column = jnp.where(column == row[:, end:], 1.0, 0.0)
    query_t, key_t = transposed(query_ref), transposed(key_ref)
    d_queries, d_keys = [], []
    for h in range(heads):
        narrow, wide = slice(FEAT * h, FEAT * (h + 1)), slice(HEAD_V * h, HEAD_V * (h + 1))
        query, key, value = query_ref[0, :, narrow], key_ref[0, :, narrow], value_ref[0, :, wide]
        d_numer, d_denom = numer_back(h, d_mixed_ref, ratio_ref, denom_ref)
        kernel_dot = dot_general(query, key, 1, 1) * 0.25
        scores = low(jnp.where(visible, 1.0 + kernel_dot + 0.5 * kernel_dot * kernel_dot, 0.0))
        d_scores = low(jnp.where(visible, dot_general(d_numer, value, 1, 1) + d_denom, 0.0))
        d_kernel = low(d_scores.astype(jnp.float32) * (1.0 + kernel_dot))
        d_query = dot_general(key, d_kernel, 0, 1) * 0.25
        d_key = dot_general(query, d_kernel, 0, 0) * 0.25
        d_value = dot_general(scores, d_numer, 0, 0)

        wide_denom = low(jnp.broadcast_to(d_denom, (d_denom.shape[0], 8)))
        state, norm = get_state((prior_ref, prior_four_ref), h)
        mapped_back = dot_general(state, d_numer, 1, 1)
        mapped_back = mapped_back + dot_general(norm, wide_denom, 0, 1) * 0.125
        d_queries.append(d_query + features_back(query_t[narrow], mapped_back * uses))

        later, norm = get_state((later_ref, later_four_ref), h)
        mapped_back = dot_general(later, value, 1, 1)
        mapped_back = mapped_back + dot_general(norm, jnp.ones((value.shape[0], 8), jnp.bfloat16), 0, 1) * 0.125
        d_keys.append(d_key + features_back(key_t[narrow], mapped_back * tail))
        d_value = d_value + tail_column * dot_general(low(features(key_t[narrow])), later, 0, 0)
        d_value_ref[0, :, wide] = low(d_value)
    d_query_ref[0] = low(jnp.transpose(jnp.concatenate(d_queries, 0)))
    d_key_ref[0] = low(jnp.transpose(jnp.concatenate(d_keys, 0)))


def per_sequence(kernel, out_shapes, *arrays, after=()):
    def spec(shape):
        rest = (0,) * (len(shape) - 1)
        return pl.BlockSpec((1,) + tuple(shape[1:]), lambda s: (s,) + rest)

    def body(*refs):
        kernel(*refs[: len(arrays)], *refs[len(arrays) + len(after) :])

    outs = [jax.ShapeDtypeStruct(shape, dtype) for shape, dtype in out_shapes]
    result = pl.pallas_call(
        body,
        grid=(arrays[0].shape[0],),
        in_specs=[spec(a.shape) for a in arrays] + [pl.BlockSpec(memory_space=pl.ANY) for _ in after],
        out_specs=[spec(o.shape) for o in outs],
        out_shape=outs,
        cost_estimate=LONG,
        compiler_params=pltpu.CompilerParams(vmem_limit_bytes=48 << 20),
    )(*arrays, *after)
    return result if len(outs) > 1 else result[0]


def along_pair(part):
    return lax.ppermute(part, "seq", [(k, k ^ 1) for k in range(lax.axis_size("seq"))])


def along_line(parts):
    groups = [[k for k in range(8) if k % 2 == y] for y in range(2)]
    return lax.psum_scatter(parts, "seq", scatter_dimension=0, axis_index_groups=groups, tiled=True)


def scattered(left, right):
    rows, columns = jnp.concatenate(left, 0), jnp.concatenate(right, 0)
    return lax.psum_scatter(columns_dot(rows, columns), "seq", scatter_dimension=0, tiled=True)


def named(k, where):
    return 0, where[k]


def blocks_dot(terms, where, span, came=None, after=()):
    parts = len(terms)
    block = terms[0][0].shape[1] // lax.axis_size("seq")
    count, width = where.shape[0], span[1] - span[0]

    wide = [t[3].dtype != jnp.bfloat16 for t in terms]
    scratch = [pltpu.VMEM((t[3].shape[0], width), jnp.bfloat16) for t, w in zip(terms, wide) if w]

    def kernel(where_ref, *refs):
        lefts, rights = refs[:parts], refs[parts : 2 * parts]
        out_ref, narrow = refs[len(refs) - 1 - len(scratch)], list(refs[len(refs) - len(scratch) :])
        total = refs[2 * parts][...] if came is not None else None
        for n in range(parts):
            left_ref, columns = lefts[n], slice(*terms[n][4])
            if wide[n]:
                kept_ref = narrow.pop(0)

                @pl.when(pl.program_id(0) == 0)
                def _():
                    kept_ref[...] = low(rights[n][:, columns])

                right = kept_ref[...]
            else:
                right = rights[n][:, columns]
            part = dot_general(low(left_ref[...]), right, 0, 0)
            total = part if total is None else total + part
        out_ref[...] = total

    specs = [pl.BlockSpec((rows, block), at) for _, rows, at, _, _ in terms]
    specs += [pl.BlockSpec(right.shape, lambda k, where: (0, 0)) for _, _, _, right, _ in terms]
    extra = []
    if came is not None:
        specs.append(pl.BlockSpec((block, width), lambda k, where: (k, 0)))
        extra.append(came)
    specs += [pl.BlockSpec(memory_space=pl.ANY) for _ in after]
    return pl.pallas_call(
        kernel,
        grid_spec=pltpu.PrefetchScalarGridSpec(
            num_scalar_prefetch=1,
            grid=(count,),
            in_specs=specs,
            out_specs=pl.BlockSpec((block, width), lambda k, where: (k, 0)),
            scratch_shapes=scratch,
        ),
        out_shape=jax.ShapeDtypeStruct((count * block, width), jnp.float32),
        compiler_params=pltpu.CompilerParams(vmem_limit_bytes=44 << 20),
        cost_estimate=LONG,
    )(where, *[t[0] for t in terms], *[t[3] for t in terms], *extra, *after)


def own_terms(left, right, span):
    return [(l, l.shape[0], named, r, span) for l, r in zip(left, right)]


def pair_places(y):
    return (2 * jnp.arange(4) + y).astype(jnp.int32)


def picked_columns(chunks, where, after=()):
    block = chunks[0].shape[1] // 8
    rows = [c.shape[0] for c in chunks]

    def kernel(where_ref, *refs):
        at = 0
        for ref, count in zip(refs, rows):
            refs[-1][at : at + count] = ref[...].astype(jnp.float32)
            at += count

    return pl.pallas_call(
        kernel,
        grid_spec=pltpu.PrefetchScalarGridSpec(
            num_scalar_prefetch=1,
            grid=(where.shape[0],),
            in_specs=[pl.BlockSpec((count, block), named) for count in rows]
            + [pl.BlockSpec(memory_space=pl.ANY) for _ in after],
            out_specs=pl.BlockSpec((sum(rows), block), lambda k, where: (0, k)),
        ),
        out_shape=jax.ShapeDtypeStruct((sum(rows), where.shape[0] * block), jnp.float32),
        cost_estimate=LONG,
    )(where, *chunks, *after)


def add_after(terms, after):
    rows, width = terms[0].shape
    steps = 4 if rows % 32 == 0 else 1

    def kernel(*refs):
        refs[-1][...] = sum(ref[...] for ref in refs[: len(terms)])

    spec = pl.BlockSpec((rows // steps, width), lambda k: (k, 0))
    return pl.pallas_call(
        kernel,
        grid=(steps,),
        in_specs=[spec] * len(terms) + [pl.BlockSpec(memory_space=pl.ANY) for _ in after],
        out_specs=spec,
        out_shape=jax.ShapeDtypeStruct((rows, width), jnp.float32),
        cost_estimate=LONG,
    )(*terms, *after)


def transposed_after(terms, after):
    value = terms[0]

    def kernel(*refs):
        refs[-1][...] = jnp.transpose(sum(ref[...] for ref in refs[: len(terms)]))

    return pl.pallas_call(
        kernel,
        grid=(1,),
        in_specs=[pl.BlockSpec(value.shape, lambda k: (0, 0)) for _ in terms]
        + [pl.BlockSpec(memory_space=pl.ANY) for _ in after],
        out_specs=pl.BlockSpec(value.shape[::-1], lambda k: (0, 0)),
        out_shape=jax.ShapeDtypeStruct(value.shape[::-1], value.dtype),
        cost_estimate=LONG,
    )(*terms, *after)


def dot_after(left, right, after):
    rows, inner = left.shape
    width = right.shape[1]
    tile = width // 4

    def kernel(left_ref, right_ref, *refs):
        refs[-1][...] = dot(left_ref[...], right_ref[...])

    return pl.pallas_call(
        kernel,
        grid=(4,),
        in_specs=[pl.BlockSpec((rows, inner), lambda k: (0, 0)), pl.BlockSpec((inner, tile), lambda k: (0, k))]
        + [pl.BlockSpec(memory_space=pl.ANY) for _ in after],
        out_specs=pl.BlockSpec((rows, tile), lambda k: (0, k)),
        out_shape=jax.ShapeDtypeStruct((rows, width), jnp.float32),
        cost_estimate=LONG,
        compiler_params=pltpu.CompilerParams(vmem_limit_bytes=40 << 20),
    )(left, right, *after)


def dots_after(lefts, rights, after):
    rows, width, count = lefts[0].shape[0], rights[0].shape[0], len(lefts)
    tile = width // 4

    def kernel(*refs):
        refs[-1][...] = sum(dot_t(refs[k][...], refs[count + k][...]) for k in range(count))

    return pl.pallas_call(
        kernel,
        grid=(4,),
        in_specs=[pl.BlockSpec(left.shape, lambda k: (0, 0)) for left in lefts]
        + [pl.BlockSpec((tile, right.shape[1]), lambda k: (k, 0)) for right in rights]
        + [pl.BlockSpec(memory_space=pl.ANY) for _ in after],
        out_specs=pl.BlockSpec((rows, tile), lambda k: (0, k)),
        out_shape=jax.ShapeDtypeStruct((rows, width), jnp.float32),
        cost_estimate=LONG,
        compiler_params=pltpu.CompilerParams(vmem_limit_bytes=40 << 20),
    )(*lefts, *rights, *after)


class PairFirst:
    def __init__(self, left, right, span, after=()):
        self.left, self.right, self.span = left, right, span
        self.sent = self.whole = self.both = right[0]
        self.plain = lax.axis_size("seq") != 8
        if not self.plain:
            y = lax.axis_index("seq") % 2
            self.places, theirs = pair_places(y), pair_places(1 - y)
            self.sent = blocks_dot(own_terms(left, right, span), theirs, span, after=after)
            self.came = along_pair(self.sent)

    def line(self, after=()):
        if self.plain:
            self.sum = scattered(self.left, [r[:, self.span[0] : self.span[1]] for r in self.right])
            return
        terms = own_terms(self.left, self.right, self.span)
        self.whole = blocks_dot(terms, self.places, self.span, self.came, after)
        self.sum = along_line(self.whole)


class FactorsFirst:
    def __init__(self, left, span, after=()):
        self.left, self.span, self.right, self.came = left, span, [], []
        self.left_came = self.whole = self.sent = left[0]
        self.plain = lax.axis_size("seq") != 8
        if not self.plain:
            y = lax.axis_index("seq") % 2
            self.places = pair_places(y)
            self.left_came = along_pair(picked_columns(left, pair_places(1 - y), after))

    def add(self, right):
        self.right.append(right)
        if not self.plain:
            self.sent = right[:, self.span[0] : self.span[1]].astype(jnp.float32)
            self.came.append(along_pair(self.sent))

    def line(self, after=()):
        if self.plain:
            self.sum = scattered(self.left, [r[:, self.span[0] : self.span[1]] for r in self.right])
            return
        terms, width = own_terms(self.left, self.right, self.span), self.span[1] - self.span[0]
        for n, came in enumerate(self.came):
            terms.append((self.left_came, came.shape[0], lambda k, where, n=n: (n, k), came, (0, width)))
        self.whole = blocks_dot(terms, self.places, self.span, after=after)
        self.sum = along_line(self.whole)


class LineFirst:
    def __init__(self, left, right, span, after=()):
        self.left, self.right, self.span = left, right, span
        self.sent = self.whole = self.both = right[0]
        self.plain = lax.axis_size("seq") != 8
        if not self.plain:
            self.block = left[0].shape[1] // 8
            y = lax.axis_index("seq") % 2
            both = 2 * jnp.arange(4)[:, None] + jnp.stack([y, 1 - y])[None, :]
            self.whole = blocks_dot(own_terms(left, right, span), both.reshape(8).astype(jnp.int32), span, after=after)
            self.both = along_line(self.whole)

    def pair(self, after):
        if not self.plain:
            self.came = along_pair(add_after((self.both[self.block :],), after))

    def end(self, after):
        if self.plain:
            self.sum = scattered(self.left, [r[:, self.span[0] : self.span[1]] for r in self.right])
        else:
            self.sum = add_after((self.both[: self.block], self.came), after)


def pick_by(bit, zero, one):
    return jnp.where(bit == 0, zero, one)


def rms_norm(values):
    scale = lax.rsqrt(jnp.mean(values * values, -1, keepdims=True) + EPS)
    return values * scale, scale


def rms_back(normed, scale, gain, grad):
    d_normed = grad * gain
    d_values = scale * (d_normed - normed * jnp.mean(d_normed * normed, -1, keepdims=True))
    return (d_values, jnp.sum(grad * normed, 0))


CUTS = (0, 256, 512)


def per_device(
    tokens,
    gain_attn,
    query_weight,
    key_weight,
    value_weight,
    output_weight,
    gain_mlp,
    sigmoid_switch_matrix,
    up_weight,
    down_weight,
    segment_ids,
    cotangent,
):
    seq_count, tok_count, model_width = tokens.shape
    narrow, wide = query_weight.shape[1], value_weight.shape[1]
    head_count = narrow // FEAT
    reach = min(lax.axis_size("seq") - 1, -(-(PASSAGE_CEILING - 1) // tok_count))
    assert reach <= 4
    core = lax.axis_index("head") % 2
    order = Order()
    run = order.run

    segments = segment_ids.astype(jnp.float32) + 1.0
    row, column = segments[:, None, :], segments[:, :, None]
    first, last = segments[:, 0], segments[:, -1]

    def meta(*values):
        at = jnp.arange(8)[None, :, None]
        total = jnp.zeros((seq_count, 8, 128), jnp.float32)
        for k, value in enumerate(values):
            total = jnp.where(at == k + META - NORM, value[:, None, None], total)
        return total

    resid = tokens.astype(jnp.float32)
    h_attn = (rms_norm(resid)[0] * gain_attn).astype(jnp.bfloat16)
    h_rows = h_attn.reshape(-1, model_width)

    def project(h_rows, weight):
        return dot(h_rows, weight).astype(jnp.bfloat16).reshape(seq_count, tok_count, -1)

    key_proj, value_proj = project(h_rows, key_weight), project(h_rows, value_weight)
    payload = ((seq_count, head_count, ROWS, HEAD_V), jnp.float32)
    state = run(
        functools.partial(per_sequence, state_kernel, [payload]), key_proj, value_proj, row, meta(first, last)
    )
    near, far = shift(state, 1), shift(state, 2)
    query_rows = run(project, h_rows, query_weight)
    spans = [slice(a, b) for a, b in zip(CUTS[:-1], CUTS[1:])]
    cots = run(lambda cot: [cot[:, s].reshape(-1, model_width) for s in spans], cotangent)

    def at_row(part, k):
        return part[:, :, k : k + 1, :1]

    index = jnp.arange(ROWS)[None, None, :, None]

    def join_two(near, far, first, last):
        carried_near = (
            (at_row(near, FIRST) == at_row(near, LAST)) & (at_row(near, LAST) == at_row(far, LAST))
        ).astype(jnp.float32)
        first, last = first[:, None, None, None], last[:, None, None, None]
        carried = ((first == last) & (last == at_row(near, LAST))).astype(jnp.float32)
        total = jnp.where(index < META, near + carried_near * far, near)
        total = jnp.where(index == NEXT, carried_near, total)
        return jnp.where(index == CARRIED, carried, total), carried

    hidden_width = down_weight.shape[0]
    cut_b = (hidden_width * 3 // 11) // 128 * 128
    cut = (hidden_width * 6 // 11) // 128 * 128
    down_a = FactorsFirst(cots, (cut_b, hidden_width), [query_rows])
    prior_two, carried = run(join_two, near, far, first, last)
    carried = carried[:, 0, 0, 0]

    prior_four = shift(prior_two, 2) if reach > 2 else jnp.zeros_like(prior_two)

    d_hiddens = [run(dot_t, cot, down_weight) for cot in cots]

    block = (seq_count, tok_count)
    mixed, ratio, denominator = run(
        functools.partial(
            per_sequence,
            forward_kernel,
            [(block + (wide,), jnp.bfloat16), (block + (wide,), jnp.float32), (block + (head_count,), jnp.float32)],
        ),
        query_rows, key_proj, value_proj, row, column, prior_two, prior_four,
    )
    head_size = lax.axis_size("head")

    def exchange(parts):
        groups = [[k, k + 1] for k in range(0, head_size, 2)]
        return lax.all_to_all(parts, "head", 0, 0, axis_index_groups=groups, tiled=True)

    def spread(own):
        return exchange(jnp.stack([own, own]))

    def mine(both):
        return jnp.where(core == 0, both[0], both[1])

    def head_part(work, *values):
        def summed(*values):
            both = exchange(work(*values))
            return both[0] + both[1]

        chip = run(summed, *values)
        bit = 2
        while 2 * bit < head_size:
            chip = chip + swap(chip, bit)
            bit *= 2
        return chip, swap(chip, bit) if bit < head_size else jnp.zeros_like(chip)

    def total(pair):
        return pair[0] + pair[1]

    def joined(parts):
        return jnp.concatenate(parts, 0)

    def flat(part):
        return part.reshape(-1, part.shape[-1])

    def paired(part):
        return part.reshape(seq_count, -1, part.shape[-1])

    def branch_part(mixed, weight):
        return paired(dot(flat(mixed), weight))

    branches = [head_part(branch_part, mixed[:, s], output_weight) for s in spans]

    mids, normeds, scales, h_mlps, hiddens, d_gates, d_ups, d_hs = [], [], [], [], [], [], [], []

    def feed(h_mlp, d_hidden, gate_weight, up_weight):
        gate, up = dot(h_mlp, gate_weight), dot(h_mlp, up_weight)
        sigmoid = jax.nn.sigmoid(gate)
        hidden = (gate * sigmoid * up).astype(jnp.bfloat16)
        d_gate = (d_hidden * up * sigmoid * (1.0 + gate * (1.0 - sigmoid))).astype(jnp.bfloat16)
        d_up = (d_hidden * gate * sigmoid).astype(jnp.bfloat16)
        return hidden, d_gate, d_up

    def feed_back(d_gate, d_up, gate_weight, up_weight, after):
        return paired(dots_after((d_gate, d_up), (gate_weight, up_weight), after))

    for k, s in enumerate(spans):
        branch = run(lambda pair: spread(total(pair)), branches[k])

        def middle(tokens, branch):
            mid = tokens.astype(jnp.float32) + branch
            normed, scale = rms_norm(mid)
            return mid, mine(normed), mine(scale), flat((normed * gain_mlp).astype(jnp.bfloat16))

        mid, normed, scale, h_mlp = run(middle, tokens[:, s], branch)
        hidden, d_gate, d_up = run(feed, h_mlp, d_hiddens[k], sigmoid_switch_matrix, up_weight)
        for into, value in zip((mids, normeds, scales, h_mlps, hiddens, d_gates, d_ups),
                               (mid, normed, scale, h_mlp, hidden, d_gate, d_up)):
            into.append(value)
        down_a.add(hidden)
        begun = [down_a.left_came]
        if k == len(spans) - 1:
            down_b = LineFirst(cots, hiddens, (0, cut_b), [down_a.sent])
            gate_a = PairFirst(h_mlps, d_gates, (0, cut), [down_b.whole])
            begun = [gate_a.sent]
        d_hs.append(head_part(feed_back, d_gate, d_up, sigmoid_switch_matrix, up_weight, begun))


    def out_part(k, after):
        return head_part(lambda hidden, weight: paired(dot_after(hidden, weight, after)), hiddens[k], down_weight)

    d_mids, d_branches, d_mixeds = [], [], []

    def middle_back(k, after):
        def work(d_h, normed, scale):
            d_own, d_gain = rms_back(normed, scale, gain_mlp, d_h)
            return spread(d_own), d_gain

        d_norm, d_gain = run(work, add_after(d_hs[k], after), normeds[k], scales[k])

        def work(d_norm, cot, weight):
            d_mid = cot.astype(jnp.float32) + d_norm
            d_branch = flat(d_mid.astype(jnp.bfloat16))
            return mine(d_mid), d_branch, paired(dot_t(d_branch, weight))

        d_mid, d_branch, d_mixed = run(work, d_norm, cotangent[:, spans[k]], output_weight)
        d_mids.append(d_mid)
        d_branches.append(d_branch)
        d_mixeds.append(d_mixed)
        return d_gain

    results = []

    def outcome(k, pair, after):
        own = add_after(pair, after)
        results.append(run(lambda mid, own: (mid + spread(own)).astype(jnp.bfloat16), mids[k], own))

    down_a.line([d_hs[1][0]])
    d_gain_mlp = middle_back(0, [down_a.whole, down_b.both])
    gate_b = PairFirst(h_mlps, d_gates, (cut, hidden_width), [d_mixeds[0]])
    d_gain_mlp = d_gain_mlp + middle_back(1, [gate_b.sent])

    d_mixed = jnp.concatenate(d_mixeds, 1)
    d_state = run(
        functools.partial(per_sequence, state_back_kernel, [payload]),
        query_rows, d_mixed, ratio, denominator, row, prior_two, meta(first, last, carried),
    )
    near, far = shift(d_state, -1), shift(d_state, -2)
    gate_a.line([d_state])
    up_a = PairFirst(h_mlps, d_ups, (0, cut), [gate_a.whole, down_a.sum])
    gate_b.line([up_a.sent])
    mixed_rows = [flat(mixed[:, s]) for s in spans]

    two = per_sequence(
        join_back_kernel, [payload], near, far, jnp.broadcast_to(carried[:, None, None], (seq_count, 1, HEAD_V)),
        after=[gate_b.whole],
    )
    four = shift(two, -2) if reach > 2 else jnp.zeros_like(two)
    out_0 = out_part(0, [two])
    up_b = PairFirst(h_mlps, d_ups, (cut, hidden_width), [out_0[0]])
    d_query, d_key, d_value = run(
        functools.partial(
            per_sequence,
            backward_kernel,
            [(block + (narrow,), jnp.bfloat16), (block + (narrow,), jnp.bfloat16), (block + (wide,), jnp.bfloat16)],
            after=[up_b.sent, gate_a.sum],
        ),
        query_rows, key_proj, value_proj, row, column, d_mixed, ratio, denominator, prior_two, prior_four,
        two, four,
    )

    def in_part(k, after):
        def work(*parts):
            return paired(dots_after([flat(p) for p in parts], (query_weight, key_weight, value_weight), after))

        s = spans[k]
        return head_part(work, d_query[:, s], d_key[:, s], d_value[:, s])

    up_a.line([d_query])
    qkv_right = flat(jnp.concatenate([d_query, d_key, d_value], -1))
    qkv = PairFirst([h_rows], [qkv_right], (0, qkv_right.shape[1]), [up_a.whole])
    in_0 = in_part(0, [qkv.sent, gate_b.sum])
    outcome(0, out_0, [in_0[0]])
    in_1 = in_part(1, [results[0]])
    up_b.line([in_1[0]])

    d_tokens = []

    def first_back(k, pair, after):
        def work(d_h, tokens, d_mid):
            normed, scale = rms_norm(mine(tokens).astype(jnp.float32))
            d_own, d_gain = rms_back(normed, scale, gain_attn, d_h)
            return spread(d_own + d_mid), d_gain

        d_part, d_gain = run(work, add_after(pair, after), tokens[:, spans[k]], d_mids[k])
        d_tokens.append(d_part)
        return d_gain

    out = PairFirst(d_branches, mixed_rows, (0, wide), [up_b.whole])
    d_gain_attn = first_back(0, in_0, [out.sent, up_a.sum])
    out_1 = out_part(1, [d_tokens[0]])
    qkv.line([out_1[0]])
    out.line([qkv.whole, up_b.sum])
    d_gain_attn = d_gain_attn + first_back(1, in_1, [out.whole])
    down_b.pair([d_tokens[1]])
    count = lax.axis_size("seq")

    def gain_blocks(d_gain_attn, d_gain_mlp):
        gains = jnp.sum(spread(jnp.stack([d_gain_attn, d_gain_mlp])), 0)
        if count != 8:
            return gains
        y = lax.axis_index("seq") % 2
        blocks = gains.reshape(2, 4, 2, -1).transpose(2, 1, 0, 3).reshape(2, 8, -1)
        return pick_by(y, blocks[0], blocks[1]), pick_by(y, blocks[1], blocks[0])

    gains = run(gain_blocks, d_gain_attn, d_gain_mlp)
    if count == 8:
        gains_came = along_pair(gains[1])
    if count == 8:
        gains = along_line(add_after((gains[0], gains_came), [d_tokens[1]]))
    else:
        gains = lax.psum_scatter(gains, "seq", scatter_dimension=1, tiled=True)
    outcome(1, out_1, [d_tokens[1], qkv.sum])
    down_b.end([results[1]])
    output_weight_gradient = transposed_after([out.sum], [results[1]])
    qkv = qkv.sum
    result = jnp.concatenate(results, 1)
    d_tokens = jnp.concatenate(d_tokens, 1)
    down = jnp.concatenate([down_b.sum, down_a.sum], 1).T
    gate = jnp.concatenate([gate_a.sum, gate_b.sum], 1)
    up = jnp.concatenate([up_a.sum, up_b.sum], 1)
    return (
        result,
        d_tokens,
        gains[0],
        qkv[:, :narrow],
        qkv[:, narrow : 2 * narrow],
        qkv[:, 2 * narrow :],
        output_weight_gradient,
        gains[1],
        gate,
        up,
        down,
    )


def solution(mesh):
    return jax.shard_map(
        per_device,
        mesh=mesh,
        in_specs=(
            P(None, "seq", None),
            P(),
            P(None, "head"),
            P(None, "head"),
            P(None, "head"),
            P("head", None),
            P(),
            P(None, "head"),
            P(None, "head"),
            P("head", None),
            P(None, "seq"),
            P(None, "seq", None),
        ),
        out_specs=(
            P(None, "seq", None),
            P(None, "seq", None),
            P("seq"),
            P("seq", "head"),
            P("seq", "head"),
            P("seq", "head"),
            P("head", "seq"),
            P("seq"),
            P("seq", "head"),
            P("seq", "head"),
            P("head", "seq"),
        ),
        check_vma=False,
    )
```

```python
import functools
import math

import jax
import jax.numpy as jnp
from jax import lax
from jax.experimental import pallas as pl
from jax.experimental.pallas import tpu as pltpu
from jax.sharding import PartitionSpec as P

FEAT = 16
HEAD_V = 128
EPS = 1e-05
PASSAGE_CEILING = 2000

MAPPED = 160
NORM = MAPPED
META = MAPPED + 2
ROWS = MAPPED + 8
FIRST, LAST, CARRIED, NEXT = META, META + 1, META + 2, META + 3

LONG = pl.CostEstimate(flops=1 << 39, bytes_accessed=1 << 20, transcendentals=0)


def swap(part, bit):
    count = lax.axis_size("head")
    return lax.ppermute(part, "head", [(k, k ^ bit) for k in range(count)])


def shift(part, by):
    count = lax.axis_size("seq")
    return lax.ppermute(part, "seq", [(k, k + by) for k in range(count) if 0 <= k + by < count])


def dot(left, right):
    return jnp.dot(left, right, preferred_element_type=jnp.float32)


def dot_t(left, right):
    return lax.dot_general(left, right, (((1,), (1,)), ((), ())), preferred_element_type=jnp.float32)


def columns_dot(left, right):
    return lax.dot_general(left, right, (((0,), (0,)), ((), ())), preferred_element_type=jnp.float32)


class Order:
    def __init__(self):
        self.last = None

    def after(self, *values):
        if self.last is not None:
            leaves, tree = jax.tree.flatten(values)
            values = jax.tree.unflatten(tree, lax.optimization_barrier((*leaves, self.last))[:-1])
        return values if len(values) > 1 else values[0]

    def mark(self, value):
        self.last = jax.tree.leaves(value)[0]
        return value

    def run(self, work, *values):
        if len(values) == 1:
            return self.mark(work(self.after(values[0])))
        return self.mark(work(*self.after(*values)))


def features(feats):
    row = lax.broadcasted_iota(jnp.int32, (8, feats.shape[1]), 0)
    parts = [jnp.where(row == 0, 1.0, 0.0), feats * 0.5, feats * feats * (1.0 / math.sqrt(32.0))]
    for k in range(1, 8):
        parts.append(feats * jnp.concatenate([feats[k:], feats[:k]], 0) * 0.25)
    parts.append(feats[:8] * feats[8:] * 0.25)
    return jnp.concatenate(parts, 0)


def features_back(feats, grad):
    total = grad[8:24] * 0.5 + grad[24:40] * feats * (2.0 / math.sqrt(32.0))
    for k in range(1, 8):
        part = grad[24 + 16 * k : 40 + 16 * k] * 0.25
        back = part * feats
        total = total + part * jnp.concatenate([feats[k:], feats[:k]], 0)
        total = total + jnp.concatenate([back[16 - k :], back[: 16 - k]], 0)
    part = grad[152:160] * 0.25
    return total + jnp.concatenate([part * feats[8:], part * feats[:8]], 0)


def low(value):
    return value.astype(jnp.bfloat16)


def dot_general(left, right, a, b):
    return lax.dot_general(left, right, (((a,), (b,)), ((), ())), preferred_element_type=jnp.float32)


def put_state(out_ref, h, mapped, right, weights, meta):
    mapped = low(mapped)
    out_ref[0, h, :MAPPED, :] = dot_general(mapped, right, 1, 0)
    norm = dot_general(weights, mapped, 0, 1)
    rest = jnp.concatenate([norm[:, 128:], jnp.zeros((8, 256 - MAPPED), jnp.float32)], 1)
    at = lax.broadcasted_iota(jnp.int32, (8, HEAD_V), 0)
    out_ref[0, h, NORM:, :] = jnp.where(at == 0, norm[:, :128], jnp.where(at == 1, rest, meta))


def get_state(refs, h):
    two, four = refs
    joined = two[0, h] + two[0, h, NEXT : NEXT + 1, :1] * four[0, h, CARRIED : CARRIED + 1, :1] * four[0, h]
    norm = jnp.concatenate([joined[NORM : NORM + 1], joined[NORM + 1 : NORM + 2, : MAPPED - 128]], 1)
    return low(joined[:MAPPED]), low(jnp.broadcast_to(norm, (8, MAPPED)))


def transposed(ref):
    return jnp.transpose(ref[0].astype(jnp.float32))


def state_kernel(key_ref, value_ref, row_ref, meta_ref, out_ref):
    heads = key_ref.shape[2] // FEAT
    row = row_ref[0]
    tail = jnp.where(row == row[:, row.shape[1] - 1 :], 1.0, 0.0)
    key_t = transposed(key_ref)
    ones = jnp.ones((key_ref.shape[1], 8), jnp.bfloat16)
    for h in range(heads):
        mapped = features(key_t[FEAT * h : FEAT * (h + 1)]) * tail
        put_state(out_ref, h, mapped, value_ref[0, :, HEAD_V * h : HEAD_V * (h + 1)], ones, meta_ref[0])


def seen(row, column, start=0):
    shape = (column.shape[0], row.shape[1])
    causal = lax.broadcasted_iota(jnp.int32, shape, 0) + start >= lax.broadcasted_iota(jnp.int32, shape, 1)
    return causal & (column == row)


def forward_kernel(
    span, query_ref, key_ref, value_ref, row_ref, column_ref, prior_ref, prior_four_ref, mixed_ref, ratio_ref, denom_ref
):
    heads = key_ref.shape[2] // FEAT
    begin, end = span
    column = column_ref[0, begin:end]
    visible = seen(row_ref[0, :, :end], column, begin)
    uses = jnp.where(column == prior_ref[0, 0, LAST : LAST + 1, :1], 1.0, 0.0)
    query_t = jnp.transpose(query_ref[0, begin:end].astype(jnp.float32))
    ones = jnp.ones((end, HEAD_V), jnp.bfloat16)
    for h in range(heads):
        narrow, wide = slice(FEAT * h, FEAT * (h + 1)), slice(HEAD_V * h, HEAD_V * (h + 1))
        kernel_dot = dot_general(query_ref[0, begin:end, narrow], key_ref[0, :end, narrow], 1, 1) * 0.25
        scores = low(jnp.where(visible, 1.0 + kernel_dot + 0.5 * kernel_dot * kernel_dot, 0.0))
        both = dot(scores, jnp.concatenate([value_ref[0, :end, wide], ones], 1))
        mapped = low(features(query_t[narrow]))
        state, norm = get_state((prior_ref, prior_four_ref), h)
        numerator = both[:, :HEAD_V] + uses * dot_general(mapped, state, 0, 0)
        denominator = both[:, HEAD_V : HEAD_V + 1] + uses * dot_general(mapped, norm, 0, 1)[:, :1]
        ratio = numerator / denominator
        mixed_ref[0, :, wide] = low(ratio)
        ratio_ref[0, :, wide] = ratio
        denom_ref[0, :, h : h + 1] = denominator


def numer_back(h, d_mixed_ref, ratio_ref, denom_ref):
    wide = slice(HEAD_V * h, HEAD_V * (h + 1))
    inverse = 1.0 / denom_ref[0, :, h : h + 1]
    d_mixed = d_mixed_ref[0, :, wide]
    d_denom = -jnp.sum(d_mixed * ratio_ref[0, :, wide], 1, keepdims=True) * inverse
    return low(d_mixed * inverse), d_denom


def state_back_kernel(query_ref, d_mixed_ref, ratio_ref, denom_ref, row_ref, prior_ref, meta_ref, out_ref):
    heads = query_ref.shape[2] // FEAT
    uses = jnp.where(row_ref[0] == prior_ref[0, 0, LAST : LAST + 1, :1], 1.0, 0.0)
    query_t = transposed(query_ref)
    for h in range(heads):
        d_numer, d_denom = numer_back(h, d_mixed_ref, ratio_ref, denom_ref)
        mapped = features(query_t[FEAT * h : FEAT * (h + 1)]) * uses
        put_state(out_ref, h, mapped, d_numer, low(jnp.broadcast_to(d_denom, (d_denom.shape[0], 8))), meta_ref[0])


def join_back_kernel(near_ref, far_ref, carried_ref, out_ref):
    for h in range(near_ref.shape[1]):
        near, far = near_ref[0, h], far_ref[0, h]
        at = lax.broadcasted_iota(jnp.int32, near.shape, 0)
        total = jnp.where(at < META, near + near[CARRIED : CARRIED + 1, :1] * far, near)
        total = jnp.where(at == NEXT, near[CARRIED : CARRIED + 1, :1], total)
        out_ref[0, h] = jnp.where(at == CARRIED, carried_ref[0], total)


def backward_kernel(
    query_ref, key_ref, value_ref, row_ref, column_ref, d_mixed_ref, ratio_ref, denom_ref, prior_ref, prior_four_ref,
    later_ref, later_four_ref, d_query_ref, d_key_ref, d_value_ref,
):
    heads = key_ref.shape[2] // FEAT
    row, column = row_ref[0], column_ref[0]
    visible = seen(row, column)
    uses = jnp.where(row == prior_ref[0, 0, LAST : LAST + 1, :1], 1.0, 0.0)
    end = row.shape[1] - 1
    tail = jnp.where(row == row[:, end:], 1.0, 0.0)
    tail_column = jnp.where(column == row[:, end:], 1.0, 0.0)
    query_t, key_t = transposed(query_ref), transposed(key_ref)
    d_queries, d_keys = [], []
    for h in range(heads):
        narrow, wide = slice(FEAT * h, FEAT * (h + 1)), slice(HEAD_V * h, HEAD_V * (h + 1))
        query, key, value = query_ref[0, :, narrow], key_ref[0, :, narrow], value_ref[0, :, wide]
        d_numer, d_denom = numer_back(h, d_mixed_ref, ratio_ref, denom_ref)
        kernel_dot = dot_general(query, key, 1, 1) * 0.25
        scores = low(jnp.where(visible, 1.0 + kernel_dot + 0.5 * kernel_dot * kernel_dot, 0.0))
        d_scores = low(jnp.where(visible, dot_general(d_numer, value, 1, 1) + d_denom, 0.0))
        d_kernel = low(d_scores.astype(jnp.float32) * (1.0 + kernel_dot))
        d_query = dot_general(key, d_kernel, 0, 1) * 0.25
        d_key = dot_general(query, d_kernel, 0, 0) * 0.25
        d_value = dot_general(scores, d_numer, 0, 0)

        wide_denom = low(jnp.broadcast_to(d_denom, (d_denom.shape[0], 8)))
        state, norm = get_state((prior_ref, prior_four_ref), h)
        mapped_back = dot_general(state, d_numer, 1, 1)
        mapped_back = mapped_back + dot_general(norm, wide_denom, 0, 1) * 0.125
        d_queries.append(d_query + features_back(query_t[narrow], mapped_back * uses))

        later, norm = get_state((later_ref, later_four_ref), h)
        mapped_back = dot_general(later, value, 1, 1)
        mapped_back = mapped_back + dot_general(norm, jnp.ones((value.shape[0], 8), jnp.bfloat16), 0, 1) * 0.125
        d_keys.append(d_key + features_back(key_t[narrow], mapped_back * tail))
        d_value = d_value + tail_column * dot_general(low(features(key_t[narrow])), later, 0, 0)
        d_value_ref[0, :, wide] = low(d_value)
    d_query_ref[0] = low(jnp.transpose(jnp.concatenate(d_queries, 0)))
    d_key_ref[0] = low(jnp.transpose(jnp.concatenate(d_keys, 0)))


def per_sequence(kernel, out_shapes, *arrays, after=()):
    def spec(shape):
        rest = (0,) * (len(shape) - 1)
        return pl.BlockSpec((1,) + tuple(shape[1:]), lambda s: (s,) + rest)

    def body(*refs):
        kernel(*refs[: len(arrays)], *refs[len(arrays) + len(after) :])

    outs = [jax.ShapeDtypeStruct(shape, dtype) for shape, dtype in out_shapes]
    result = pl.pallas_call(
        body,
        grid=(arrays[0].shape[0],),
        in_specs=[spec(a.shape) for a in arrays] + [pl.BlockSpec(memory_space=pl.ANY) for _ in after],
        out_specs=[spec(o.shape) for o in outs],
        out_shape=outs,
        cost_estimate=LONG,
        compiler_params=pltpu.CompilerParams(vmem_limit_bytes=48 << 20),
    )(*arrays, *after)
    return result if len(outs) > 1 else result[0]


def along_pair(part):
    return lax.ppermute(part, "seq", [(k, k ^ 1) for k in range(lax.axis_size("seq"))])


def along_line(parts):
    groups = [[k for k in range(8) if k % 2 == y] for y in range(2)]
    return lax.psum_scatter(parts, "seq", scatter_dimension=0, axis_index_groups=groups, tiled=True)


def scattered(left, right):
    rows, columns = jnp.concatenate(left, 0), jnp.concatenate(right, 0)
    return lax.psum_scatter(columns_dot(rows, columns), "seq", scatter_dimension=0, tiled=True)


def named(k, where):
    return 0, where[k]


def blocks_dot(terms, where, span, came=None, after=()):
    parts = len(terms)
    block = terms[0][0].shape[1] // lax.axis_size("seq")
    count, width = where.shape[0], span[1] - span[0]

    wide = [t[3].dtype != jnp.bfloat16 for t in terms]
    scratch = [pltpu.VMEM((t[3].shape[0], width), jnp.bfloat16) for t, w in zip(terms, wide) if w]

    def kernel(where_ref, *refs):
        lefts, rights = refs[:parts], refs[parts : 2 * parts]
        out_ref, narrow = refs[len(refs) - 1 - len(scratch)], list(refs[len(refs) - len(scratch) :])
        total = refs[2 * parts][...] if came is not None else None
        for n in range(parts):
            left_ref, columns = lefts[n], slice(*terms[n][4])
            if wide[n]:
                kept_ref = narrow.pop(0)

                @pl.when(pl.program_id(0) == 0)
                def _():
                    kept_ref[...] = low(rights[n][:, columns])

                right = kept_ref[...]
            else:
                right = rights[n][:, columns]
            part = dot_general(low(left_ref[...]), right, 0, 0)
            total = part if total is None else total + part
        out_ref[...] = total

    specs = [pl.BlockSpec((rows, block), at) for _, rows, at, _, _ in terms]
    specs += [pl.BlockSpec(right.shape, lambda k, where: (0, 0)) for _, _, _, right, _ in terms]
    extra = []
    if came is not None:
        specs.append(pl.BlockSpec((block, width), lambda k, where: (k, 0)))
        extra.append(came)
    specs += [pl.BlockSpec(memory_space=pl.ANY) for _ in after]
    return pl.pallas_call(
        kernel,
        grid_spec=pltpu.PrefetchScalarGridSpec(
            num_scalar_prefetch=1,
            grid=(count,),
            in_specs=specs,
            out_specs=pl.BlockSpec((block, width), lambda k, where: (k, 0)),
            scratch_shapes=scratch,
        ),
        out_shape=jax.ShapeDtypeStruct((count * block, width), jnp.float32),
        compiler_params=pltpu.CompilerParams(vmem_limit_bytes=44 << 20),
        cost_estimate=LONG,
    )(where, *[t[0] for t in terms], *[t[3] for t in terms], *extra, *after)


def own_terms(left, right, span):
    return [(l, l.shape[0], named, r, span) for l, r in zip(left, right)]


def pair_places(y):
    return (2 * jnp.arange(4) + y).astype(jnp.int32)


def picked_columns(chunks, where, after=()):
    block = chunks[0].shape[1] // 8
    rows = [c.shape[0] for c in chunks]

    def kernel(where_ref, *refs):
        at = 0
        for ref, count in zip(refs, rows):
            refs[-1][at : at + count] = ref[...].astype(jnp.float32)
            at += count

    return pl.pallas_call(
        kernel,
        grid_spec=pltpu.PrefetchScalarGridSpec(
            num_scalar_prefetch=1,
            grid=(where.shape[0],),
            in_specs=[pl.BlockSpec((count, block), named) for count in rows]
            + [pl.BlockSpec(memory_space=pl.ANY) for _ in after],
            out_specs=pl.BlockSpec((sum(rows), block), lambda k, where: (0, k)),
        ),
        out_shape=jax.ShapeDtypeStruct((sum(rows), where.shape[0] * block), jnp.float32),
        cost_estimate=LONG,
    )(where, *chunks, *after)


def add_after(terms, after):
    rows, width = terms[0].shape
    steps = 4 if rows % 32 == 0 else 1

    def kernel(*refs):
        refs[-1][...] = sum(ref[...] for ref in refs[: len(terms)])

    spec = pl.BlockSpec((rows // steps, width), lambda k: (k, 0))
    return pl.pallas_call(
        kernel,
        grid=(steps,),
        in_specs=[spec] * len(terms) + [pl.BlockSpec(memory_space=pl.ANY) for _ in after],
        out_specs=spec,
        out_shape=jax.ShapeDtypeStruct((rows, width), jnp.float32),
        cost_estimate=LONG,
    )(*terms, *after)


def transposed_after(terms, after):
    value = terms[0]

    def kernel(*refs):
        refs[-1][...] = jnp.transpose(sum(ref[...] for ref in refs[: len(terms)]))

    return pl.pallas_call(
        kernel,
        grid=(1,),
        in_specs=[pl.BlockSpec(value.shape, lambda k: (0, 0)) for _ in terms]
        + [pl.BlockSpec(memory_space=pl.ANY) for _ in after],
        out_specs=pl.BlockSpec(value.shape[::-1], lambda k: (0, 0)),
        out_shape=jax.ShapeDtypeStruct(value.shape[::-1], value.dtype),
        cost_estimate=LONG,
    )(*terms, *after)


def dot_after(left, right, after):
    rows, inner = left.shape
    width = right.shape[1]
    tile = width // 4

    def kernel(left_ref, right_ref, *refs):
        refs[-1][...] = dot(left_ref[...], right_ref[...])

    return pl.pallas_call(
        kernel,
        grid=(4,),
        in_specs=[pl.BlockSpec((rows, inner), lambda k: (0, 0)), pl.BlockSpec((inner, tile), lambda k: (0, k))]
        + [pl.BlockSpec(memory_space=pl.ANY) for _ in after],
        out_specs=pl.BlockSpec((rows, tile), lambda k: (0, k)),
        out_shape=jax.ShapeDtypeStruct((rows, width), jnp.float32),
        cost_estimate=LONG,
        compiler_params=pltpu.CompilerParams(vmem_limit_bytes=40 << 20),
    )(left, right, *after)


def dots_after(lefts, rights, after):
    rows, width, count = lefts[0].shape[0], rights[0].shape[0], len(lefts)
    tile = width // 4

    def kernel(*refs):
        refs[-1][...] = sum(dot_t(refs[k][...], refs[count + k][...]) for k in range(count))

    return pl.pallas_call(
        kernel,
        grid=(4,),
        in_specs=[pl.BlockSpec(left.shape, lambda k: (0, 0)) for left in lefts]
        + [pl.BlockSpec((tile, right.shape[1]), lambda k: (k, 0)) for right in rights]
        + [pl.BlockSpec(memory_space=pl.ANY) for _ in after],
        out_specs=pl.BlockSpec((rows, tile), lambda k: (0, k)),
        out_shape=jax.ShapeDtypeStruct((rows, width), jnp.float32),
        cost_estimate=LONG,
        compiler_params=pltpu.CompilerParams(vmem_limit_bytes=40 << 20),
    )(*lefts, *rights, *after)


class PairFirst:
    def __init__(self, left, right, span, after=()):
        self.left, self.right, self.span = left, right, span
        self.sent = self.whole = self.both = right[0]
        self.plain = lax.axis_size("seq") != 8
        if not self.plain:
            y = lax.axis_index("seq") % 2
            self.places, theirs = pair_places(y), pair_places(1 - y)
            self.sent = blocks_dot(own_terms(left, right, span), theirs, span, after=after)
            self.came = along_pair(self.sent)

    def line(self, after=()):
        if self.plain:
            self.sum = scattered(self.left, [r[:, self.span[0] : self.span[1]] for r in self.right])
            return
        terms = own_terms(self.left, self.right, self.span)
        self.whole = blocks_dot(terms, self.places, self.span, self.came, after)
        self.sum = along_line(self.whole)


class FactorsFirst:
    def __init__(self, left, span, after=()):
        self.left, self.span, self.right, self.came = left, span, [], []
        self.left_came = self.whole = self.sent = left[0]
        self.plain = lax.axis_size("seq") != 8
        if not self.plain:
            y = lax.axis_index("seq") % 2
            self.places = pair_places(y)
            self.left_came = along_pair(picked_columns(left, pair_places(1 - y), after))

    def add(self, right):
        self.right.append(right)
        if not self.plain:
            self.sent = right[:, self.span[0] : self.span[1]].astype(jnp.float32)
            self.came.append(along_pair(self.sent))

    def line(self, after=()):
        if self.plain:
            self.sum = scattered(self.left, [r[:, self.span[0] : self.span[1]] for r in self.right])
            return
        terms, width = own_terms(self.left, self.right, self.span), self.span[1] - self.span[0]
        for n, came in enumerate(self.came):
            terms.append((self.left_came, came.shape[0], lambda k, where, n=n: (n, k), came, (0, width)))
        self.whole = blocks_dot(terms, self.places, self.span, after=after)
        self.sum = along_line(self.whole)


class LineFirst:
    def __init__(self, left, right, span, after=()):
        self.left, self.right, self.span = left, right, span
        self.sent = self.whole = self.both = right[0]
        self.plain = lax.axis_size("seq") != 8
        if not self.plain:
            self.block = left[0].shape[1] // 8
            y = lax.axis_index("seq") % 2
            both = 2 * jnp.arange(4)[:, None] + jnp.stack([y, 1 - y])[None, :]
            self.whole = blocks_dot(own_terms(left, right, span), both.reshape(8).astype(jnp.int32), span, after=after)
            self.both = along_line(self.whole)

    def pair(self, after):
        if not self.plain:
            self.came = along_pair(add_after((self.both[self.block :],), after))

    def end(self, after):
        if self.plain:
            self.sum = scattered(self.left, [r[:, self.span[0] : self.span[1]] for r in self.right])
        else:
            self.sum = add_after((self.both[: self.block], self.came), after)


def pick_by(bit, zero, one):
    return jnp.where(bit == 0, zero, one)


def rms_norm(values):
    scale = lax.rsqrt(jnp.mean(values * values, -1, keepdims=True) + EPS)
    return values * scale, scale


def rms_back(normed, scale, gain, grad):
    d_normed = grad * gain
    d_values = scale * (d_normed - normed * jnp.mean(d_normed * normed, -1, keepdims=True))
    return (d_values, jnp.sum(grad * normed, 0))


CUTS = (0, 256, 512)


def per_device(
    tokens,
    gain_attn,
    query_weight,
    key_weight,
    value_weight,
    output_weight,
    gain_mlp,
    sigmoid_switch_matrix,
    up_weight,
    down_weight,
    segment_ids,
    cotangent,
):
    seq_count, tok_count, model_width = tokens.shape
    narrow, wide = query_weight.shape[1], value_weight.shape[1]
    head_count = narrow // FEAT
    reach = min(lax.axis_size("seq") - 1, -(-(PASSAGE_CEILING - 1) // tok_count))
    assert reach <= 4
    core = lax.axis_index("head") % 2
    order = Order()
    run = order.run

    segments = segment_ids.astype(jnp.float32) + 1.0
    row, column = segments[:, None, :], segments[:, :, None]
    first, last = segments[:, 0], segments[:, -1]

    def meta(*values):
        at = jnp.arange(8)[None, :, None]
        total = jnp.zeros((seq_count, 8, 128), jnp.float32)
        for k, value in enumerate(values):
            total = jnp.where(at == k + META - NORM, value[:, None, None], total)
        return total

    resid = tokens.astype(jnp.float32)
    h_attn = (rms_norm(resid)[0] * gain_attn).astype(jnp.bfloat16)
    h_rows = h_attn.reshape(-1, model_width)

    def project(h_rows, weight):
        return dot(h_rows, weight).astype(jnp.bfloat16).reshape(seq_count, tok_count, -1)

    key_proj, value_proj = project(h_rows, key_weight), project(h_rows, value_weight)
    payload = ((seq_count, head_count, ROWS, HEAD_V), jnp.float32)
    state = run(
        functools.partial(per_sequence, state_kernel, [payload]), key_proj, value_proj, row, meta(first, last)
    )
    near, far = shift(state, 1), shift(state, 2)
    query_rows = run(project, h_rows, query_weight)
    spans = [slice(a, b) for a, b in zip(CUTS[:-1], CUTS[1:])]
    cots = run(lambda cot: [cot[:, s].reshape(-1, model_width) for s in spans], cotangent)

    def at_row(part, k):
        return part[:, :, k : k + 1, :1]

    index = jnp.arange(ROWS)[None, None, :, None]

    def join_two(near, far, first, last):
        carried_near = (
            (at_row(near, FIRST) == at_row(near, LAST)) & (at_row(near, LAST) == at_row(far, LAST))
        ).astype(jnp.float32)
        first, last = first[:, None, None, None], last[:, None, None, None]
        carried = ((first == last) & (last == at_row(near, LAST))).astype(jnp.float32)
        total = jnp.where(index < META, near + carried_near * far, near)
        total = jnp.where(index == NEXT, carried_near, total)
        return jnp.where(index == CARRIED, carried, total), carried

    hidden_width = down_weight.shape[0]
    cut_b = (hidden_width * 3 // 11) // 128 * 128
    cut = (hidden_width * 6 // 11) // 128 * 128
    down_a = FactorsFirst(cots, (cut_b, hidden_width), [query_rows])
    prior_two, carried = run(join_two, near, far, first, last)
    carried = carried[:, 0, 0, 0]

    prior_four = shift(prior_two, 2) if reach > 2 else jnp.zeros_like(prior_two)

    d_hiddens = [run(dot_t, cot, down_weight) for cot in cots]

    block = (seq_count, tok_count)

    def attend(s, after):
        part = (seq_count, s.stop - s.start)
        return per_sequence(
            functools.partial(forward_kernel, (s.start, s.stop)),
            [(part + (wide,), jnp.bfloat16), (part + (wide,), jnp.float32), (part + (head_count,), jnp.float32)],
            query_rows, key_proj, value_proj, row, column, prior_two, prior_four, after=after,
        )

    head_size = lax.axis_size("head")

    def exchange(parts):
        groups = [[k, k + 1] for k in range(0, head_size, 2)]
        return lax.all_to_all(parts, "head", 0, 0, axis_index_groups=groups, tiled=True)

    def spread(own):
        return exchange(jnp.stack([own, own]))

    def mine(both):
        return jnp.where(core == 0, both[0], both[1])

    def head_part(work, *values):
        def summed(*values):
            both = exchange(work(*values))
            return both[0] + both[1]

        chip = run(summed, *values)
        bit = 2
        while 2 * bit < head_size:
            chip = chip + swap(chip, bit)
            bit *= 2
        return chip, swap(chip, bit) if bit < head_size else jnp.zeros_like(chip)

    def total(pair):
        return pair[0] + pair[1]

    def joined(parts):
        return jnp.concatenate(parts, 0)

    def flat(part):
        return part.reshape(-1, part.shape[-1])

    def paired(part):
        return part.reshape(seq_count, -1, part.shape[-1])

    def branch_part(mixed, weight):
        return paired(dot(flat(mixed), weight))

    mixeds, ratios, denominators, branches = [], [], [], []
    for s in spans:
        for into, value in zip((mixeds, ratios, denominators), attend(s, [b[0] for b in branches])):
            into.append(value)
        branches.append(head_part(branch_part, mixeds[-1], output_weight))

    mids, normeds, scales, h_mlps, hiddens, d_gates, d_ups, d_hs = [], [], [], [], [], [], [], []

    def feed(h_mlp, d_hidden, gate_weight, up_weight):
        gate, up = dot(h_mlp, gate_weight), dot(h_mlp, up_weight)
        sigmoid = jax.nn.sigmoid(gate)
        hidden = (gate * sigmoid * up).astype(jnp.bfloat16)
        d_gate = (d_hidden * up * sigmoid * (1.0 + gate * (1.0 - sigmoid))).astype(jnp.bfloat16)
        d_up = (d_hidden * gate * sigmoid).astype(jnp.bfloat16)
        return hidden, d_gate, d_up

    def feed_back(d_gate, d_up, gate_weight, up_weight, after):
        return paired(dots_after((d_gate, d_up), (gate_weight, up_weight), after))

    for k, s in enumerate(spans):
        branch = run(lambda pair: spread(total(pair)), branches[k])

        def middle(tokens, branch):
            mid = tokens.astype(jnp.float32) + branch
            normed, scale = rms_norm(mid)
            return mid, mine(normed), mine(scale), flat((normed * gain_mlp).astype(jnp.bfloat16))

        mid, normed, scale, h_mlp = run(middle, tokens[:, s], branch)
        hidden, d_gate, d_up = run(feed, h_mlp, d_hiddens[k], sigmoid_switch_matrix, up_weight)
        for into, value in zip((mids, normeds, scales, h_mlps, hiddens, d_gates, d_ups),
                               (mid, normed, scale, h_mlp, hidden, d_gate, d_up)):
            into.append(value)
        down_a.add(hidden)
        begun = [down_a.left_came]
        if k == len(spans) - 1:
            down_b = LineFirst(cots, hiddens, (0, cut_b), [down_a.sent])
            gate_a = PairFirst(h_mlps, d_gates, (0, cut), [down_b.whole])
            begun = [gate_a.sent]
        d_hs.append(head_part(feed_back, d_gate, d_up, sigmoid_switch_matrix, up_weight, begun))


    def out_part(k, after):
        return head_part(lambda hidden, weight: paired(dot_after(hidden, weight, after)), hiddens[k], down_weight)

    d_mids, d_branches, d_mixeds = [], [], []

    def middle_back(k, after):
        def work(d_h, normed, scale):
            d_own, d_gain = rms_back(normed, scale, gain_mlp, d_h)
            return spread(d_own), d_gain

        d_norm, d_gain = run(work, add_after(d_hs[k], after), normeds[k], scales[k])

        def work(d_norm, cot, weight):
            d_mid = cot.astype(jnp.float32) + d_norm
            d_branch = flat(d_mid.astype(jnp.bfloat16))
            return mine(d_mid), d_branch, paired(dot_t(d_branch, weight))

        d_mid, d_branch, d_mixed = run(work, d_norm, cotangent[:, spans[k]], output_weight)
        d_mids.append(d_mid)
        d_branches.append(d_branch)
        d_mixeds.append(d_mixed)
        return d_gain

    results = []

    def outcome(k, pair, after):
        own = add_after(pair, after)
        results.append(run(lambda mid, own: (mid + spread(own)).astype(jnp.bfloat16), mids[k], own))

    down_a.line([d_hs[1][0]])
    d_gain_mlp = middle_back(0, [down_a.whole, down_b.both])
    gate_b = PairFirst(h_mlps, d_gates, (cut, hidden_width), [d_mixeds[0]])
    d_gain_mlp = d_gain_mlp + middle_back(1, [gate_b.sent])

    d_mixed = jnp.concatenate(d_mixeds, 1)
    ratio, denominator = jnp.concatenate(ratios, 1), jnp.concatenate(denominators, 1)
    d_state = run(
        functools.partial(per_sequence, state_back_kernel, [payload]),
        query_rows, d_mixed, ratio, denominator, row, prior_two, meta(first, last, carried),
    )
    far = shift(d_state, -2)
    onward = run(lambda own, far: pick_by(lax.axis_index("seq") % 2, far, own), d_state, far)
    near = along_pair(onward)
    gate_a.line([d_state])
    up_a = PairFirst(h_mlps, d_ups, (0, cut), [gate_a.whole, down_a.sum, onward])
    gate_b.line([up_a.sent])
    mixed_rows = [flat(mixed) for mixed in mixeds]

    two = per_sequence(
        join_back_kernel, [payload], near, far, jnp.broadcast_to(carried[:, None, None], (seq_count, 1, HEAD_V)),
        after=[gate_b.whole],
    )
    four = shift(two, -2) if reach > 2 else jnp.zeros_like(two)
    out_0 = out_part(0, [two])
    up_b = PairFirst(h_mlps, d_ups, (cut, hidden_width), [out_0[0]])
    d_query, d_key, d_value = run(
        functools.partial(
            per_sequence,
            backward_kernel,
            [(block + (narrow,), jnp.bfloat16), (block + (narrow,), jnp.bfloat16), (block + (wide,), jnp.bfloat16)],
            after=[up_b.sent, gate_a.sum],
        ),
        query_rows, key_proj, value_proj, row, column, d_mixed, ratio, denominator, prior_two, prior_four,
        two, four,
    )

    def in_part(k, after):
        def work(*parts):
            return paired(dots_after([flat(p) for p in parts], (query_weight, key_weight, value_weight), after))

        s = spans[k]
        return head_part(work, d_query[:, s], d_key[:, s], d_value[:, s])

    up_a.line([d_query])
    qkv_right = flat(jnp.concatenate([d_query, d_key, d_value], -1))
    qkv = PairFirst([h_rows], [qkv_right], (0, qkv_right.shape[1]), [up_a.whole])
    in_0 = in_part(0, [qkv.sent, gate_b.sum])
    outcome(0, out_0, [in_0[0]])
    up_b.line([results[0]])

    d_tokens = []

    def first_back(k, pair, after):
        def work(d_h, tokens, d_mid):
            normed, scale = rms_norm(mine(tokens).astype(jnp.float32))
            d_own, d_gain = rms_back(normed, scale, gain_attn, d_h)
            return spread(d_own + d_mid), d_gain

        d_part, d_gain = run(work, add_after(pair, after), tokens[:, spans[k]], d_mids[k])
        d_tokens.append(d_part)
        return d_gain

    out = PairFirst(d_branches, mixed_rows, (0, wide), [up_b.whole])
    in_1 = in_part(1, [out.sent, up_a.sum])
    d_gain_attn = first_back(0, in_0, [in_1[0]])
    out_1 = out_part(1, [d_tokens[0]])
    qkv.line([out_1[0]])
    out.line([qkv.whole, up_b.sum])
    d_gain_attn = d_gain_attn + first_back(1, in_1, [out.whole])
    down_b.pair([d_tokens[1]])
    count = lax.axis_size("seq")

    def gain_blocks(d_gain_attn, d_gain_mlp):
        gains = jnp.sum(spread(jnp.stack([d_gain_attn, d_gain_mlp])), 0)
        if count != 8:
            return gains
        y = lax.axis_index("seq") % 2
        blocks = gains.reshape(2, 4, 2, -1).transpose(2, 1, 0, 3).reshape(2, 8, -1)
        return pick_by(y, blocks[0], blocks[1]), pick_by(y, blocks[1], blocks[0])

    gains = run(gain_blocks, d_gain_attn, d_gain_mlp)
    if count == 8:
        gains_came = along_pair(gains[1])
    if count == 8:
        gains = along_line(add_after((gains[0], gains_came), [d_tokens[1]]))
    else:
        gains = lax.psum_scatter(gains, "seq", scatter_dimension=1, tiled=True)
    outcome(1, out_1, [d_tokens[1], qkv.sum])
    down_b.end([results[1]])
    output_weight_gradient = transposed_after([out.sum], [results[1]])
    qkv = qkv.sum
    result = jnp.concatenate(results, 1)
    d_tokens = jnp.concatenate(d_tokens, 1)
    down = jnp.concatenate([down_b.sum, down_a.sum], 1).T
    gate = jnp.concatenate([gate_a.sum, gate_b.sum], 1)
    up = jnp.concatenate([up_a.sum, up_b.sum], 1)
    return (
        result,
        d_tokens,
        gains[0],
        qkv[:, :narrow],
        qkv[:, narrow : 2 * narrow],
        qkv[:, 2 * narrow :],
        output_weight_gradient,
        gains[1],
        gate,
        up,
        down,
    )


def solution(mesh):
    return jax.shard_map(
        per_device,
        mesh=mesh,
        in_specs=(
            P(None, "seq", None),
            P(),
            P(None, "head"),
            P(None, "head"),
            P(None, "head"),
            P("head", None),
            P(),
            P(None, "head"),
            P(None, "head"),
            P("head", None),
            P(None, "seq"),
            P(None, "seq", None),
        ),
        out_specs=(
            P(None, "seq", None),
            P(None, "seq", None),
            P("seq"),
            P("seq", "head"),
            P("seq", "head"),
            P("seq", "head"),
            P("head", "seq"),
            P("seq"),
            P("seq", "head"),
            P("seq", "head"),
            P("head", "seq"),
        ),
        check_vma=False,
    )
```

```python
import functools
import math

import jax
import jax.numpy as jnp
from jax import lax
from jax.experimental import pallas as pl
from jax.experimental.pallas import tpu as pltpu
from jax.sharding import PartitionSpec as P

FEAT = 16
HEAD_V = 128
EPS = 1e-05
PASSAGE_CEILING = 2000

MAPPED = 160
NORM = MAPPED
META = MAPPED + 2
ROWS = MAPPED + 8
FIRST, LAST, CARRIED, NEXT = META, META + 1, META + 2, META + 3

LONG = pl.CostEstimate(flops=1 << 39, bytes_accessed=1 << 20, transcendentals=0)


def swap(part, bit):
    count = lax.axis_size("head")
    return lax.ppermute(part, "head", [(k, k ^ bit) for k in range(count)])


def shift(part, by):
    count = lax.axis_size("seq")
    return lax.ppermute(part, "seq", [(k, k + by) for k in range(count) if 0 <= k + by < count])


def dot(left, right):
    return jnp.dot(left, right, preferred_element_type=jnp.float32)


def dot_t(left, right):
    return lax.dot_general(left, right, (((1,), (1,)), ((), ())), preferred_element_type=jnp.float32)


def columns_dot(left, right):
    return lax.dot_general(left, right, (((0,), (0,)), ((), ())), preferred_element_type=jnp.float32)


class Order:
    def __init__(self):
        self.last = None

    def after(self, *values):
        if self.last is not None:
            leaves, tree = jax.tree.flatten(values)
            values = jax.tree.unflatten(tree, lax.optimization_barrier((*leaves, self.last))[:-1])
        return values if len(values) > 1 else values[0]

    def mark(self, value):
        self.last = jax.tree.leaves(value)[0]
        return value

    def run(self, work, *values):
        if len(values) == 1:
            return self.mark(work(self.after(values[0])))
        return self.mark(work(*self.after(*values)))


def features(feats):
    row = lax.broadcasted_iota(jnp.int32, (8, feats.shape[1]), 0)
    parts = [jnp.where(row == 0, 1.0, 0.0), feats * 0.5, feats * feats * (1.0 / math.sqrt(32.0))]
    for k in range(1, 8):
        parts.append(feats * jnp.concatenate([feats[k:], feats[:k]], 0) * 0.25)
    parts.append(feats[:8] * feats[8:] * 0.25)
    return jnp.concatenate(parts, 0)


def features_back(feats, grad):
    total = grad[8:24] * 0.5 + grad[24:40] * feats * (2.0 / math.sqrt(32.0))
    for k in range(1, 8):
        part = grad[24 + 16 * k : 40 + 16 * k] * 0.25
        back = part * feats
        total = total + part * jnp.concatenate([feats[k:], feats[:k]], 0)
        total = total + jnp.concatenate([back[16 - k :], back[: 16 - k]], 0)
    part = grad[152:160] * 0.25
    return total + jnp.concatenate([part * feats[8:], part * feats[:8]], 0)


def low(value):
    return value.astype(jnp.bfloat16)


def dot_general(left, right, a, b):
    return lax.dot_general(left, right, (((a,), (b,)), ((), ())), preferred_element_type=jnp.float32)


def put_state(out_ref, h, mapped, right, weights, meta):
    mapped = low(mapped)
    out_ref[0, h, :MAPPED, :] = dot_general(mapped, right, 1, 0)
    norm = dot_general(weights, mapped, 0, 1)
    rest = jnp.concatenate([norm[:, 128:], jnp.zeros((8, 256 - MAPPED), jnp.float32)], 1)
    at = lax.broadcasted_iota(jnp.int32, (8, HEAD_V), 0)
    out_ref[0, h, NORM:, :] = jnp.where(at == 0, norm[:, :128], jnp.where(at == 1, rest, meta))


def get_state(refs, h):
    two, four = refs
    joined = two[0, h] + two[0, h, NEXT : NEXT + 1, :1] * four[0, h, CARRIED : CARRIED + 1, :1] * four[0, h]
    norm = jnp.concatenate([joined[NORM : NORM + 1], joined[NORM + 1 : NORM + 2, : MAPPED - 128]], 1)
    return low(joined[:MAPPED]), low(jnp.broadcast_to(norm, (8, MAPPED)))


def transposed(ref):
    return jnp.transpose(ref[0].astype(jnp.float32))


def state_kernel(key_ref, value_ref, row_ref, meta_ref, out_ref):
    heads = key_ref.shape[2] // FEAT
    row = row_ref[0]
    tail = jnp.where(row == row[:, row.shape[1] - 1 :], 1.0, 0.0)
    key_t = transposed(key_ref)
    ones = jnp.ones((key_ref.shape[1], 8), jnp.bfloat16)
    for h in range(heads):
        mapped = features(key_t[FEAT * h : FEAT * (h + 1)]) * tail
        put_state(out_ref, h, mapped, value_ref[0, :, HEAD_V * h : HEAD_V * (h + 1)], ones, meta_ref[0])


def seen(row, column, start=0):
    shape = (column.shape[0], row.shape[1])
    causal = lax.broadcasted_iota(jnp.int32, shape, 0) + start >= lax.broadcasted_iota(jnp.int32, shape, 1)
    return causal & (column == row)


def forward_kernel(
    span, query_ref, key_ref, value_ref, row_ref, column_ref, prior_ref, prior_four_ref, mixed_ref, ratio_ref, denom_ref
):
    heads = key_ref.shape[2] // FEAT
    begin, end = span
    column = column_ref[0, begin:end]
    visible = seen(row_ref[0, :, :end], column, begin)
    uses = jnp.where(column == prior_ref[0, 0, LAST : LAST + 1, :1], 1.0, 0.0)
    query_t = jnp.transpose(query_ref[0, begin:end].astype(jnp.float32))
    ones = jnp.ones((end, HEAD_V), jnp.bfloat16)
    for h in range(heads):
        narrow, wide = slice(FEAT * h, FEAT * (h + 1)), slice(HEAD_V * h, HEAD_V * (h + 1))
        kernel_dot = dot_general(query_ref[0, begin:end, narrow], key_ref[0, :end, narrow], 1, 1) * 0.25
        scores = low(jnp.where(visible, 1.0 + kernel_dot + 0.5 * kernel_dot * kernel_dot, 0.0))
        both = dot(scores, jnp.concatenate([value_ref[0, :end, wide], ones], 1))
        mapped = low(features(query_t[narrow]))
        state, norm = get_state((prior_ref, prior_four_ref), h)
        numerator = both[:, :HEAD_V] + uses * dot_general(mapped, state, 0, 0)
        denominator = both[:, HEAD_V : HEAD_V + 1] + uses * dot_general(mapped, norm, 0, 1)[:, :1]
        ratio = numerator / denominator
        mixed_ref[0, :, wide] = low(ratio)
        ratio_ref[0, :, wide] = ratio
        denom_ref[0, :, h : h + 1] = denominator


def numer_back(h, d_mixed_ref, ratio_ref, denom_ref):
    wide = slice(HEAD_V * h, HEAD_V * (h + 1))
    inverse = 1.0 / denom_ref[0, :, h : h + 1]
    d_mixed = d_mixed_ref[0, :, wide]
    d_denom = -jnp.sum(d_mixed * ratio_ref[0, :, wide], 1, keepdims=True) * inverse
    return low(d_mixed * inverse), d_denom


def state_back_kernel(query_ref, d_mixed_ref, ratio_ref, denom_ref, row_ref, prior_ref, meta_ref, out_ref):
    heads = query_ref.shape[2] // FEAT
    uses = jnp.where(row_ref[0] == prior_ref[0, 0, LAST : LAST + 1, :1], 1.0, 0.0)
    query_t = transposed(query_ref)
    for h in range(heads):
        d_numer, d_denom = numer_back(h, d_mixed_ref, ratio_ref, denom_ref)
        mapped = features(query_t[FEAT * h : FEAT * (h + 1)]) * uses
        put_state(out_ref, h, mapped, d_numer, low(jnp.broadcast_to(d_denom, (d_denom.shape[0], 8))), meta_ref[0])


def join_back_kernel(near_ref, far_ref, carried_ref, out_ref):
    for h in range(near_ref.shape[1]):
        near, far = near_ref[0, h], far_ref[0, h]
        at = lax.broadcasted_iota(jnp.int32, near.shape, 0)
        total = jnp.where(at < META, near + near[CARRIED : CARRIED + 1, :1] * far, near)
        total = jnp.where(at == NEXT, near[CARRIED : CARRIED + 1, :1], total)
        out_ref[0, h] = jnp.where(at == CARRIED, carried_ref[0], total)


def backward_kernel(
    query_ref, key_ref, value_ref, row_ref, column_ref, d_mixed_ref, ratio_ref, denom_ref, prior_ref, prior_four_ref,
    later_ref, later_four_ref, d_query_ref, d_key_ref, d_value_ref,
):
    heads = key_ref.shape[2] // FEAT
    row, column = row_ref[0], column_ref[0]
    visible = seen(row, column)
    uses = jnp.where(row == prior_ref[0, 0, LAST : LAST + 1, :1], 1.0, 0.0)
    end = row.shape[1] - 1
    tail = jnp.where(row == row[:, end:], 1.0, 0.0)
    tail_column = jnp.where(column == row[:, end:], 1.0, 0.0)
    query_t, key_t = transposed(query_ref), transposed(key_ref)
    d_queries, d_keys = [], []
    for h in range(heads):
        narrow, wide = slice(FEAT * h, FEAT * (h + 1)), slice(HEAD_V * h, HEAD_V * (h + 1))
        query, key, value = query_ref[0, :, narrow], key_ref[0, :, narrow], value_ref[0, :, wide]
        d_numer, d_denom = numer_back(h, d_mixed_ref, ratio_ref, denom_ref)
        kernel_dot = dot_general(query, key, 1, 1) * 0.25
        scores = low(jnp.where(visible, 1.0 + kernel_dot + 0.5 * kernel_dot * kernel_dot, 0.0))
        d_scores = low(jnp.where(visible, dot_general(d_numer, value, 1, 1) + d_denom, 0.0))
        d_kernel = low(d_scores.astype(jnp.float32) * (1.0 + kernel_dot))
        d_query = dot_general(key, d_kernel, 0, 1) * 0.25
        d_key = dot_general(query, d_kernel, 0, 0) * 0.25
        d_value = dot_general(scores, d_numer, 0, 0)

        wide_denom = low(jnp.broadcast_to(d_denom, (d_denom.shape[0], 8)))
        state, norm = get_state((prior_ref, prior_four_ref), h)
        mapped_back = dot_general(state, d_numer, 1, 1)
        mapped_back = mapped_back + dot_general(norm, wide_denom, 0, 1) * 0.125
        d_queries.append(d_query + features_back(query_t[narrow], mapped_back * uses))

        later, norm = get_state((later_ref, later_four_ref), h)
        mapped_back = dot_general(later, value, 1, 1)
        mapped_back = mapped_back + dot_general(norm, jnp.ones((value.shape[0], 8), jnp.bfloat16), 0, 1) * 0.125
        d_keys.append(d_key + features_back(key_t[narrow], mapped_back * tail))
        d_value = d_value + tail_column * dot_general(low(features(key_t[narrow])), later, 0, 0)
        d_value_ref[0, :, wide] = low(d_value)
    d_query_ref[0] = low(jnp.transpose(jnp.concatenate(d_queries, 0)))
    d_key_ref[0] = low(jnp.transpose(jnp.concatenate(d_keys, 0)))


def per_sequence(kernel, out_shapes, *arrays, after=(), vmem=48):
    def spec(shape):
        rest = (0,) * (len(shape) - 1)
        return pl.BlockSpec((1,) + tuple(shape[1:]), lambda s: (s,) + rest)

    def body(*refs):
        kernel(*refs[: len(arrays)], *refs[len(arrays) + len(after) :])

    outs = [jax.ShapeDtypeStruct(shape, dtype) for shape, dtype in out_shapes]
    result = pl.pallas_call(
        body,
        grid=(arrays[0].shape[0],),
        in_specs=[spec(a.shape) for a in arrays] + [pl.BlockSpec(memory_space=pl.ANY) for _ in after],
        out_specs=[spec(o.shape) for o in outs],
        out_shape=outs,
        cost_estimate=LONG,
        compiler_params=pltpu.CompilerParams(vmem_limit_bytes=vmem << 20),
    )(*arrays, *after)
    return result if len(outs) > 1 else result[0]


def along_pair(part):
    return lax.ppermute(part, "seq", [(k, k ^ 1) for k in range(lax.axis_size("seq"))])


def along_line(parts):
    groups = [[k for k in range(8) if k % 2 == y] for y in range(2)]
    return lax.psum_scatter(parts, "seq", scatter_dimension=0, axis_index_groups=groups, tiled=True)


def scattered(left, right):
    rows, columns = jnp.concatenate(left, 0), jnp.concatenate(right, 0)
    return lax.psum_scatter(columns_dot(rows, columns), "seq", scatter_dimension=0, tiled=True)


def named(k, where):
    return 0, where[k]


def blocks_dot(terms, where, span, came=None, after=()):
    parts = len(terms)
    block = terms[0][0].shape[1] // lax.axis_size("seq")
    count, width = where.shape[0], span[1] - span[0]

    wide = [t[3].dtype != jnp.bfloat16 for t in terms]
    scratch = [pltpu.VMEM((t[3].shape[0], width), jnp.bfloat16) for t, w in zip(terms, wide) if w]

    def kernel(where_ref, *refs):
        lefts, rights = refs[:parts], refs[parts : 2 * parts]
        out_ref, narrow = refs[len(refs) - 1 - len(scratch)], list(refs[len(refs) - len(scratch) :])
        total = refs[2 * parts][...] if came is not None else None
        for n in range(parts):
            left_ref, columns = lefts[n], slice(*terms[n][4])
            if wide[n]:
                kept_ref = narrow.pop(0)

                @pl.when(pl.program_id(0) == 0)
                def _():
                    kept_ref[...] = low(rights[n][:, columns])

                right = kept_ref[...]
            else:
                right = rights[n][:, columns]
            part = dot_general(low(left_ref[...]), right, 0, 0)
            total = part if total is None else total + part
        out_ref[...] = total

    specs = [pl.BlockSpec((rows, block), at) for _, rows, at, _, _ in terms]
    specs += [pl.BlockSpec(right.shape, lambda k, where: (0, 0)) for _, _, _, right, _ in terms]
    extra = []
    if came is not None:
        specs.append(pl.BlockSpec((block, width), lambda k, where: (k, 0)))
        extra.append(came)
    specs += [pl.BlockSpec(memory_space=pl.ANY) for _ in after]
    return pl.pallas_call(
        kernel,
        grid_spec=pltpu.PrefetchScalarGridSpec(
            num_scalar_prefetch=1,
            grid=(count,),
            in_specs=specs,
            out_specs=pl.BlockSpec((block, width), lambda k, where: (k, 0)),
            scratch_shapes=scratch,
        ),
        out_shape=jax.ShapeDtypeStruct((count * block, width), jnp.float32),
        compiler_params=pltpu.CompilerParams(vmem_limit_bytes=44 << 20),
        cost_estimate=LONG,
    )(where, *[t[0] for t in terms], *[t[3] for t in terms], *extra, *after)


def own_terms(left, right, span):
    return [(l, l.shape[0], named, r, span) for l, r in zip(left, right)]


def pair_places(y):
    return (2 * jnp.arange(4) + y).astype(jnp.int32)


def picked_columns(chunks, where, after=()):
    block = chunks[0].shape[1] // 8
    rows = [c.shape[0] for c in chunks]

    def kernel(where_ref, *refs):
        at = 0
        for ref, count in zip(refs, rows):
            refs[-1][at : at + count] = ref[...].astype(jnp.float32)
            at += count

    return pl.pallas_call(
        kernel,
        grid_spec=pltpu.PrefetchScalarGridSpec(
            num_scalar_prefetch=1,
            grid=(where.shape[0],),
            in_specs=[pl.BlockSpec((count, block), named) for count in rows]
            + [pl.BlockSpec(memory_space=pl.ANY) for _ in after],
            out_specs=pl.BlockSpec((sum(rows), block), lambda k, where: (0, k)),
        ),
        out_shape=jax.ShapeDtypeStruct((sum(rows), where.shape[0] * block), jnp.float32),
        cost_estimate=LONG,
    )(where, *chunks, *after)


def add_after(terms, after):
    rows, width = terms[0].shape
    steps = 4 if rows % 32 == 0 else 1

    def kernel(*refs):
        refs[-1][...] = sum(ref[...] for ref in refs[: len(terms)])

    spec = pl.BlockSpec((rows // steps, width), lambda k: (k, 0))
    return pl.pallas_call(
        kernel,
        grid=(steps,),
        in_specs=[spec] * len(terms) + [pl.BlockSpec(memory_space=pl.ANY) for _ in after],
        out_specs=spec,
        out_shape=jax.ShapeDtypeStruct((rows, width), jnp.float32),
        cost_estimate=LONG,
    )(*terms, *after)


def transposed_after(terms, after):
    value = terms[0]

    def kernel(*refs):
        refs[-1][...] = jnp.transpose(sum(ref[...] for ref in refs[: len(terms)]))

    return pl.pallas_call(
        kernel,
        grid=(1,),
        in_specs=[pl.BlockSpec(value.shape, lambda k: (0, 0)) for _ in terms]
        + [pl.BlockSpec(memory_space=pl.ANY) for _ in after],
        out_specs=pl.BlockSpec(value.shape[::-1], lambda k: (0, 0)),
        out_shape=jax.ShapeDtypeStruct(value.shape[::-1], value.dtype),
        cost_estimate=LONG,
    )(*terms, *after)


def dot_after(left, right, after):
    rows, inner = left.shape
    width = right.shape[1]
    tile = width // 4

    def kernel(left_ref, right_ref, *refs):
        refs[-1][...] = dot(left_ref[...], right_ref[...])

    return pl.pallas_call(
        kernel,
        grid=(4,),
        in_specs=[pl.BlockSpec((rows, inner), lambda k: (0, 0)), pl.BlockSpec((inner, tile), lambda k: (0, k))]
        + [pl.BlockSpec(memory_space=pl.ANY) for _ in after],
        out_specs=pl.BlockSpec((rows, tile), lambda k: (0, k)),
        out_shape=jax.ShapeDtypeStruct((rows, width), jnp.float32),
        cost_estimate=LONG,
        compiler_params=pltpu.CompilerParams(vmem_limit_bytes=40 << 20),
    )(left, right, *after)


def dots_after(lefts, rights, after):
    rows, width, count = lefts[0].shape[0], rights[0].shape[0], len(lefts)
    tile = width // 4

    def kernel(*refs):
        refs[-1][...] = sum(dot_t(refs[k][...], refs[count + k][...]) for k in range(count))

    return pl.pallas_call(
        kernel,
        grid=(4,),
        in_specs=[pl.BlockSpec(left.shape, lambda k: (0, 0)) for left in lefts]
        + [pl.BlockSpec((tile, right.shape[1]), lambda k: (k, 0)) for right in rights]
        + [pl.BlockSpec(memory_space=pl.ANY) for _ in after],
        out_specs=pl.BlockSpec((rows, tile), lambda k: (0, k)),
        out_shape=jax.ShapeDtypeStruct((rows, width), jnp.float32),
        cost_estimate=LONG,
        compiler_params=pltpu.CompilerParams(vmem_limit_bytes=40 << 20),
    )(*lefts, *rights, *after)


class PairFirst:
    def __init__(self, left, right, span, after=()):
        self.left, self.right, self.span = left, right, span
        self.sent = self.whole = self.both = right[0]
        self.plain = lax.axis_size("seq") != 8
        if not self.plain:
            y = lax.axis_index("seq") % 2
            self.places, theirs = pair_places(y), pair_places(1 - y)
            self.sent = blocks_dot(own_terms(left, right, span), theirs, span, after=after)
            self.came = along_pair(self.sent)

    def line(self, after=()):
        if self.plain:
            self.sum = scattered(self.left, [r[:, self.span[0] : self.span[1]] for r in self.right])
            return
        terms = own_terms(self.left, self.right, self.span)
        self.whole = blocks_dot(terms, self.places, self.span, self.came, after)
        self.sum = along_line(self.whole)


class FactorsFirst:
    def __init__(self, left, span, after=()):
        self.left, self.span, self.right, self.came = left, span, [], []
        self.left_came = self.whole = self.sent = left[0]
        self.plain = lax.axis_size("seq") != 8
        if not self.plain:
            y = lax.axis_index("seq") % 2
            self.places = pair_places(y)
            self.left_came = along_pair(picked_columns(left, pair_places(1 - y), after))

    def add(self, right):
        self.right.append(right)
        if not self.plain:
            self.sent = right[:, self.span[0] : self.span[1]].astype(jnp.float32)
            self.came.append(along_pair(self.sent))

    def line(self, after=()):
        if self.plain:
            self.sum = scattered(self.left, [r[:, self.span[0] : self.span[1]] for r in self.right])
            return
        terms, width = own_terms(self.left, self.right, self.span), self.span[1] - self.span[0]
        for n, came in enumerate(self.came):
            terms.append((self.left_came, came.shape[0], lambda k, where, n=n: (n, k), came, (0, width)))
        self.whole = blocks_dot(terms, self.places, self.span, after=after)
        self.sum = along_line(self.whole)


class LineFirst:
    def __init__(self, left, right, span, after=()):
        self.left, self.right, self.span = left, right, span
        self.sent = self.whole = self.both = right[0]
        self.plain = lax.axis_size("seq") != 8
        if not self.plain:
            self.block = left[0].shape[1] // 8
            y = lax.axis_index("seq") % 2
            both = 2 * jnp.arange(4)[:, None] + jnp.stack([y, 1 - y])[None, :]
            self.whole = blocks_dot(own_terms(left, right, span), both.reshape(8).astype(jnp.int32), span, after=after)
            self.both = along_line(self.whole)

    def pair(self, after):
        if not self.plain:
            self.came = along_pair(add_after((self.both[self.block :],), after))

    def end(self, after):
        if self.plain:
            self.sum = scattered(self.left, [r[:, self.span[0] : self.span[1]] for r in self.right])
        else:
            self.sum = add_after((self.both[: self.block], self.came), after)


def pick_by(bit, zero, one):
    return jnp.where(bit == 0, zero, one)


def rms_norm(values):
    scale = lax.rsqrt(jnp.mean(values * values, -1, keepdims=True) + EPS)
    return values * scale, scale


def rms_back(normed, scale, gain, grad):
    d_normed = grad * gain
    d_values = scale * (d_normed - normed * jnp.mean(d_normed * normed, -1, keepdims=True))
    return (d_values, jnp.sum(grad * normed, 0))


CUTS = (0, 256, 512)


def per_device(
    tokens,
    gain_attn,
    query_weight,
    key_weight,
    value_weight,
    output_weight,
    gain_mlp,
    sigmoid_switch_matrix,
    up_weight,
    down_weight,
    segment_ids,
    cotangent,
):
    seq_count, tok_count, model_width = tokens.shape
    narrow, wide = query_weight.shape[1], value_weight.shape[1]
    head_count = narrow // FEAT
    reach = min(lax.axis_size("seq") - 1, -(-(PASSAGE_CEILING - 1) // tok_count))
    assert reach <= 4
    core = lax.axis_index("head") % 2
    order = Order()
    run = order.run

    segments = segment_ids.astype(jnp.float32) + 1.0
    row, column = segments[:, None, :], segments[:, :, None]
    first, last = segments[:, 0], segments[:, -1]

    def meta(*values):
        at = jnp.arange(8)[None, :, None]
        total = jnp.zeros((seq_count, 8, 128), jnp.float32)
        for k, value in enumerate(values):
            total = jnp.where(at == k + META - NORM, value[:, None, None], total)
        return total

    resid = tokens.astype(jnp.float32)
    h_attn = (rms_norm(resid)[0] * gain_attn).astype(jnp.bfloat16)
    h_rows = h_attn.reshape(-1, model_width)

    def project(h_rows, weight):
        return dot(h_rows, weight).astype(jnp.bfloat16).reshape(seq_count, tok_count, -1)

    key_proj, value_proj = project(h_rows, key_weight), project(h_rows, value_weight)
    payload = ((seq_count, head_count, ROWS, HEAD_V), jnp.float32)
    state = run(
        functools.partial(per_sequence, state_kernel, [payload]), key_proj, value_proj, row, meta(first, last)
    )
    near, far = shift(state, 1), shift(state, 2)
    query_rows = run(project, h_rows, query_weight)
    spans = [slice(a, b) for a, b in zip(CUTS[:-1], CUTS[1:])]
    cots = run(lambda cot: [cot[:, s].reshape(-1, model_width) for s in spans], cotangent)

    def at_row(part, k):
        return part[:, :, k : k + 1, :1]

    index = jnp.arange(ROWS)[None, None, :, None]

    def join_two(near, far, first, last):
        carried_near = (
            (at_row(near, FIRST) == at_row(near, LAST)) & (at_row(near, LAST) == at_row(far, LAST))
        ).astype(jnp.float32)
        first, last = first[:, None, None, None], last[:, None, None, None]
        carried = ((first == last) & (last == at_row(near, LAST))).astype(jnp.float32)
        total = jnp.where(index < META, near + carried_near * far, near)
        total = jnp.where(index == NEXT, carried_near, total)
        return jnp.where(index == CARRIED, carried, total), carried

    hidden_width = down_weight.shape[0]
    cut_b = (hidden_width * 3 // 11) // 128 * 128
    cut = (hidden_width * 6 // 11) // 128 * 128
    down_a = FactorsFirst(cots, (cut_b, hidden_width), [query_rows])
    prior_two, carried = run(join_two, near, far, first, last)
    carried = carried[:, 0, 0, 0]

    prior_four = shift(prior_two, 2) if reach > 2 else jnp.zeros_like(prior_two)

    d_hiddens = [run(dot_t, cot, down_weight) for cot in cots]

    block = (seq_count, tok_count)

    def attend(s, after):
        part = (seq_count, s.stop - s.start)
        return per_sequence(
            functools.partial(forward_kernel, (s.start, s.stop)),
            [(part + (wide,), jnp.bfloat16), (part + (wide,), jnp.float32), (part + (head_count,), jnp.float32)],
            query_rows, key_proj, value_proj, row, column, prior_two, prior_four, after=after, vmem=60,
        )

    head_size = lax.axis_size("head")

    def exchange(parts):
        groups = [[k, k + 1] for k in range(0, head_size, 2)]
        return lax.all_to_all(parts, "head", 0, 0, axis_index_groups=groups, tiled=True)

    def spread(own):
        return exchange(jnp.stack([own, own]))

    def mine(both):
        return jnp.where(core == 0, both[0], both[1])

    def head_part(work, *values):
        def summed(*values):
            both = exchange(work(*values))
            return both[0] + both[1]

        chip = run(summed, *values)
        bit = 2
        while 2 * bit < head_size:
            chip = chip + swap(chip, bit)
            bit *= 2
        return chip, swap(chip, bit) if bit < head_size else jnp.zeros_like(chip)

    def total(pair):
        return pair[0] + pair[1]

    def joined(parts):
        return jnp.concatenate(parts, 0)

    def flat(part):
        return part.reshape(-1, part.shape[-1])

    def paired(part):
        return part.reshape(seq_count, -1, part.shape[-1])

    def branch_part(mixed, weight):
        return paired(dot(flat(mixed), weight))

    mixeds, ratios, denominators, branches = [], [], [], []
    for s in spans:
        for into, value in zip((mixeds, ratios, denominators), attend(s, [b[0] for b in branches])):
            into.append(value)
        branches.append(head_part(branch_part, mixeds[-1], output_weight))

    mids, normeds, scales, h_mlps, hiddens, d_gates, d_ups, d_hs = [], [], [], [], [], [], [], []

    def feed(h_mlp, d_hidden, gate_weight, up_weight):
        gate, up = dot(h_mlp, gate_weight), dot(h_mlp, up_weight)
        sigmoid = jax.nn.sigmoid(gate)
        hidden = (gate * sigmoid * up).astype(jnp.bfloat16)
        d_gate = (d_hidden * up * sigmoid * (1.0 + gate * (1.0 - sigmoid))).astype(jnp.bfloat16)
        d_up = (d_hidden * gate * sigmoid).astype(jnp.bfloat16)
        return hidden, d_gate, d_up

    def feed_back(d_gate, d_up, gate_weight, up_weight, after):
        return paired(dots_after((d_gate, d_up), (gate_weight, up_weight), after))

    for k, s in enumerate(spans):
        branch = run(lambda pair: spread(total(pair)), branches[k])

        def middle(tokens, branch):
            mid = tokens.astype(jnp.float32) + branch
            normed, scale = rms_norm(mid)
            return mid, mine(normed), mine(scale), flat((normed * gain_mlp).astype(jnp.bfloat16))

        mid, normed, scale, h_mlp = run(middle, tokens[:, s], branch)
        hidden, d_gate, d_up = run(feed, h_mlp, d_hiddens[k], sigmoid_switch_matrix, up_weight)
        for into, value in zip((mids, normeds, scales, h_mlps, hiddens, d_gates, d_ups),
                               (mid, normed, scale, h_mlp, hidden, d_gate, d_up)):
            into.append(value)
        down_a.add(hidden)
        begun = [down_a.left_came]
        if k == len(spans) - 1:
            down_b = LineFirst(cots, hiddens, (0, cut_b), [down_a.sent])
            gate_a = PairFirst(h_mlps, d_gates, (0, cut), [down_b.whole])
            begun = [gate_a.sent]
        d_hs.append(head_part(feed_back, d_gate, d_up, sigmoid_switch_matrix, up_weight, begun))


    def out_part(k, after):
        return head_part(lambda hidden, weight: paired(dot_after(hidden, weight, after)), hiddens[k], down_weight)

    d_mids, d_branches, d_mixeds = [], [], []

    def middle_back(k, after):
        def work(d_h, normed, scale):
            d_own, d_gain = rms_back(normed, scale, gain_mlp, d_h)
            return spread(d_own), d_gain

        d_norm, d_gain = run(work, add_after(d_hs[k], after), normeds[k], scales[k])

        def work(d_norm, cot, weight):
            d_mid = cot.astype(jnp.float32) + d_norm
            d_branch = flat(d_mid.astype(jnp.bfloat16))
            return mine(d_mid), d_branch, paired(dot_t(d_branch, weight))

        d_mid, d_branch, d_mixed = run(work, d_norm, cotangent[:, spans[k]], output_weight)
        d_mids.append(d_mid)
        d_branches.append(d_branch)
        d_mixeds.append(d_mixed)
        return d_gain

    results = []

    def outcome(k, pair, after):
        own = add_after(pair, after)
        results.append(run(lambda mid, own: (mid + spread(own)).astype(jnp.bfloat16), mids[k], own))

    down_a.line([d_hs[1][0]])
    d_gain_mlp = middle_back(0, [down_a.whole, down_b.both])
    gate_b = PairFirst(h_mlps, d_gates, (cut, hidden_width), [d_mixeds[0]])
    d_gain_mlp = d_gain_mlp + middle_back(1, [gate_b.sent])

    d_mixed = jnp.concatenate(d_mixeds, 1)
    ratio, denominator = jnp.concatenate(ratios, 1), jnp.concatenate(denominators, 1)
    d_state = run(
        functools.partial(per_sequence, state_back_kernel, [payload]),
        query_rows, d_mixed, ratio, denominator, row, prior_two, meta(first, last, carried),
    )
    far = shift(d_state, -2)
    onward = run(lambda own, far: pick_by(lax.axis_index("seq") % 2, far, own), d_state, far)
    near = along_pair(onward)
    gate_a.line([d_state])
    up_a = PairFirst(h_mlps, d_ups, (0, cut), [gate_a.whole, down_a.sum, onward])
    gate_b.line([up_a.sent])
    mixed_rows = [flat(mixed) for mixed in mixeds]

    two = per_sequence(
        join_back_kernel, [payload], near, far, jnp.broadcast_to(carried[:, None, None], (seq_count, 1, HEAD_V)),
        after=[gate_b.whole],
    )
    four = shift(two, -2) if reach > 2 else jnp.zeros_like(two)
    out_0 = out_part(0, [two])
    up_b = PairFirst(h_mlps, d_ups, (cut, hidden_width), [out_0[0]])
    d_query, d_key, d_value = run(
        functools.partial(
            per_sequence,
            backward_kernel,
            [(block + (narrow,), jnp.bfloat16), (block + (narrow,), jnp.bfloat16), (block + (wide,), jnp.bfloat16)],
            after=[up_b.sent, gate_a.sum],
        ),
        query_rows, key_proj, value_proj, row, column, d_mixed, ratio, denominator, prior_two, prior_four,
        two, four,
    )

    def in_part(k, after):
        def work(*parts):
            return paired(dots_after([flat(p) for p in parts], (query_weight, key_weight, value_weight), after))

        s = spans[k]
        return head_part(work, d_query[:, s], d_key[:, s], d_value[:, s])

    up_a.line([d_query])
    qkv_right = flat(jnp.concatenate([d_query, d_key, d_value], -1))
    qkv = PairFirst([h_rows], [qkv_right], (0, qkv_right.shape[1]), [up_a.whole])
    in_0 = in_part(0, [qkv.sent, gate_b.sum])
    outcome(0, out_0, [in_0[0]])
    up_b.line([results[0]])

    d_tokens = []

    def first_back(k, pair, after):
        def work(d_h, tokens, d_mid):
            normed, scale = rms_norm(mine(tokens).astype(jnp.float32))
            d_own, d_gain = rms_back(normed, scale, gain_attn, d_h)
            return spread(d_own + d_mid), d_gain

        d_part, d_gain = run(work, add_after(pair, after), tokens[:, spans[k]], d_mids[k])
        d_tokens.append(d_part)
        return d_gain

    out = PairFirst(d_branches, mixed_rows, (0, wide), [up_b.whole])
    in_1 = in_part(1, [out.sent, up_a.sum])
    d_gain_attn = first_back(0, in_0, [in_1[0]])
    out_1 = out_part(1, [d_tokens[0]])
    qkv.line([out_1[0]])
    out.line([qkv.whole, up_b.sum])
    d_gain_attn = d_gain_attn + first_back(1, in_1, [out.whole])
    down_b.pair([d_tokens[1]])
    count = lax.axis_size("seq")

    def gain_blocks(d_gain_attn, d_gain_mlp):
        gains = jnp.sum(spread(jnp.stack([d_gain_attn, d_gain_mlp])), 0)
        if count != 8:
            return gains
        y = lax.axis_index("seq") % 2
        blocks = gains.reshape(2, 4, 2, -1).transpose(2, 1, 0, 3).reshape(2, 8, -1)
        return pick_by(y, blocks[0], blocks[1]), pick_by(y, blocks[1], blocks[0])

    gains = run(gain_blocks, d_gain_attn, d_gain_mlp)
    if count == 8:
        gains_came = along_pair(gains[1])
    if count == 8:
        gains = along_line(add_after((gains[0], gains_came), [d_tokens[1]]))
    else:
        gains = lax.psum_scatter(gains, "seq", scatter_dimension=1, tiled=True)
    outcome(1, out_1, [d_tokens[1], qkv.sum])
    down_b.end([results[1]])
    output_weight_gradient = transposed_after([out.sum], [results[1]])
    qkv = qkv.sum
    result = jnp.concatenate(results, 1)
    d_tokens = jnp.concatenate(d_tokens, 1)
    down = jnp.concatenate([down_b.sum, down_a.sum], 1).T
    gate = jnp.concatenate([gate_a.sum, gate_b.sum], 1)
    up = jnp.concatenate([up_a.sum, up_b.sum], 1)
    return (
        result,
        d_tokens,
        gains[0],
        qkv[:, :narrow],
        qkv[:, narrow : 2 * narrow],
        qkv[:, 2 * narrow :],
        output_weight_gradient,
        gains[1],
        gate,
        up,
        down,
    )


def solution(mesh):
    return jax.shard_map(
        per_device,
        mesh=mesh,
        in_specs=(
            P(None, "seq", None),
            P(),
            P(None, "head"),
            P(None, "head"),
            P(None, "head"),
            P("head", None),
            P(),
            P(None, "head"),
            P(None, "head"),
            P("head", None),
            P(None, "seq"),
            P(None, "seq", None),
        ),
        out_specs=(
            P(None, "seq", None),
            P(None, "seq", None),
            P("seq"),
            P("seq", "head"),
            P("seq", "head"),
            P("seq", "head"),
            P("head", "seq"),
            P("seq"),
            P("seq", "head"),
            P("seq", "head"),
            P("head", "seq"),
        ),
        check_vma=False,
    )
```
